32 devices in a mesh: section: 2 (over core), dp: 8 (over z, y), tensor: 2 (over x).
Axes of the slice: x: 2, y: 2, z: 4, core: 2. Of those that a mesh axis runs over, the one named last changes fastest.
Arguments:
- tokens: bfloat16 [2, 4096, 1024], P(None, ('dp', 'tensor')), may hold values from -6 to 6
- lengths: int32 [8, 2, 25], P('dp'), may hold values from 1 to 60, 512 in all within a row
- w_qkv: bfloat16 [2, 1024, 3, 1024], P('section', None, None, 'tensor'), may hold values from -0.1875 to 0.1875
- w_out: bfloat16 [2, 1024, 1024], P('section', 'tensor'), may hold values from -0.5 to 0.5
- w_up: bfloat16 [2, 1024, 2048], P('section', None, 'tensor'), may hold values from -0.1875 to 0.1875
- w_down: bfloat16 [2, 2048, 1024], P('section', 'tensor'), may hold values from -0.1875 to 0.1875
- norm_gain: float32 [2, 2, 1024], P('section'), may hold values from 0.25 to 1.75
- norm_bias: float32 [2, 2, 1024], P('section'), may hold values from -1.5 to 1.5
- cotangent: bfloat16 [2, 4096, 1024], P(None, ('dp', 'tensor')), may hold values from -6 to 6
Outputs:
- layer_outputs: bfloat16 [2, 2, 4096, 1024], P('section', None, ('dp', 'tensor'))
- grad_inputs: bfloat16 [2, 2, 4096, 1024], P('section', None, ('dp', 'tensor'))
- grad_qkv: float32 [2, 1024, 3, 1024], P('section', None, None, 'tensor')
- grad_out: float32 [2, 1024, 1024], P('section', 'tensor')
- grad_up: float32 [2, 1024, 2048], P('section', None, 'tensor')
- grad_down: float32 [2, 2048, 1024], P('section', 'tensor')
- grad_gain: float32 [2, 2, 1024], P('section', None, 'tensor')
- grad_bias: float32 [2, 2, 1024], P('section', None, 'tensor')
The draws below stay inside these ranges and needn't reach their ends.
Inputs may be any that keep to these rules, and one draw needn't show every extreme that they name: Each row along the last dimension lists in order the lengths of the 25 series packed into the 512 tokens of one micro-batch of one data rank; each row sums to 512 and its longest entry is exactly 60.
All inputs are finite; a program needn't handle non-finite values.
Results may differ from the reference program's by a relative error of at most 0.025.
Values may be sent and summed in bfloat16 or wider, within the bound.
No kernel may reach another device: no remote copies, remote signals or barrier semaphores. Data moves between devices by JAX's collectives and lax.ppermute only.
A program may use at most 128 MiB of HBM per device.

```python
import math
import jax
import jax.numpy as jnp
import numpy as np
from jax import lax

D = 1024
HEADS = 8
HEAD_DIM = 128
FF = 2048
MB = 2
MBTOK = 512
LONGEST = 60
NSER = 25
TOK_MB = 4096
N_DP = 8
N_TENSOR = 2


def block_levels(key, dims, shards, least, top_value):
    def one(position, parts):
        draws = jax.random.uniform(jax.random.fold_in(jax.random.fold_in(key, 6), position), (parts,), jnp.float32, least / len(shards), top_value / len(shards))
        return jnp.repeat(jnp.exp(draws), dims[position] // parts).reshape((-1,) + (1,) * (len(dims) - position - 1))

    level = one(*shards[0])
    for cut in shards[1:]:
        level = level * one(*cut)
    return level


def split_up(amount, total, most, skew):
    loads = [(1 << 20) // math.isqrt(standing ** skew) + 1 for standing in range(2, amount + 1)]
    rest, counts = total - most - (amount - 1), [1] * (amount - 1)
    while rest > 0:
        free = [i for i in range(amount - 1) if counts[i] < most]
        mass, budget = sum([loads[i] for i in free]), rest
        for i in free:
            addition = min(most - counts[i], max(1, budget * loads[i] // mass), rest)
            counts[i] = counts[i] + addition
            rest = rest - addition
    return np.array([most] + counts)


def ragged(own_key, amount, total, most, skew):
    if amount == 2:
        one = jax.random.randint(own_key, (), max(1, total - most), min(most, total - 1) + 1)
        return jnp.stack([one, total - one])
    tallies = jnp.asarray(split_up(amount, total, most, skew), jnp.int32)
    twos = (amount - 1) // 2
    donor, taker = tallies[1:1 + 2 * twos:2], tallies[2:2 + 2 * twos:2]
    slack = jnp.minimum(donor - 1, most - taker)
    shifted = jax.random.randint(jax.random.fold_in(own_key, 1), (twos,), 0, 1 << 20) % (slack + 1)
    tallies = tallies.at[1:1 + 2 * twos:2].set(donor - shifted).at[2:2 + 2 * twos:2].set(taker + shifted)
    return tallies[jax.random.permutation(jax.random.fold_in(own_key, 2), amount)]


def bell_draw(stream_key, shape, deviation, most, cuts=(), held_as=jnp.bfloat16):
    level = block_levels(stream_key, shape, cuts, -0.22, 0.18) if cuts else 1.0
    drawn = jax.random.normal(stream_key, shape, jnp.float32) * deviation * level
    return jnp.minimum(jnp.maximum(drawn, -most), most).astype(held_as)


def setup_inputs(seed: int = 0) -> dict:
    splits = jax.random.split(jax.random.key(seed), 10)
    tokens = bell_draw(splits[0], (MB, TOK_MB, D), 1.0, 6.0, ((1, 16),))
    lengths = jax.vmap(lambda own: ragged(own, NSER, MBTOK, LONGEST, 2))(jax.random.split(splits[1], N_DP * MB)).reshape((N_DP, MB, NSER)).astype(jnp.int32)
    w_qkv = bell_draw(splits[2], (2, D, 3, D), D ** -0.5, 0.1875, ((0, 2), (3, 2)))
    w_out = bell_draw(splits[3], (2, D, D), (D // 8) ** -0.5, 0.5, ((0, 2), (1, 2)))
    w_up = bell_draw(splits[4], (2, D, FF), D ** -0.5, 0.1875, ((0, 2), (2, 2)))
    w_down = bell_draw(splits[5], (2, FF, D), (FF // 2) ** -0.5, 0.1875, ((0, 2), (1, 2)))
    norm_gain = jnp.clip(1.0 + 0.15 * jax.random.normal(splits[6], (2, 2, D), jnp.float32), 0.25, 1.75)
    norm_bias = bell_draw(splits[7], (2, 2, D), 0.3, 1.5, ((0, 2),), jnp.float32)
    cotangent = bell_draw(splits[8], (MB, TOK_MB, D), 1.0, 6.0, ((1, 16),))
    return dict(tokens=tokens, lengths=lengths, w_qkv=w_qkv, w_out=w_out, w_up=w_up, w_down=w_down, norm_gain=norm_gain, norm_bias=norm_bias, cotangent=cotangent)


highest = lax.Precision.HIGHEST
epsilon = 1e-05
masked_score = -1e+30

@jax.custom_vjp
def low(v):
    return lax.optimization_barrier(v.astype(jnp.bfloat16)).astype(jnp.float32)

@jax.custom_vjp
def low_back(v):
    return v

def low_keep(v):
    return (low(v), None)

def low_pass(kept, grad):
    return (grad,)

def back_keep(v):
    return (v, None)

def back_low(kept, grad):
    return (low(grad),)
low.defvjp(low_keep, low_pass)
low_back.defvjp(back_keep, back_low)

def segment_ids(series_lengths, row_count):
    series_ends = jnp.cumsum(series_lengths).astype(jnp.int32)
    places = jnp.arange(row_count, dtype=jnp.int32)
    return lax.optimization_barrier(jnp.sum((places[:, None] >= series_ends[None, :]).astype(jnp.int32), axis=1)).astype(jnp.int32)

def allowed_pairs(series_lengths, row_count):
    segment = segment_ids(series_lengths, row_count)
    places = jnp.arange(row_count, dtype=jnp.int32)
    return (segment[:, None] == segment[None, :]) & (places[None, :] <= places[:, None])

def layer_norm(values, gain_row, bias_row):
    centre = values - lax.optimization_barrier(jnp.mean(values, axis=-1, keepdims=True))
    spread = lax.optimization_barrier(jnp.mean(centre * centre, axis=-1, keepdims=True))
    return centre * lax.rsqrt(spread + epsilon) * gain_row + bias_row

def block_layer(params, layer_input, series_lengths):
    w_qkv, w_out, w_up, w_down, norm_gain, norm_bias = params
    allowed = allowed_pairs(series_lengths, MBTOK)
    first_low = low(layer_norm(layer_input, norm_gain[0], norm_bias[0]))
    qkv_rows = jnp.dot(first_low, w_qkv.reshape(D, 3 * D), precision=highest)
    qkv_rows = low(low_back(qkv_rows)).reshape(MBTOK, 3, HEADS, HEAD_DIM)
    scores = jnp.einsum('thd,shd->hts', qkv_rows[:, 0], qkv_rows[:, 1], precision=highest)
    scores = jnp.where(allowed[None], low_back(scores) * HEAD_DIM ** (-0.5), masked_score)
    row_peak = lax.optimization_barrier(jnp.max(scores, axis=-1, keepdims=True))
    expo_rows = jnp.exp(scores - row_peak)
    attention_probs = low(expo_rows / lax.optimization_barrier(jnp.sum(expo_rows, axis=-1, keepdims=True)))
    heads_out = jnp.einsum('hts,shd->thd', attention_probs, qkv_rows[:, 2], precision=highest).reshape(MBTOK, D)
    heads_out = low(low_back(heads_out))
    head_terms = jnp.einsum('tnk,nkd->ntd', heads_out.reshape(MBTOK, N_TENSOR, D // N_TENSOR), w_out.reshape(N_TENSOR, D // N_TENSOR, D), precision=highest)
    mixed_rows = layer_input + low_back(lax.optimization_barrier(jnp.sum(low(head_terms), axis=0)))
    second_low = low(layer_norm(mixed_rows, norm_gain[1], norm_bias[1]))
    pre_act = low_back(jnp.dot(second_low, w_up, precision=highest))
    hidden_rows = low(jax.nn.gelu(pre_act))
    unit_terms = jnp.einsum('tnk,nkd->ntd', hidden_rows.reshape(MBTOK, N_TENSOR, FF // N_TENSOR), w_down.reshape(N_TENSOR, FF // N_TENSOR, D), precision=highest)
    return mixed_rows + low_back(lax.optimization_barrier(jnp.sum(low(unit_terms), axis=0)))

def run_layer(layer_input, lengths_rows, params):

    def one_block(block_pair):
        return jax.checkpoint(block_layer)(params, block_pair[0], block_pair[1])
    return lax.map(one_block, (layer_input, lengths_rows))

def reference(tokens, lengths, w_qkv, w_out, w_up, w_down, norm_gain, norm_bias, cotangent):
    block_count = MB * N_DP
    lengths_rows = jnp.transpose(lengths, (1, 0, 2)).reshape(block_count, NSER).astype(jnp.int32)
    first_input = tokens.astype(jnp.float32).reshape(block_count, MBTOK, D)
    params = tuple((tuple((weight[layer].astype(jnp.float32) for weight in (w_qkv, w_out, w_up, w_down, norm_gain, norm_bias))) for layer in range(2)))
    returned_probe = jnp.zeros_like(first_input)

    def model(first_input, returned_probe, params):
        first_output = low(run_layer(first_input, lengths_rows, params[0]))
        second_input = low_back(first_output + returned_probe)
        second_output = low(run_layer(second_input, lengths_rows, params[1]))
        return (first_output, second_output)
    (first_output, second_output), pull_back = jax.vjp(model, first_input, returned_probe, params)
    cot_rows = cotangent.astype(jnp.float32).reshape(block_count, MBTOK, D)
    grad_first, grad_second, grad_params = pull_back((jnp.zeros_like(first_output), cot_rows))
    layer_outputs = jnp.stack([first_output, second_output]).reshape(2, MB, TOK_MB, D).astype(jnp.bfloat16)
    grad_inputs = jnp.stack([grad_first, grad_second]).reshape(2, MB, TOK_MB, D).astype(jnp.bfloat16)
    stacked = [jnp.stack([grad_params[0][index], grad_params[1][index]]) for index in range(6)]
    return (layer_outputs, grad_inputs, stacked[0], stacked[1], stacked[2], stacked[3], stacked[4], stacked[5])
```

```python
import functools

import jax
import jax.numpy as jnp
import numpy as np
from jax import lax
from jax.experimental import pallas as pl
from jax.experimental.pallas import tpu as pltpu
from jax.sharding import PartitionSpec as P

HEAD_DIM = 128
BAND = 128
EPSILON = 1e-05
MASKED = -1e30
VMEM = 56 * 1024 * 1024
bf16 = jnp.bfloat16
f32 = jnp.float32


def params(*semantics):
    return pltpu.CompilerParams(
        dimension_semantics=semantics or None, vmem_limit_bytes=VMEM
    )


def cost(flops, moved):
    return pl.CostEstimate(
        flops=int(flops), bytes_accessed=int(moved), transcendentals=0
    )


def dot(a, b):
    return jnp.dot(a, b, preferred_element_type=f32)


def dot_nt(a, b):
    return lax.dot_general(a, b, (((1,), (1,)), ((), ())), preferred_element_type=f32)


def dot_tn(a, b):
    return lax.dot_general(a, b, (((0,), (0,)), ((), ())), preferred_element_type=f32)


def unit_of(values):
    centre = values - jnp.mean(values, axis=-1, keepdims=True)
    spread = jnp.mean(centre * centre, axis=-1, keepdims=True)
    scale = lax.rsqrt(spread + EPSILON)
    return centre * scale, scale


def norm_back(incoming, values, gain):
    unit, scale = unit_of(values)
    scaled = incoming * gain
    inner = (
        scaled
        - jnp.mean(scaled, axis=-1, keepdims=True)
        - unit * jnp.mean(scaled * unit, axis=-1, keepdims=True)
    )
    grads = jnp.concatenate(
        [
            jnp.sum(incoming * unit, axis=0, keepdims=True),
            jnp.sum(incoming, axis=0, keepdims=True),
        ],
        axis=0,
    )
    return scale * inner, grads


def qkv_body(u_ref, gain_ref, bias_ref, w_ref, n1_ref, qkv_ref):
    @pl.when(pl.program_id(0) == 0)
    def _():
        unit, _ = unit_of(u_ref[...].astype(f32))
        n1_ref[...] = (unit * gain_ref[...] + bias_ref[...]).astype(bf16)

    qkv_ref[...] = dot(n1_ref[...], w_ref[...]).astype(bf16)


def qkv_call(u, gain, bias, w):
    rows, width = u.shape
    columns = w.shape[1]
    tile = 512
    return pl.pallas_call(
        qkv_body,
        grid=(columns // tile,),
        in_specs=[
            pl.BlockSpec((rows, width), lambda i: (0, 0)),
            pl.BlockSpec((1, width), lambda i: (0, 0)),
            pl.BlockSpec((1, width), lambda i: (0, 0)),
            pl.BlockSpec((width, tile), lambda i: (0, i)),
        ],
        out_specs=[
            pl.BlockSpec((rows, width), lambda i: (0, 0)),
            pl.BlockSpec((rows, tile), lambda i: (0, i)),
        ],
        out_shape=[
            jax.ShapeDtypeStruct((rows, width), bf16),
            jax.ShapeDtypeStruct((rows, columns), bf16),
        ],
        compiler_params=params("arbitrary"),
        cost_estimate=cost(
            2 * rows * width * columns, 2 * width * columns + 2 * rows * columns
        ),
        name="qkv",
    )(u, gain, bias, w)


def band_probs(q, k, start_ref, block):
    low = max(block - 1, 0) * BAND
    high = (block + 1) * BAND
    keys = k[low:high]
    scores = dot_nt(q[block * BAND : high], keys) * HEAD_DIM**-0.5
    row = lax.broadcasted_iota(jnp.int32, scores.shape, 0) + block * BAND
    column = lax.broadcasted_iota(jnp.int32, scores.shape, 1) + low
    first = start_ref[block * BAND : high, :]
    allowed = (column <= row) & (column >= first)
    scores = jnp.where(allowed, scores, MASKED)
    expo = jnp.exp(scores - jnp.max(scores, axis=-1, keepdims=True))
    return expo / jnp.sum(expo, axis=-1, keepdims=True), low, high


def attention_body(
    heads, q_ref, k_ref, v_ref, start_ref, w_ref, u_ref, gain_ref, bias_ref,
    o_ref, h_ref, n2_ref,
):
    step = pl.program_id(0)
    rows = q_ref.shape[0]
    for head in range(heads):
        cut = slice(head * HEAD_DIM, (head + 1) * HEAD_DIM)
        q, k, v = q_ref[:, cut], k_ref[:, cut], v_ref[:, cut]
        for block in range(rows // BAND):
            probs, low, high = band_probs(q, k, start_ref, block)
            o_ref[block * BAND : high, cut] = dot(probs.astype(bf16), v[low:high]).astype(bf16)
    term = dot(o_ref[...], w_ref[...])

    @pl.when(step == 0)
    def _():
        h_ref[...] = u_ref[...].astype(f32) + term

    @pl.when(step > 0)
    def _():
        h_ref[...] += term

    @pl.when(step == pl.num_programs(0) - 1)
    def _():
        unit, _ = unit_of(h_ref[...])
        n2_ref[...] = (unit * gain_ref[...] + bias_ref[...]).astype(bf16)


def attention_call(qkv, start, w_out, u, gain, bias):
    rows, width = u.shape
    heads = 2
    wide = heads * HEAD_DIM
    steps = w_out.shape[0] // wide
    return pl.pallas_call(
        functools.partial(attention_body, heads),
        grid=(steps,),
        in_specs=[
            pl.BlockSpec((rows, wide), lambda i: (0, i)),
            pl.BlockSpec((rows, wide), lambda i: (0, steps + i)),
            pl.BlockSpec((rows, wide), lambda i: (0, 2 * steps + i)),
            pl.BlockSpec((rows, 1), lambda i: (0, 0)),
            pl.BlockSpec((wide, width), lambda i: (i, 0)),
            pl.BlockSpec((rows, width), lambda i: (0, 0)),
            pl.BlockSpec((1, width), lambda i: (0, 0)),
            pl.BlockSpec((1, width), lambda i: (0, 0)),
        ],
        out_specs=[
            pl.BlockSpec((rows, wide), lambda i: (0, i)),
            pl.BlockSpec((rows, width), lambda i: (0, 0)),
            pl.BlockSpec((rows, width), lambda i: (0, 0)),
        ],
        out_shape=[
            jax.ShapeDtypeStruct((rows, steps * wide), bf16),
            jax.ShapeDtypeStruct((rows, width), f32),
            jax.ShapeDtypeStruct((rows, width), bf16),
        ],
        compiler_params=params("arbitrary"),
        cost_estimate=cost(8e9, 10e6),
        name="attention",
    )(qkv, qkv, qkv, start, w_out, u, gain, bias)


def mlp_body(n2_ref, h_ref, up_ref, down_ref, z_ref, slope_ref, y_ref, total):
    step = pl.program_id(0)
    a = dot(n2_ref[...], up_ref[...])
    c = np.float32(np.sqrt(2 / np.pi))
    square = a * a
    t = jnp.tanh(c * a * (1.0 + 0.044715 * square))
    half = 0.5 * (1.0 + t)
    z = (a * half).astype(bf16)
    slope = half + 0.5 * c * a * (1.0 - t * t) * (1.0 + 3 * 0.044715 * square)
    z_ref[...] = z
    slope_ref[...] = slope.astype(bf16)
    term = dot(z, down_ref[...])

    @pl.when(step == 0)
    def _():
        total[...] = h_ref[...] + term

    @pl.when(step > 0)
    def _():
        total[...] += term

    @pl.when(step == pl.num_programs(0) - 1)
    def _():
        y_ref[...] = total[...].astype(bf16)


def mlp_call(n2, h, w_up, w_down):
    rows, width = h.shape
    units = w_up.shape[1]
    tile = 512
    return pl.pallas_call(
        mlp_body,
        grid=(units // tile,),
        in_specs=[
            pl.BlockSpec((rows, width), lambda i: (0, 0)),
            pl.BlockSpec((rows, width), lambda i: (0, 0)),
            pl.BlockSpec((width, tile), lambda i: (0, i)),
            pl.BlockSpec((tile, width), lambda i: (i, 0)),
        ],
        out_specs=[
            pl.BlockSpec((rows, tile), lambda i: (0, i)),
            pl.BlockSpec((rows, tile), lambda i: (0, i)),
            pl.BlockSpec((rows, width), lambda i: (0, 0)),
        ],
        out_shape=[
            jax.ShapeDtypeStruct((rows, units), bf16),
            jax.ShapeDtypeStruct((rows, units), bf16),
            jax.ShapeDtypeStruct((rows, width), bf16),
        ],
        scratch_shapes=[pltpu.VMEM((rows, width), f32)],
        compiler_params=params("arbitrary"),
        cost_estimate=cost(4 * rows * width * units, 4 * width * units + 8 * rows * units),
        name="mlp",
    )(n2, h, w_up, w_down)


def mlp_back_body(
    gy_ref, slope_ref, up_ref, down_ref, h_ref, gain_ref,
    da_ref, dh_ref, gh_ref, grads_ref, total,
):
    step = pl.program_id(0)
    dz = dot_nt(gy_ref[...], down_ref[...])
    da = (dz * slope_ref[...].astype(f32)).astype(bf16)
    da_ref[...] = da
    term = dot_nt(da, up_ref[...])

    @pl.when(step == 0)
    def _():
        total[...] = term

    @pl.when(step > 0)
    def _():
        total[...] += term

    @pl.when(step == pl.num_programs(0) - 1)
    def _():
        back, grads = norm_back(total[...], h_ref[...], gain_ref[...])
        dh = gy_ref[...].astype(f32) + back
        dh_ref[...] = dh
        gh_ref[...] = dh.astype(bf16)
        grads_ref[...] = grads


def mlp_back_call(gy, slope, w_up, w_down, h, gain):
    rows, width = h.shape
    units = w_up.shape[1]
    tile = 512
    return pl.pallas_call(
        mlp_back_body,
        grid=(units // tile,),
        in_specs=[
            pl.BlockSpec((rows, width), lambda i: (0, 0)),
            pl.BlockSpec((rows, tile), lambda i: (0, i)),
            pl.BlockSpec((width, tile), lambda i: (0, i)),
            pl.BlockSpec((tile, width), lambda i: (i, 0)),
            pl.BlockSpec((rows, width), lambda i: (0, 0)),
            pl.BlockSpec((1, width), lambda i: (0, 0)),
        ],
        out_specs=[
            pl.BlockSpec((rows, tile), lambda i: (0, i)),
            pl.BlockSpec((rows, width), lambda i: (0, 0)),
            pl.BlockSpec((rows, width), lambda i: (0, 0)),
            pl.BlockSpec((2, width), lambda i: (0, 0)),
        ],
        out_shape=[
            jax.ShapeDtypeStruct((rows, units), bf16),
            jax.ShapeDtypeStruct((rows, width), f32),
            jax.ShapeDtypeStruct((rows, width), bf16),
            jax.ShapeDtypeStruct((2, width), f32),
        ],
        scratch_shapes=[pltpu.VMEM((rows, width), f32)],
        compiler_params=params("arbitrary"),
        cost_estimate=cost(4 * rows * width * units, 4 * width * units + 8 * rows * units),
        name="mlp_back",
    )(gy, slope, w_up, w_down, h, gain)


def mlp_grads_body(sec_ref, z_ref, gy_ref, n2_ref, da_ref, out_ref):
    half = out_ref.shape[0] // 2
    out_ref[:half, :] = dot_tn(z_ref[...], gy_ref[...]).astype(bf16)
    out_ref[half:, :] = dot_tn(n2_ref[...], da_ref[...]).astype(bf16)


def mlp_grads_call(sec, z, gy, n2, da):
    rows, width = gy.shape
    units = width
    half = units // 2

    def pick(i, sec_ref):
        return lax.rem(sec_ref[0] + 1 + i, 2)

    return pl.pallas_call(
        mlp_grads_body,
        grid_spec=pltpu.PrefetchScalarGridSpec(
            num_scalar_prefetch=1,
            grid=(2,),
            in_specs=[
                pl.BlockSpec((rows, half), lambda i, s: (0, pick(i, s))),
                pl.BlockSpec((rows, width), lambda i, s: (0, 0)),
                pl.BlockSpec((rows, width // 2), lambda i, s: (0, pick(i, s))),
                pl.BlockSpec((rows, units), lambda i, s: (0, 0)),
            ],
            out_specs=pl.BlockSpec((None, 2 * half, width), lambda i, s: (i, 0, 0)),
        ),
        out_shape=jax.ShapeDtypeStruct((2, 2 * half, width), bf16),
        compiler_params=params("arbitrary"),
        cost_estimate=cost(4 * rows * width * units, 8 * width * units),
        name="mlp_grads",
    )(sec, z, gy, n2, da)


def attention_back_body(
    heads, q_ref, k_ref, v_ref, start_ref, gh_ref, w_ref, dq_ref, dk_ref, dv_ref
):
    rows = q_ref.shape[0]
    blocks = rows // BAND
    do_all = dot_nt(gh_ref[...], w_ref[...]).astype(bf16)
    for head in range(heads):
        cut = slice(head * HEAD_DIM, (head + 1) * HEAD_DIM)
        q, k, v = q_ref[:, cut], k_ref[:, cut], v_ref[:, cut]
        do = do_all[:, cut]
        dk_parts, dv_parts = [None] * blocks, [None] * blocks

        def put(parts, block, term, low):
            for piece in range(term.shape[0] // BAND):
                place = low // BAND + piece
                add = term[piece * BAND : (piece + 1) * BAND]
                parts[place] = add if parts[place] is None else parts[place] + add

        for block in range(blocks):
            probs, low, high = band_probs(q, k, start_ref, block)
            here = slice(block * BAND, high)
            dp = dot_nt(do[here], v[low:high])
            inner = jnp.sum(probs * dp, axis=-1, keepdims=True)
            ds = (probs * (dp - inner) * HEAD_DIM**-0.5).astype(bf16)
            dq_ref[here, cut] = dot(ds, k[low:high]).astype(bf16)
            put(dk_parts, block, dot_tn(ds, q[here]), low)
            put(dv_parts, block, dot_tn(probs.astype(bf16), do[here]), low)
        for block in range(blocks):
            here = slice(block * BAND, (block + 1) * BAND)
            dk_ref[here, cut] = dk_parts[block].astype(bf16)
            dv_ref[here, cut] = dv_parts[block].astype(bf16)


def attention_back_call(qkv, start, gh, w_out):
    rows, width = gh.shape
    heads = 2
    wide = heads * HEAD_DIM
    steps = w_out.shape[0] // wide
    out = jax.ShapeDtypeStruct((rows, steps * wide), bf16)
    return pl.pallas_call(
        functools.partial(attention_back_body, heads),
        grid=(steps,),
        in_specs=[
            pl.BlockSpec((rows, wide), lambda i: (0, i)),
            pl.BlockSpec((rows, wide), lambda i: (0, steps + i)),
            pl.BlockSpec((rows, wide), lambda i: (0, 2 * steps + i)),
            pl.BlockSpec((rows, 1), lambda i: (0, 0)),
            pl.BlockSpec((rows, width), lambda i: (0, 0)),
            pl.BlockSpec((wide, width), lambda i: (i, 0)),
        ],
        out_specs=[pl.BlockSpec((rows, wide), lambda i: (0, i))] * 3,
        out_shape=[out] * 3,
        compiler_params=params("arbitrary"),
        cost_estimate=cost(12e9, 10e6),
        name="attention_back",
    )(qkv, qkv, qkv, start, gh, w_out)


def attention_grads_body(
    sec_ref, o_ref, gh_ref, n1_ref, dq_ref, dk_ref, dv_ref, out_ref
):
    first = o_ref.shape[1]
    local = dq_ref.shape[1]
    out_ref[:first, :] = dot_tn(o_ref[...], gh_ref[...]).astype(bf16)
    for place, ref in enumerate((dq_ref, dk_ref, dv_ref)):
        term = dot_tn(n1_ref[...], ref[...]).astype(bf16)
        deep = term.shape[0] // 2
        at = first + place * deep
        out_ref[at : at + deep, :local] = term[:deep]
        out_ref[at : at + deep, local:] = term[deep:]


def attention_grads_call(sec, o, gh, n1, dq, dk, dv):
    rows, width = gh.shape
    local = width // 2

    def pick(i, sec_ref):
        return lax.rem(sec_ref[0] + 1 + i, 2)

    whole = local // 2 + 3 * width // 4
    return pl.pallas_call(
        attention_grads_body,
        grid_spec=pltpu.PrefetchScalarGridSpec(
            num_scalar_prefetch=1,
            grid=(2,),
            in_specs=[
                pl.BlockSpec((rows, local // 2), lambda i, s: (0, pick(i, s))),
                pl.BlockSpec((rows, width), lambda i, s: (0, 0)),
                pl.BlockSpec((rows, width // 2), lambda i, s: (0, pick(i, s))),
                pl.BlockSpec((rows, local), lambda i, s: (0, 0)),
                pl.BlockSpec((rows, local), lambda i, s: (0, 0)),
                pl.BlockSpec((rows, local), lambda i, s: (0, 0)),
            ],
            out_specs=pl.BlockSpec((None, whole, width), lambda i, s: (i, 0, 0)),
        ),
        out_shape=jax.ShapeDtypeStruct((2, whole, width), bf16),
        compiler_params=params("arbitrary"),
        cost_estimate=cost(4 * rows * width * width, 8 * width * width),
        name="attention_grads",
    )(sec, o, gh, n1, dq, dk, dv)


def input_back_body(
    dq_ref, dk_ref, dv_ref, wq_ref, wk_ref, wv_ref, dh_ref, u_ref, gain_ref,
    du_ref, grads_ref, total,
):
    step = pl.program_id(0)
    term = (
        dot_nt(dq_ref[...], wq_ref[...])
        + dot_nt(dk_ref[...], wk_ref[...])
        + dot_nt(dv_ref[...], wv_ref[...])
    )

    @pl.when(step == 0)
    def _():
        total[...] = term

    @pl.when(step > 0)
    def _():
        total[...] += term

    @pl.when(step == pl.num_programs(0) - 1)
    def _():
        back, grads = norm_back(total[...], u_ref[...].astype(f32), gain_ref[...])
        du_ref[...] = (dh_ref[...] + back).astype(bf16)
        grads_ref[...] = grads


def input_back_call(dq, dk, dv, w_qkv, dh, u, gain):
    rows, width = dh.shape
    tile = 512
    steps = dq.shape[1] // tile
    return pl.pallas_call(
        input_back_body,
        grid=(steps,),
        in_specs=[pl.BlockSpec((rows, tile), lambda i: (0, i))] * 3
        + [
            pl.BlockSpec((width, tile), functools.partial(lambda j, i: (0, j * steps + i), j))
            for j in range(3)
        ]
        + [
            pl.BlockSpec((rows, width), lambda i: (0, 0)),
            pl.BlockSpec((rows, width), lambda i: (0, 0)),
            pl.BlockSpec((1, width), lambda i: (0, 0)),
        ],
        out_specs=[
            pl.BlockSpec((rows, width), lambda i: (0, 0)),
            pl.BlockSpec((2, width), lambda i: (0, 0)),
        ],
        out_shape=[
            jax.ShapeDtypeStruct((rows, width), bf16),
            jax.ShapeDtypeStruct((2, width), f32),
        ],
        scratch_shapes=[pltpu.VMEM((rows, width), f32)],
        compiler_params=params("arbitrary"),
        cost_estimate=cost(
            2 * rows * width * w_qkv.shape[1], 2 * width * w_qkv.shape[1] + 8 * rows * width
        ),
        name="input_back",
    )(dq, dk, dv, w_qkv, w_qkv, w_qkv, dh, u, gain)


def ring_places(count):
    size = min(8, count)
    walk = list(range(0, size, 2)) + list(range(1, size, 2))[::-1]
    return size, walk


def ring_routes(count):
    size, walk = ring_places(count)
    up = []
    for base in range(0, count, size):
        for place in range(size):
            up.append((base + walk[place], base + walk[(place + 1) % size]))
    return up, [(b, a) for a, b in up]


def ring_gather(piece, up, down, size):
    rows = piece.shape[0]
    ups, downs = [piece], [piece]
    reach = (size - 1) // 2
    for _ in range(reach):
        ups.append(lax.ppermute(ups[-1], "dp", up))
        downs.append(lax.ppermute(downs[-1], "dp", down))
    far_up = lax.ppermute(ups[-1][: rows // 2], "dp", up)
    far_down = lax.ppermute(downs[-1][rows // 2 :], "dp", down)
    return jnp.concatenate(ups + downs[1:] + [far_up, far_down], axis=0)


def slot_places(place, size):
    reach = (size - 1) // 2
    steps = list(range(0, -reach - 1, -1)) + list(range(1, reach + 1)) + [size // 2]
    return lax.rem(place + np.asarray(steps, np.int32) + size, size).astype(jnp.int32)


def halving_order(count):
    bits = count.bit_length() - 1
    first = list(range(bits))
    second = [1, 0] + first[2:] if bits > 1 else first
    return first, second


def pairs_of(count, step):
    routes = []
    for core, order in enumerate(halving_order(count)):
        for i in range(count):
            routes.append((core * count + i, core * count + (i ^ (1 << order[step]))))
    return routes


def own_bits(sec, rank, count):
    first, second = halving_order(count)
    return [
        lax.rem(rank >> jnp.where(sec == 0, a, b), 2) for a, b in zip(first, second)
    ]


def halving_sum(kept, received, bits, count):
    rows = kept.shape[0] // 2

    def both(side):
        a = lax.dynamic_slice_in_dim(kept, side * rows, rows, 0).astype(f32)
        b = lax.dynamic_slice_in_dim(received, side * rows, rows, 0).astype(f32)
        return a + b

    away = lax.ppermute(both(1 - bits[0]).astype(bf16), ("section", "dp"), pairs_of(count, 0))
    held = (both(bits[0]) + away.astype(f32)).astype(bf16)
    for step in range(1, len(bits)):
        rows //= 2
        send = lax.dynamic_slice_in_dim(held, (1 - bits[step]) * rows, rows, 0)
        keep = lax.dynamic_slice_in_dim(held, bits[step] * rows, rows, 0)
        away = lax.ppermute(send, ("section", "dp"), pairs_of(count, step))
        held = (keep.astype(f32) + away.astype(f32)).astype(bf16)
    return held


def doubling_gather(held, bits, count):
    for step in reversed(range(len(bits))):
        away = lax.ppermute(held, ("section", "dp"), pairs_of(count, step))
        low = bits[step] == 0
        held = jnp.concatenate([jnp.where(low, held, away), jnp.where(low, away, held)], axis=0)
    return held


def place_attention_body(
    size, sec_ref, at_ref, mine_qkv, swap_qkv, mine_out, swap_out, own_ref, far_ref,
    qkv_ref, out_ref, sem,
):
    layer, sec = at_ref[size], sec_ref[0]
    width = out_ref.shape[1]
    local = width // 2
    copies = []

    def put(source, target):
        copies.append(pltpu.make_async_copy(source, target, sem.at[len(copies)]))

    def put_own(qkv, out):
        for j in range(3):
            yield pltpu.make_async_copy(
                qkv.at[:, j * local : (j + 1) * local],
                qkv_ref.at[:, j * width : j * width + local],
                sem.at[j],
            )
        yield pltpu.make_async_copy(out, out_ref.at[:local, :], sem.at[3])

    @pl.when(layer == sec)
    def _():
        for c in put_own(mine_qkv, mine_out):
            c.start()

    @pl.when(layer != sec)
    def _():
        for c in put_own(swap_qkv, swap_out):
            c.start()

    rows = width // size // 2
    out_rows = local // size // 2

    def each(act):
        def body(slot, _):
            place = at_ref[slot]
            for side, ref in ((0, own_ref), (1, far_ref)):
                core = lax.rem(sec + side, 2)
                source = slot * 2 * rows
                row = place * 2 * rows + core * rows
                out_row = local + place * 2 * out_rows + core * out_rows
                base = 4 + side
                act(
                    ref.at[pl.ds(source, rows), :local],
                    qkv_ref.at[pl.ds(row, rows), local:width],
                    sem.at[base],
                )
                act(
                    ref.at[pl.ds(source, rows), local:],
                    qkv_ref.at[pl.ds(row, rows), width + local : 2 * width],
                    sem.at[base],
                )
                for part in range(2):
                    act(
                        ref.at[pl.ds(source + rows, rows // 2), part * local : (part + 1) * local],
                        qkv_ref.at[
                            pl.ds(row + part * (rows // 2), rows // 2), 2 * width + local :
                        ],
                        sem.at[base],
                    )
                act(
                    ref.at[pl.ds(source + rows + rows // 2, out_rows), :],
                    out_ref.at[pl.ds(out_row, out_rows), :],
                    sem.at[base],
                )
            return 0

        lax.fori_loop(0, size, body, 0)

    each(lambda a, b, s: pltpu.make_async_copy(a, b, s).start())
    for c in put_own(mine_qkv, mine_out):
        c.wait()
    for side, ref in ((0, own_ref), (1, far_ref)):
        pltpu.make_async_copy(ref, ref, sem.at[4 + side]).wait()


def any_specs(n):
    return [pl.BlockSpec(memory_space=pl.ANY)] * n


def place_attention_call(size, sec, at, mine_qkv, swap_qkv, mine_out, swap_out, own, far):
    width = mine_qkv.shape[0]
    return pl.pallas_call(
        functools.partial(place_attention_body, size),
        in_specs=[pl.BlockSpec(memory_space=pltpu.SMEM)] * 2 + any_specs(6),
        out_specs=[pl.BlockSpec(memory_space=pltpu.VMEM)] * 2,
        out_shape=[
            jax.ShapeDtypeStruct((width, 3 * width), bf16),
            jax.ShapeDtypeStruct((width, width), bf16),
        ],
        scratch_shapes=[pltpu.SemaphoreType.DMA((6,))],
        compiler_params=params(),
        cost_estimate=cost(0, 16 * width * width),
        name="place_attention",
    )(sec, at, mine_qkv, swap_qkv, mine_out, swap_out, own, far)


def place_mlp_body(
    size, direct, sec_ref, at_ref, mine_up, swap_up, mine_down, swap_down, own_ref, far_ref,
    up_ref, down_ref, sem,
):
    layer, sec = at_ref[size], sec_ref[0]
    units = up_ref.shape[1] // 2

    def put_own(up, down):
        yield pltpu.make_async_copy(up, up_ref.at[:, :units], sem.at[0])
        yield pltpu.make_async_copy(down, down_ref.at[:units, :], sem.at[1])

    @pl.when(layer == sec)
    def _():
        for c in put_own(mine_up, mine_down):
            c.start()

    @pl.when(layer != sec)
    def _():
        for c in put_own(swap_up, swap_down):
            c.start()

    rows = units // 2 if direct else units // size // 2

    def body(slot, _):
        place = 0 if direct else at_ref[slot]
        for side, ref in ((0, own_ref), (1, far_ref)):
            core = lax.rem(sec + side, 2)
            source = slot * 2 * rows
            row = place * 2 * rows + core * rows
            pltpu.make_async_copy(
                ref.at[pl.ds(source, rows), :],
                up_ref.at[pl.ds(row, rows), units:],
                sem.at[2 + side],
            ).start()
            pltpu.make_async_copy(
                ref.at[pl.ds(source + rows, rows), :],
                down_ref.at[pl.ds(units + row, rows), :],
                sem.at[2 + side],
            ).start()
        return 0

    lax.fori_loop(0, 1 if direct else size, body, 0)
    for c in put_own(mine_up, mine_down):
        c.wait()
    for side, ref in ((0, own_ref), (1, far_ref)):
        pltpu.make_async_copy(ref, ref, sem.at[2 + side]).wait()


def place_mlp_call(size, direct, sec, at, mine_up, swap_up, mine_down, swap_down, own, far):
    width, units = mine_up.shape
    return pl.pallas_call(
        functools.partial(place_mlp_body, size, direct),
        in_specs=[pl.BlockSpec(memory_space=pltpu.SMEM)] * 2 + any_specs(6),
        out_specs=[pl.BlockSpec(memory_space=pltpu.VMEM)] * 2,
        out_shape=[
            jax.ShapeDtypeStruct((width, 2 * units), bf16),
            jax.ShapeDtypeStruct((2 * units, width), bf16),
        ],
        scratch_shapes=[pltpu.SemaphoreType.DMA((4,))],
        compiler_params=params(),
        cost_estimate=cost(0, 16 * width * units),
        name="place_mlp",
    )(sec, at, mine_up, swap_up, mine_down, swap_down, own, far)


def final_mlp_body(
    sec_ref, own0, far0, own1, far1, down_ref, up_ref, held, sem
):
    sec = sec_ref[0]
    whole = held.shape[1]

    def start(own, far):
        for side, ref in ((0, own), (1, far)):
            pltpu.make_async_copy(ref, held.at[side], sem.at[side]).start()

    @pl.when(sec == 0)
    def _():
        start(own0, far0)

    @pl.when(sec != 0)
    def _():
        start(own1, far1)

    half = whole // 2
    for side in range(2):
        pltpu.make_async_copy(own0, held.at[side], sem.at[side]).wait()
    for side in range(2):
        at = pl.multiple_of(lax.rem(sec + side, 2) * half, half)
        down_ref[pl.ds(at, half), :] = held[side, :half, :].astype(f32)
        up_ref[pl.ds(at, half), :] = held[side, half:, :].astype(f32)


def final_mlp_call(sec, own0, far0, own1, far1):
    whole, width = own0.shape
    return pl.pallas_call(
        final_mlp_body,
        in_specs=[pl.BlockSpec(memory_space=pltpu.SMEM)] + any_specs(4),
        out_specs=[pl.BlockSpec(memory_space=pltpu.VMEM)] * 2,
        out_shape=[jax.ShapeDtypeStruct((whole, width), f32)] * 2,
        scratch_shapes=[
            pltpu.VMEM((2, whole, width), bf16),
            pltpu.SemaphoreType.DMA((2,)),
        ],
        compiler_params=params(),
        cost_estimate=cost(0, 12 * whole * width),
        name="final_mlp",
    )(sec, own0, far0, own1, far1)


def final_attention_body(
    sec_ref, own0, far0, own1, far1, out_ref, qkv_ref, held, sem
):
    sec = sec_ref[0]
    whole = held.shape[1]

    def start(own, far):
        for side, ref in ((0, own), (1, far)):
            pltpu.make_async_copy(ref, held.at[side], sem.at[side]).start()

    @pl.when(sec == 0)
    def _():
        start(own0, far0)

    @pl.when(sec != 0)
    def _():
        start(own1, far1)

    first = out_ref.shape[0] // 2
    local = qkv_ref.shape[2]
    deep = qkv_ref.shape[1] // 4
    for side in range(2):
        pltpu.make_async_copy(own0, held.at[side], sem.at[side]).wait()
    for side in range(2):
        core = lax.rem(sec + side, 2)
        at = pl.multiple_of(core * first, first)
        out_ref[pl.ds(at, first), :] = held[side, :first, :].astype(f32)
        low = pl.multiple_of(core * 2 * deep, 2 * deep)
        for j in range(3):
            block = held[side, first + j * deep : first + (j + 1) * deep, :].astype(f32)
            qkv_ref[j, pl.ds(low, deep), :] = block[:, :local]
            qkv_ref[j, pl.ds(low + deep, deep), :] = block[:, local:]


def final_attention_call(sec, own0, far0, own1, far1):
    whole, width = own0.shape
    local = width // 2
    return pl.pallas_call(
        final_attention_body,
        in_specs=[pl.BlockSpec(memory_space=pltpu.SMEM)] + any_specs(4),
        out_specs=[pl.BlockSpec(memory_space=pltpu.VMEM)] * 2,
        out_shape=[
            jax.ShapeDtypeStruct((local, width), f32),
            jax.ShapeDtypeStruct((3, width, local), f32),
        ],
        scratch_shapes=[
            pltpu.VMEM((2, whole, width), bf16),
            pltpu.SemaphoreType.DMA((2,)),
        ],
        compiler_params=params(),
        cost_estimate=cost(0, 12 * whole * width),
        name="final_attention",
    )(sec, own0, far0, own1, far1)


def series_starts(lengths, rows):
    ends = jnp.cumsum(lengths)
    places = jnp.arange(rows, dtype=jnp.int32)
    passed = jnp.where(ends[None, :] <= places[:, None], ends[None, :], 0)
    return jnp.max(passed, axis=1, keepdims=True).astype(jnp.int32)


def per_device(tokens, lengths, w_qkv, w_out, w_up, w_down, norm_gain, norm_bias, cotangent):
    sec = lax.axis_index("section")
    tensor = lax.axis_index("tensor")
    rank = lax.axis_index("dp")
    count = lax.axis_size("dp")
    own_rows = tokens.shape[1]
    rows = 2 * own_rows
    width = tokens.shape[2]
    local = width // 2
    swap = [(0, 1), (1, 0)]
    size, walk = ring_places(count)
    up, down = ring_routes(count)
    place = jnp.asarray(np.argsort(walk), jnp.int32)[lax.rem(rank, size)]
    slots = slot_places(place, size)
    sec_one = sec.astype(jnp.int32).reshape(1)
    bits = own_bits(sec, rank, count)
    at_layer = [
        jnp.concatenate([slots, jnp.full((1,), layer, jnp.int32)]) for layer in range(2)
    ]

    def across(shard):
        other = lax.ppermute(shard, "tensor", swap)
        return jnp.where(
            tensor == 0,
            jnp.concatenate([shard, other], axis=0),
            jnp.concatenate([other, shard], axis=0),
        )

    def to_other_core(value):
        return lax.ppermute(value, "section", swap)

    mine = (w_qkv[0].reshape(width, 3 * local), w_out[0], w_up[0], w_down[0])
    u0 = across(lax.dynamic_index_in_dim(tokens, sec, 0, False))
    gy1 = across(lax.dynamic_index_in_dim(cotangent, sec, 0, False))
    start = series_starts(lax.dynamic_index_in_dim(lengths[0], sec, 0, False), rows)
    norms = jnp.concatenate([norm_gain[0], norm_bias[0]], axis=0)
    swap_norms = to_other_core(norms)
    norm_of = [
        jnp.where(sec == 0, norms, swap_norms),
        jnp.where(sec == 0, swap_norms, norms),
    ]

    step = width // size
    fine = step // 2

    def attention_piece(core):
        low = place * step + core * fine
        q, k, v = (
            lax.dynamic_slice(mine[0], (low, j * local), (fine, local)) for j in range(3)
        )
        out = lax.dynamic_slice_in_dim(
            mine[1], place * (step // 2) + core * (fine // 2), fine // 2, 0
        )
        return jnp.concatenate(
            [
                jnp.concatenate([q, k], axis=1),
                jnp.concatenate([v[: fine // 2], v[fine // 2 :]], axis=1),
                out,
            ],
            axis=0,
        )

    def mlp_piece(core, pieces):
        span = width // pieces
        low = (place if pieces > 1 else 0) * span + core * (span // 2)
        return jnp.concatenate(
            [
                lax.dynamic_slice_in_dim(mine[2], low, span // 2, 0),
                lax.dynamic_slice_in_dim(mine[3], low, span // 2, 0),
            ],
            axis=0,
        )

    def shares(make):
        kept = make(sec)
        came = to_other_core(make(1 - sec))
        return jnp.where(sec == 0, kept, came), jnp.where(sec == 0, came, kept)

    attention_share = shares(attention_piece)
    mlp_share = shares(lambda core: mlp_piece(core, size))
    direct_share = shares(lambda core: mlp_piece(core, 1))

    def through_ring(piece):
        crossed = lax.ppermute(piece, "tensor", swap)
        own = ring_gather(crossed, up, down, size)
        return own, to_other_core(own)

    swapped = tuple(to_other_core(w) for w in mine)

    weights = []
    for layer in range(2):
        own, far = through_ring(attention_share[layer])
        qkv_full, out_full = place_attention_call(
            size, sec_one, at_layer[layer], mine[0], swapped[0], mine[1], swapped[1], own, far
        )
        if layer == 0:
            own, far = through_ring(mlp_share[layer])
        else:
            own = lax.ppermute(direct_share[layer], "tensor", swap)
            far = to_other_core(own)
        up_full, down_full = place_mlp_call(
            size, layer == 1, sec_one, at_layer[layer], mine[2], swapped[2], mine[3], swapped[3], own, far
        )
        weights.append((qkv_full, out_full, up_full, down_full))

    kept = []
    u = u0
    layer_out = []
    for layer in range(2):
        qkv_full, out_full, up_full, down_full = weights[layer]
        norm = norm_of[layer]
        n1, qkv = qkv_call(u, norm[0:1], norm[2:3], qkv_full)
        o, h, n2 = attention_call(qkv, start, out_full, u, norm[1:2], norm[3:4])
        z, slope, y = mlp_call(n2, h, up_full, down_full)
        kept.append((u, n1, qkv, o, h, n2, z, slope))
        layer_out.append(y)
        u = y

    gy = gy1
    totals = [None, None]
    norm_grads = [None, None]
    grad_in = [None, None]
    for layer in (1, 0):
        qkv_full, out_full, up_full, down_full = weights[layer]
        norm = norm_of[layer]
        u, n1, qkv, o, h, n2, z, slope = kept[layer]
        da, dh, gh, grads_two = mlp_back_call(gy, slope, up_full, down_full, h, norm[1:2])
        both = mlp_grads_call(sec_one, z, gy, n2, da)
        mlp_total = doubling_gather(
            halving_sum(both[1], to_other_core(both[0]), bits, count), bits, count
        )
        gh = lax.optimization_barrier((gh, both))[0]
        dq, dk, dv = attention_back_call(qkv, start, gh, out_full)
        both = attention_grads_call(sec_one, o, gh, n1, dq, dk, dv)
        attention_total = doubling_gather(
            halving_sum(both[1], to_other_core(both[0]), bits, count), bits, count
        )
        dh = lax.optimization_barrier((dh, both))[0]
        du, grads_one = input_back_call(dq, dk, dv, qkv_full, dh, u, norm[0:1])
        send = [(1 - layer, layer)]
        totals[layer] = (
            mlp_total,
            lax.ppermute(mlp_total, "section", send),
            attention_total,
            lax.ppermute(attention_total, "section", send),
        )
        norm_grads[layer] = jnp.concatenate([grads_one[:1], grads_two[:1], grads_one[1:], grads_two[1:]])
        grad_in[layer] = du
        gy = du

    grad_down, grad_up = final_mlp_call(
        sec_one, totals[0][0], totals[0][1], totals[1][0], totals[1][1]
    )
    grad_out, grad_qkv = final_attention_call(
        sec_one, totals[0][2], totals[0][3], totals[1][2], totals[1][3]
    )

    def butterfly(part):
        part = part + to_other_core(part)
        distance = 1
        while distance < count:
            part = part + lax.ppermute(part, "dp", [(i, i ^ distance) for i in range(count)])
            distance *= 2
        return part

    norm_total = [butterfly(part) for part in norm_grads]
    norm_sum = jnp.where(sec == 0, norm_total[0], norm_total[1])
    norm_sum = lax.dynamic_slice_in_dim(norm_sum, tensor * local, local, 1)

    def to_outputs(pair):
        rows_of = [
            lax.dynamic_slice_in_dim(value, tensor * own_rows, own_rows, 0) for value in pair
        ]
        stay = jnp.where(sec == 0, rows_of[0], rows_of[1])
        go = jnp.where(sec == 0, rows_of[1], rows_of[0])
        came = to_other_core(go)
        return jnp.where(sec == 0, jnp.stack([stay, came]), jnp.stack([came, stay]))[None]

    return (
        to_outputs(layer_out),
        to_outputs(grad_in),
        jnp.transpose(grad_qkv, (1, 0, 2))[None],
        grad_out[None],
        grad_up[None],
        grad_down[None],
        norm_sum[None, :2],
        norm_sum[None, 2:],
    )


def solution(mesh):
    in_specs = (
        P(None, ("dp", "tensor"), None),
        P("dp", None, None),
        P("section", None, None, "tensor"),
        P("section", "tensor", None),
        P("section", None, "tensor"),
        P("section", "tensor", None),
        P("section", None, None),
        P("section", None, None),
        P(None, ("dp", "tensor"), None),
    )
    out_specs = (
        P("section", None, ("dp", "tensor"), None),
        P("section", None, ("dp", "tensor"), None),
        P("section", None, None, "tensor"),
        P("section", "tensor", None),
        P("section", None, "tensor"),
        P("section", "tensor", None),
        P("section", None, "tensor"),
        P("section", None, "tensor"),
    )
    return jax.shard_map(
        per_device, mesh=mesh, in_specs=in_specs, out_specs=out_specs, check_vma=False
    )
```

```python
import functools

import jax
import jax.numpy as jnp
import numpy as np
from jax import lax
from jax.experimental import pallas as pl
from jax.experimental.pallas import tpu as pltpu
from jax.sharding import PartitionSpec as P

HEAD_DIM = 128
BAND = 128
EPSILON = 1e-05
MASKED = -1e30
VMEM = 60 * 1024 * 1024
bf16 = jnp.bfloat16
f32 = jnp.float32


def params():
    return pltpu.CompilerParams(vmem_limit_bytes=VMEM)


def cost(flops, moved):
    return pl.CostEstimate(
        flops=int(flops), bytes_accessed=int(moved), transcendentals=0
    )


def dot(a, b):
    return jnp.dot(a, b, preferred_element_type=f32)


def dot_nt(a, b):
    return lax.dot_general(a, b, (((1,), (1,)), ((), ())), preferred_element_type=f32)


def dot_tn(a, b):
    return lax.dot_general(a, b, (((0,), (0,)), ((), ())), preferred_element_type=f32)


def unit_of(values):
    centre = values - jnp.mean(values, axis=-1, keepdims=True)
    spread = jnp.mean(centre * centre, axis=-1, keepdims=True)
    scale = lax.rsqrt(spread + EPSILON)
    return centre * scale, scale


def norm_back(incoming, values, gain):
    unit, scale = unit_of(values)
    scaled = incoming * gain
    inner = (
        scaled
        - jnp.mean(scaled, axis=-1, keepdims=True)
        - unit * jnp.mean(scaled * unit, axis=-1, keepdims=True)
    )
    grads = jnp.concatenate(
        [
            jnp.sum(incoming * unit, axis=0, keepdims=True),
            jnp.sum(incoming, axis=0, keepdims=True),
        ],
        axis=0,
    )
    return scale * inner, grads


def any_specs(n):
    return [pl.BlockSpec(memory_space=pl.ANY)] * n


class Own:
    def __init__(self, layer, sec, mine, swapped):
        self.scalars = jnp.stack([sec, jnp.full_like(sec, layer)])
        self.mine, self.swapped = mine, swapped

    def operands(self, names):
        return [self.mine[n] for n in names] + [self.swapped[n] for n in names]

    def start(self, names, scalars, refs, targets, sems):
        mine, swapped = refs[: len(names)], refs[len(names) :]
        for condition, side in ((True, mine), (False, swapped)):

            @pl.when((scalars[0] == scalars[1]) == condition)
            def _():
                for n, (ref, target) in enumerate(zip(side, targets)):
                    pltpu.make_async_copy(ref, target, sems.at[n, 0]).start()

    def wait(self, n, name, target, sems):
        pltpu.make_async_copy(target, target, sems.at[n, 0]).wait()


class Pieces:
    def __init__(self, sec, places, own, far):
        self.count = len(own)
        self.scalars = jnp.concatenate([sec.reshape(1), places])
        self.arrays, self.index = [], []
        for side in (own, far):
            rows = []
            for slot in side:
                parts = []
                for array, row in slot:
                    known = [n for n, x in enumerate(self.arrays) if x is array]
                    if not known:
                        self.arrays.append(array)
                        known = [len(self.arrays) - 1]
                    parts.append((known[0], row))
                rows.append(parts)
            self.index.append(rows)

    def operands(self, names):
        return self.arrays

    def start(self, names, scalars, refs, targets, sems):
        every = slice(None)
        for side, slots in enumerate(self.index):
            core = lax.rem(scalars[0] + side, 2)
            for slot, ((n0, row0), (n1, row1)) in enumerate(slots):
                spot = scalars[1 + slot] * 2 + core
                first, second = refs[n0], refs[n1]
                for n, (name, target) in enumerate(zip(names, targets)):

                    def put(source, place):
                        pltpu.make_async_copy(source, place, sems.at[n, side]).start()

                    if name == "qkv":
                        deep, local = target.shape[1], target.shape[2]
                        fine = deep // self.count // 2
                        half = fine // 2
                        row = spot * fine
                        for j in range(2):
                            columns = slice(j * local, (j + 1) * local)
                            put(
                                first.at[row0 : row0 + fine, columns],
                                target.at[j, pl.ds(row, fine), :],
                            )
                            put(
                                second.at[row1 : row1 + half, columns],
                                target.at[2, pl.ds(row + j * half, half), :],
                            )
                    elif name == "out":
                        fine = target.shape[0] // self.count // 2
                        put(
                            second.at[row1 + fine : row1 + 2 * fine, every],
                            target.at[pl.ds(spot * fine, fine), :],
                        )
                    else:
                        fine = target.shape[0] // self.count // 2
                        source = second.at[row1 : row1 + fine, every] if name == "down" else first.at[row0 : row0 + fine, every]
                        put(source, target.at[pl.ds(spot * fine, fine), :])

    def wait(self, n, name, target, sems):
        for side in range(2):
            if name == "qkv":
                part = target.at[:, : target.shape[1] // 2, :]
            else:
                part = target.at[: target.shape[0] // 2, :]
            pltpu.make_async_copy(part, part, sems.at[n, side]).wait()


def struct(shape, dtype):
    return jax.ShapeDtypeStruct(shape, dtype)


class Room:
    def __init__(self, refs, sources, sinks, in_sems, out_sems, weights):
        self.refs, self.sources, self.sinks = refs, sources, sinks
        self.in_sems, self.out_sems, self.weights = in_sems, out_sems, weights
        self.waited, self.leaving = set(), []

    def start(self, names):
        for n, name in enumerate(names):
            pltpu.make_async_copy(self.sources[name], self.refs[name], self.in_sems.at[n]).start()
        self.order = list(names)

    def get(self, name):
        if name in self.sources and name not in self.waited:
            self.waited.add(name)
            ref = self.refs[name]
            pltpu.make_async_copy(ref, ref, self.in_sems.at[self.order.index(name)]).wait()
        return self.refs[name]

    def weight(self, name):
        loader, place, kind, target, sems = self.weights[name]
        if name not in self.waited:
            self.waited.add(name)
            loader.wait(place, kind, target, sems)
        return target

    def send(self, pairs):
        for source, sink in pairs:
            copy = pltpu.make_async_copy(source, sink, self.out_sems.at[len(self.leaving)])
            copy.start()
            self.leaving.append(copy)

    def flush(self, *names):
        self.send([(self.refs[name], self.sinks[name]) for name in names])

    def close(self):
        for copy in self.leaving:
            copy.wait()


def room_call(name, body, scalars, weights, inputs, outputs, scratch, copies, flops):
    in_names, out_names, temp_names = list(inputs), list(outputs), list(scratch)
    operands = [loader.operands([k for k, _ in kinds]) for _, loader, kinds in weights]
    scalar_list = [scalars] + [loader.scalars for _, loader, _ in weights]
    local_out = [n for n in out_names if n not in scratch]

    def whole(*refs):
        refs = list(refs)

        def take(n):
            got = refs[:n]
            del refs[:n]
            return got

        scalar_refs = take(len(scalar_list))
        sources = dict(zip(in_names, take(len(in_names))))
        weight_sources = [take(len(o)) for o in operands]
        sinks = dict(zip(out_names, take(len(out_names))))
        held = dict(zip(in_names, take(len(in_names))))
        held.update(zip(local_out, take(len(local_out))))
        held.update(zip(temp_names, take(len(temp_names))))
        in_sems, out_sems = take(2)
        table = {}
        starts = []
        for (prefix, loader, kinds), source, scalar in zip(weights, weight_sources, scalar_refs[1:]):
            targets = take(len(kinds))
            sems = take(1)[0]
            starts.append((loader, [k for k, _ in kinds], scalar, source, targets, sems))
            for place, (kind, _) in enumerate(kinds):
                table[prefix + kind] = (loader, place, kind, targets[place], sems)
        room = Room(held, sources, sinks, in_sems, out_sems, table)
        room.start(in_names)
        for loader, kinds, scalar, source, targets, sems in starts:
            loader.start(kinds, scalar, source, targets, sems)
        body(room, scalar_refs[0])
        for name in in_names:
            room.get(name)
        for key in table:
            room.weight(key)
        room.close()

    vmem = [pltpu.VMEM(inputs[n].shape, inputs[n].dtype) for n in in_names]
    vmem += [pltpu.VMEM(outputs[n].shape, outputs[n].dtype) for n in local_out]
    vmem += [pltpu.VMEM(*scratch[n]) for n in temp_names]
    vmem += [pltpu.SemaphoreType.DMA((max(len(in_names), 1),)), pltpu.SemaphoreType.DMA((copies,))]
    for _, _, kinds in weights:
        vmem += [pltpu.VMEM(shape, bf16) for _, shape in kinds]
        vmem.append(pltpu.SemaphoreType.DMA((len(kinds), 2)))
    flat = [x for o in operands for x in o]
    moved = sum(x.size * x.dtype.itemsize for x in list(inputs.values()) + list(outputs.values()))
    moved += sum(2 * int(np.prod(shape)) for _, _, kinds in weights for _, shape in kinds)
    result = pl.pallas_call(
        whole,
        in_specs=[pl.BlockSpec(memory_space=pltpu.SMEM)] * len(scalar_list)
        + any_specs(len(in_names) + len(flat)),
        out_specs=any_specs(len(out_names)),
        out_shape=[outputs[n] for n in out_names],
        scratch_shapes=vmem,
        compiler_params=params(),
        cost_estimate=cost(flops, moved),
        name=name,
    )(*scalar_list, *inputs.values(), *flat)
    return dict(zip(out_names, result))


def band_probs(q, k, start_ref, block):
    low = max(block - 1, 0) * BAND
    high = (block + 1) * BAND
    scores = dot_nt(q[block * BAND : high], k[low:high]) * HEAD_DIM**-0.5
    row = lax.broadcasted_iota(jnp.int32, scores.shape, 0) + block * BAND
    column = lax.broadcasted_iota(jnp.int32, scores.shape, 1) + low
    first = start_ref[block * BAND : high, :]
    allowed = (column <= row) & (column >= first)
    scores = jnp.where(allowed, scores, MASKED)
    expo = jnp.exp(scores - jnp.max(scores, axis=-1, keepdims=True))
    return expo / jnp.sum(expo, axis=-1, keepdims=True), low, high


def heads_of(qkv_ref, head, local):
    return [
        qkv_ref[:, j * local + head * HEAD_DIM : j * local + (head + 1) * HEAD_DIM] for j in range(3)
    ]


def attend(qkv_ref, start_ref, o_ref):
    rows, local = o_ref.shape
    for head in range(local // HEAD_DIM):
        cut = slice(head * HEAD_DIM, (head + 1) * HEAD_DIM)
        q, k, v = heads_of(qkv_ref, head, local)
        for block in range(rows // BAND):
            probs, low, high = band_probs(q, k, start_ref, block)
            o_ref[block * BAND : high, cut] = dot(probs.astype(bf16), v[low:high]).astype(bf16)


def project(left, w, out_ref):
    local = w.shape[2]
    for j in range(3):
        out_ref[:, j * local : (j + 1) * local] = dot(left[...], w[j]).astype(bf16)


def activate(n2_ref, up, z_ref, slope_ref):
    c = np.float32(np.sqrt(2 / np.pi))
    tile = 512
    for i in range(z_ref.shape[1] // tile):
        cut = slice(i * tile, (i + 1) * tile)
        a = dot(n2_ref[...], up[:, cut])
        square = a * a
        t = jnp.tanh(c * a * (1.0 + 0.044715 * square))
        half = 0.5 * (1.0 + t)
        slope = half + 0.5 * c * a * (1.0 - t * t) * (1.0 + 3 * 0.044715 * square)
        z_ref[:, cut] = (a * half).astype(bf16)
        slope_ref[:, cut] = slope.astype(bf16)


def sizes(width):
    local, units = width // 2, width
    return {
        "qkv": (3, width, local),
        "out": (local, width),
        "up": (width, units),
        "down": (units, width),
    }


def group(prefix, loader, kinds, width):
    return prefix, loader, [(k, sizes(width)[k]) for k in kinds]


def first_call(scalars, own, u, start, gain, bias):
    rows, width = u.shape
    local = width // 2

    def body(room, _):
        u_ref = room.get("u")
        unit, _ = unit_of(u_ref[...].astype(f32))
        n1 = room.get("n1")
        n1[...] = (unit * room.get("gain")[...] + room.get("bias")[...]).astype(bf16)
        project(n1, room.weight("own_qkv"), room.get("qkv"))
        room.flush("n1", "qkv")
        attend(room.get("qkv"), room.get("start"), room.get("o"))
        room.flush("o")
        room.get("h")[...] = u_ref[...].astype(f32) + dot(room.get("o")[...], room.weight("own_out")[...])
        room.flush("h")

    return room_call(
        "first", body, scalars, [group("own_", own, ["qkv", "out"], width)],
        dict(u=u, start=start, gain=gain, bias=bias),
        dict(n1=struct((rows, width), bf16), qkv=struct((rows, 3 * local), bf16),
             o=struct((rows, local), bf16), h=struct((rows, width), f32)),
        {}, 4, 9 * rows * width * local,
    )


def second_call(scalars, far, n1, start, base, gain, bias):
    rows, width = base.shape
    local = width // 2

    def body(room, _):
        project(room.get("n1"), room.weight("far_qkv"), room.get("qkv"))
        room.flush("qkv")
        attend(room.get("qkv"), room.get("start"), room.get("o"))
        h = room.get("base")[...] + dot(room.get("o")[...], room.weight("far_out")[...])
        room.get("h")[...] = h
        unit, _ = unit_of(h)
        n2 = room.get("n2")
        n2[...] = (unit * room.get("gain")[...] + room.get("bias")[...]).astype(bf16)
        room.flush("h", "n2")

    return room_call(
        "second", body, scalars, [group("far_", far, ["qkv", "out"], width)],
        dict(n1=n1, start=start, base=base, gain=gain, bias=bias),
        dict(qkv=struct((rows, 3 * local), bf16), h=struct((rows, width), f32),
             n2=struct((rows, width), bf16)),
        dict(o=((rows, local), bf16)), 3, 9 * rows * width * local,
    )


def feed_call(scalars, own, far_two, n2, h):
    rows, width = h.shape
    units = width

    def body(room, _):
        n2 = room.get("n2")
        activate(n2, room.weight("own_up"), room.get("z"), room.get("slope"))
        room.flush("z", "slope")
        activate(n2, room.weight("two_up"), room.get("z_far"), room.get("slope_far"))
        room.flush("slope_far")
        y = room.get("h")[...] + dot(room.get("z")[...], room.weight("own_down")[...])
        room.get("y")[...] = (y + dot(room.get("z_far")[...], room.weight("two_down")[...])).astype(bf16)
        room.flush("y")

    tall = struct((rows, width), bf16)
    return room_call(
        "feed", body, scalars,
        [group("own_", own, ["up", "down"], width), group("two_", far_two, ["up", "down"], width)],
        dict(n2=n2, h=h), dict(z=tall, slope=tall, slope_far=tall, y=tall),
        dict(z_far=((rows, units), bf16)), 4, 8 * rows * width * units,
    )


def feed_back_call(scalars, own, far_two, gy, slope, slope_far, h, z, n2, gain):
    rows, width = gy.shape
    units = width
    half = units // 2

    def body(room, scalar):
        gy_ref = room.get("gy")
        dz = dot_nt(gy_ref[...], room.weight("own_down")[...])
        da = room.get("da")
        da[...] = (dz * room.get("slope")[...].astype(f32)).astype(bf16)
        down, up = room.get("grad_down"), room.get("grad_up")
        down[...] = dot_tn(room.get("z")[...], gy_ref[...]).astype(bf16)
        up[...] = dot_tn(room.get("n2")[...], da[...]).astype(bf16)
        for name, which in (("give", 1 - scalar[0]), ("keep", scalar[0])):
            at = pl.multiple_of(which * half, half)
            sink = room.sinks[name]
            room.send([(down.at[pl.ds(at, half), :], sink.at[:half, :])])
            room.send([(up.at[pl.ds(at, half), :], sink.at[half:, :])])
        term = dot_nt(da[...], room.weight("own_up")[...])
        dz = dot_nt(gy_ref[...], room.weight("two_down")[...])
        da = (dz * room.get("slope_far")[...].astype(f32)).astype(bf16)
        term = term + dot_nt(da, room.weight("two_up")[...])
        back, grads = norm_back(term, room.get("h")[...], room.get("gain")[...])
        dh = gy_ref[...].astype(f32) + back
        room.get("dh")[...] = dh
        room.get("gh")[...] = dh.astype(bf16)
        room.get("grads")[...] = grads
        room.flush("dh", "gh", "grads")

    part = struct((2 * half, width), bf16)
    tall = ((rows, width), bf16)
    return room_call(
        "feed_back", body, scalars,
        [group("own_", own, ["down", "up"], width), group("two_", far_two, ["down", "up"], width)],
        dict(gy=gy, slope=slope, z=z, n2=n2, slope_far=slope_far, h=h, gain=gain),
        dict(give=part, keep=part, dh=struct((rows, width), f32), gh=struct((rows, width), bf16),
             grads=struct((2, width), f32)),
        dict(da=tall, grad_down=((units, width), bf16), grad_up=((width, units), bf16),
             give=((16, 128), bf16), keep=((16, 128), bf16)),
        7, 12 * rows * width * units,
    )


def attend_back(qkv_ref, start_ref, do_all, out):
    rows, local = do_all.shape
    blocks = rows // BAND
    for head in range(local // HEAD_DIM):
        q, k, v = heads_of(qkv_ref, head, local)
        do = do_all[:, head * HEAD_DIM : (head + 1) * HEAD_DIM]
        columns = [
            slice(j * local + head * HEAD_DIM, j * local + (head + 1) * HEAD_DIM) for j in range(3)
        ]
        dk_parts, dv_parts = [None] * blocks, [None] * blocks

        def put(parts, term, low):
            for piece in range(term.shape[0] // BAND):
                place = low // BAND + piece
                add = term[piece * BAND : (piece + 1) * BAND]
                parts[place] = add if parts[place] is None else parts[place] + add

        for block in range(blocks):
            probs, low, high = band_probs(q, k, start_ref, block)
            here = slice(block * BAND, high)
            dp = dot_nt(do[here], v[low:high])
            inner = jnp.sum(probs * dp, axis=-1, keepdims=True)
            ds = (probs * (dp - inner) * HEAD_DIM**-0.5).astype(bf16)
            out[here, columns[0]] = dot(ds, k[low:high]).astype(bf16)
            put(dk_parts, dot_tn(ds, q[here]), low)
            put(dv_parts, dot_tn(probs.astype(bf16), do[here]), low)
        for block in range(blocks):
            here = slice(block * BAND, (block + 1) * BAND)
            out[here, columns[1]] = dk_parts[block].astype(bf16)
            out[here, columns[2]] = dv_parts[block].astype(bf16)


def heads_back_call(scalars, own, qkv, start, gh, o, n1):
    rows, width = gh.shape
    local = width // 2
    first, deep = local // 2, width // 4

    def body(room, scalar):
        gh_ref = room.get("gh")
        do_all = dot_nt(gh_ref[...], room.weight("own_out")[...]).astype(bf16)
        d = room.get("d")
        attend_back(room.get("qkv"), room.get("start"), do_all, d)
        room.flush("d")
        grad_out, grad_qkv = room.get("grad_out"), room.get("grad_qkv")
        grad_out[...] = dot_tn(room.get("o")[...], gh_ref[...]).astype(bf16)
        grad_qkv[...] = dot_tn(room.get("n1")[...], d[...]).astype(bf16)
        for name, which in (("give", 1 - scalar[0]), ("keep", scalar[0])):
            sink = room.sinks[name]
            at = pl.multiple_of(which * first, first)
            room.send([(grad_out.at[pl.ds(at, first), :], sink.at[:first, :])])
            for side in range(2):
                at = pl.multiple_of((which * 2 + side) * deep, deep)
                for j in range(3):
                    room.send([(
                        grad_qkv.at[pl.ds(at, deep), j * local : (j + 1) * local],
                        sink.at[
                            first + j * deep : first + (j + 1) * deep,
                            side * local : (side + 1) * local,
                        ],
                    )])

    part = struct((first + 3 * deep, width), bf16)
    return room_call(
        "heads_back", body, scalars, [group("own_", own, ["out"], width)],
        dict(gh=gh, qkv=qkv, start=start, o=o, n1=n1),
        dict(give=part, keep=part, d=struct((rows, 3 * local), bf16)),
        dict(grad_out=((local, width), bf16), grad_qkv=((width, 3 * local), bf16),
             give=((16, 128), bf16), keep=((16, 128), bf16)),
        15, 17 * rows * width * local,
    )


def input_back_call(scalars, own, far, qkv_far, start, gh, d, dh, u, gain):
    rows, width = gh.shape
    local = width // 2

    def body(room, _):
        do_all = dot_nt(room.get("gh")[...], room.weight("far_out")[...]).astype(bf16)
        d_far = room.get("d_far")
        attend_back(room.get("qkv"), room.get("start"), do_all, d_far)
        term = None
        for ref, w in ((room.get("d"), room.weight("own_qkv")), (d_far, room.weight("far_qkv"))):
            for j in range(3):
                part = dot_nt(ref[:, j * local : (j + 1) * local], w[j])
                term = part if term is None else term + part
        back, grads = norm_back(term, room.get("u")[...].astype(f32), room.get("gain")[...])
        room.get("du")[...] = (room.get("dh")[...] + back).astype(bf16)
        room.get("grads")[...] = grads
        room.flush("du", "grads")

    return room_call(
        "input_back", body, scalars,
        [group("far_", far, ["out", "qkv"], width), group("own_", own, ["qkv"], width)],
        dict(gh=gh, qkv=qkv_far, start=start, d=d, u=u, gain=gain, dh=dh),
        dict(du=struct((rows, width), bf16), grads=struct((2, width), f32)),
        dict(d_far=((rows, 3 * local), bf16)), 2, 21 * rows * width * local,
    )


def ring_walk(size):
    return list(range(0, size, 2)) + list(range(1, size, 2))[::-1]


def ring_routes(count, size):
    walk = ring_walk(size)
    up = []
    for base in range(0, count, size):
        for place in range(size):
            up.append((base + walk[place], base + walk[(place + 1) % size]))
    return up, [(b, a) for a, b in up]


def slot_steps(size):
    return list(range(0, -size // 2, -1)) + list(range(1, size // 2)) + [size // 2]


def halving_order(count):
    bits = count.bit_length() - 1
    first = list(range(bits))
    second = [1, 0] + first[2:] if bits > 1 else first
    return first, second


def pairs_of(count, step):
    routes = []
    for core, order in enumerate(halving_order(count)):
        for i in range(count):
            routes.append((core * count + i, core * count + (i ^ (1 << order[step]))))
    return routes


def own_bits(sec, rank, count):
    first, second = halving_order(count)
    return [
        lax.rem(rank >> jnp.where(sec == 0, a, b), 2) for a, b in zip(first, second)
    ]


class Flow:
    def __init__(self, steps):
        self.steps, self.results, self.value, self.done = steps, None, None, False

    def advance(self, after=None):
        if after is not None and self.results is not None:
            self.results, _ = lax.optimization_barrier((self.results, after))
        try:
            operands, send = self.steps.send(self.results)
        except StopIteration as stop:
            self.value, self.done = stop.value, True
            return ()
        self.results = send(operands)
        return operands


def finished(flow):
    while not flow.done:
        flow.advance()
    return flow.value


def together(flows, *others):
    moving = [flow for flow in flows if not flow.done]
    results, others = lax.optimization_barrier(([flow.results for flow in moving], others))
    for flow, result in zip(moving, results):
        flow.results = result
    return [flow.advance() for flow in moving], others


def kernel_after(kernel, moving, last, *inputs):
    operands = [flow.advance(last) for flow in moving if not flow.done]
    inputs, _ = lax.optimization_barrier((inputs, operands))
    return kernel(*inputs)


def cut_body(count, spots, qkv, out, up, down, attention, feed, sems):
    width = up.shape[0]
    local = qkv.shape[2]
    place, sec = spots[0], spots[1]
    fine = width // count // 2
    half = fine // 2
    for which in range(2):
        core = sec if which == 0 else 1 - sec
        row = (place * 2 + core) * fine
        base = which * 2 * fine

        def put(n, source, target):
            pltpu.make_async_copy(source, target, sems.at[n]).start()

        mid = base + fine
        put(0, qkv.at[0, pl.ds(row, fine), :], attention.at[base:mid, :local])
        put(0, qkv.at[1, pl.ds(row, fine), :], attention.at[base:mid, local:])
        put(0, qkv.at[2, pl.ds(row, half), :], attention.at[mid : mid + half, :local])
        put(0, qkv.at[2, pl.ds(row + half, half), :], attention.at[mid : mid + half, local:])
        put(0, out.at[pl.ds((place * 2 + core) * half, half), :], attention.at[mid + half : mid + fine, :])
        put(1, up.at[pl.ds(row, fine), :], feed.at[base:mid, :])
        put(1, down.at[pl.ds(row, fine), :], feed.at[mid : mid + fine, :])
    pltpu.make_async_copy(attention, attention, sems.at[0]).wait()
    pltpu.make_async_copy(feed, feed, sems.at[1]).wait()


def cut_call(spots, count, mine):
    width = mine[2].shape[0]
    shapes = [struct((2 * width // count, width), bf16)] * 2
    return pl.pallas_call(
        functools.partial(cut_body, count),
        grid=(1,),
        in_specs=[pl.BlockSpec(memory_space=pltpu.SMEM)] + any_specs(4),
        out_specs=[pl.BlockSpec(x.shape, lambda i: (0, 0)) for x in shapes],
        out_shape=shapes,
        scratch_shapes=[pltpu.SemaphoreType.DMA((2,))],
        compiler_params=params(),
        cost_estimate=cost(0, 4 * width * width),
        name="cut",
    )(spots, *mine)


def final_call(name, body, scalars, sums, outputs):
    whole, width = sums[0].shape

    def kernel(scalar_ref, own0, far0, own1, far1, *refs):
        refs = list(refs)
        sinks = refs[: len(outputs)]
        held, sems, out_sems, *wide = refs[len(outputs) :]
        sec = scalar_ref[0]
        for layer, sides in enumerate(((own0, far0), (own1, far1))):

            @pl.when(sec == layer)
            def _():
                for side, ref in enumerate(sides):
                    pltpu.make_async_copy(ref, held.at[side], sems.at[side]).start()

        leaving = []
        for side in range(2):
            pltpu.make_async_copy(held.at[side], held.at[side], sems.at[side]).wait()
            for source, sink in body(held, side, lax.rem(sec + side, 2), wide, sinks):
                copy = pltpu.make_async_copy(source, sink, out_sems.at[len(leaving)])
                copy.start()
                leaving.append(copy)
        for copy in leaving:
            copy.wait()

    return pl.pallas_call(
        kernel,
        in_specs=[pl.BlockSpec(memory_space=pltpu.SMEM)] + any_specs(4),
        out_specs=any_specs(len(outputs)),
        out_shape=outputs,
        scratch_shapes=[
            pltpu.VMEM((2, whole, width), bf16),
            pltpu.SemaphoreType.DMA((2,)),
            pltpu.SemaphoreType.DMA((16,)),
        ]
        + [pltpu.VMEM((2,) + x.shape[:-2] + (x.shape[-2] // 2, x.shape[-1]), f32) for x in outputs],
        compiler_params=params(),
        cost_estimate=cost(0, 12 * whole * width),
        name=name,
    )(scalars, *sums)


def final_mlp_call(scalars, sums, width):
    half = width // 2

    def body(held, side, core, wide, sinks):
        at = pl.multiple_of(core * half, half)
        for n in range(2):
            wide[n][side] = held[side, n * half : (n + 1) * half, :].astype(f32)
            yield wide[n].at[side], sinks[n].at[pl.ds(at, half), :]

    return final_call("final_mlp", body, scalars, sums, [struct((width, width), f32)] * 2)


def final_attention_call(scalars, sums, width):
    local = width // 2
    first, deep = local // 2, width // 4

    def body(held, side, core, wide, sinks):
        wide[0][side] = held[side, :first, :].astype(f32)
        yield wide[0].at[side], sinks[0].at[pl.ds(pl.multiple_of(core * first, first), first), :]
        low = pl.multiple_of(core * 2 * deep, 2 * deep)
        for j in range(3):
            block = held[side, first + j * deep : first + (j + 1) * deep, :].astype(f32)
            wide[1][side, j, :deep, :] = block[:, :local]
            wide[1][side, j, deep:, :] = block[:, local:]
            yield wide[1].at[side, j], sinks[1].at[j, pl.ds(low, 2 * deep), :]

    return final_call(
        "final_attention", body, scalars, sums,
        [struct((local, width), f32), struct((3, width, local), f32)],
    )


def series_starts(lengths, rows):
    ends = jnp.cumsum(lengths)
    places = jnp.arange(rows, dtype=jnp.int32)
    passed = jnp.where(ends[None, :] <= places[:, None], ends[None, :], 0)
    return jnp.max(passed, axis=1, keepdims=True).astype(jnp.int32)


def per_device(tokens, lengths, w_qkv, w_out, w_up, w_down, norm_gain, norm_bias, cotangent):
    sec = lax.axis_index("section").astype(jnp.int32)
    tensor = lax.axis_index("tensor")
    rank = lax.axis_index("dp")
    count = lax.axis_size("dp")
    own_rows = tokens.shape[1]
    rows = 2 * own_rows
    width = tokens.shape[2]
    local = width // 2
    swap = [(0, 1), (1, 0)]
    bits = own_bits(sec, rank, count)
    fan = min(3, len(bits))
    size = 1 << fan
    ring_up, ring_down = ring_routes(count, size)
    in_ring = lax.rem(rank, size)
    place = jnp.where(lax.rem(in_ring, 2) == 0, in_ring // 2, size - 1 - in_ring // 2)
    slot_places = lax.rem(place + np.asarray(slot_steps(size), np.int32) + size, size).astype(jnp.int32)

    def across(shard):
        other = lax.ppermute(shard, "tensor", swap)
        return jnp.where(
            tensor == 0,
            jnp.concatenate([shard, other], axis=0),
            jnp.concatenate([other, shard], axis=0),
        )

    def to_other_core(value):
        return lax.ppermute(value, "section", swap)

    def swap_cores(value):
        return lax.ppermute(value, "section", swap)

    def swap_tensor(value):
        return lax.ppermute(value, "tensor", swap)

    def move(axis, route):
        return lambda value: lax.ppermute(value, axis, route)

    def doubled(held, away, step):
        low = bits[step] == 0
        return jnp.concatenate([jnp.where(low, held, away), jnp.where(low, away, held)], axis=0)

    def sum_steps(layer, send, kept):
        received = yield send, swap_cores
        rows = kept.shape[0] // 2

        def both(side):
            a = lax.dynamic_slice_in_dim(kept, side * rows, rows, 0).astype(f32)
            b = lax.dynamic_slice_in_dim(received, side * rows, rows, 0).astype(f32)
            return a + b

        away = yield both(1 - bits[0]).astype(bf16), move(("section", "dp"), pairs_of(count, 0))
        held = (both(bits[0]) + away.astype(f32)).astype(bf16)
        for step in range(1, len(bits)):
            rows //= 2
            part = lax.dynamic_slice_in_dim(held, (1 - bits[step]) * rows, rows, 0)
            rest = lax.dynamic_slice_in_dim(held, bits[step] * rows, rows, 0)
            away = yield part, move(("section", "dp"), pairs_of(count, step))
            held = (rest.astype(f32) + away.astype(f32)).astype(bf16)
        for step in reversed(range(len(bits))):
            away = yield held, move(("section", "dp"), pairs_of(count, step))
            held = doubled(held, away, step)
        far = yield held, move("section", [(1 - layer, layer)])
        return held, far

    def around(pair):
        return lax.ppermute(pair[0], "dp", ring_up), lax.ppermute(pair[1], "dp", ring_down)

    def spread_steps(piece, route):
        send = move("section", route)

        def both_ways(pair):
            return around(pair) + (send(pair[0]), send(pair[1]))

        def first_way(pair):
            return around(pair) + (send(pair[0]),)

        a, b, far = yield (piece, piece), first_way
        ups, downs, far_ups, far_downs = [piece, a], [b], [far], []
        for _ in range(size // 2 - 2):
            a, b, c, d = yield (ups[-1], downs[-1]), both_ways
            ups.append(a)
            downs.append(b)
            far_ups.append(c)
            far_downs.append(d)
        half = piece.shape[0] // 2
        whole = ups[-1], downs[-1]

        def last_way(pair):
            return around((pair[0][:half], pair[1][half:])) + (send(pair[0]), send(pair[1]))

        a, b, c, d = yield whole, last_way
        far_ups.append(c)
        far_downs.append(d)
        c, d = yield (a, b), lambda pair: (send(pair[0]), send(pair[1]))
        return ups + downs + [a, b], far_ups + far_downs + [c, d]

    def butterfly_steps(part):
        away = yield part, swap_cores
        part = part + away
        distance = 1
        while distance < count:
            away = yield part, move("dp", [(i, i ^ distance) for i in range(count)])
            part = part + away
            distance *= 2
        return part

    mine = (jnp.transpose(w_qkv[0], (1, 0, 2)), w_out[0], w_up[0], w_down[0])
    u0 = across(lax.dynamic_index_in_dim(tokens, sec, 0, False))
    start = series_starts(lax.dynamic_index_in_dim(lengths[0], sec, 0, False), rows)
    norms = jnp.concatenate([norm_gain[0], norm_bias[0]], axis=0)
    swap_norms = to_other_core(norms)
    norm_of = [
        jnp.where(sec == 0, norms, swap_norms),
        jnp.where(sec == 0, swap_norms, norms),
    ]

    spots = jnp.stack([place, sec]).astype(jnp.int32)
    cuts = cut_call(spots, size, mine)

    swapped = tuple(to_other_core(w) for w in mine)
    names = ("qkv", "out", "up", "down")
    mine_of, swapped_of = dict(zip(names, mine)), dict(zip(names, swapped))
    def to_outputs(pair):
        rows_of = [
            lax.dynamic_slice_in_dim(value, tensor * own_rows, own_rows, 0) for value in pair
        ]
        stay = jnp.where(sec == 0, rows_of[0], rows_of[1])
        go = jnp.where(sec == 0, rows_of[1], rows_of[0])
        came = to_other_core(go)
        return jnp.where(sec == 0, jnp.stack([stay, came]), jnp.stack([came, stay]))[None]

    own_weights = [Own(layer, sec, mine_of, swapped_of) for layer in range(2)]
    here = sec.reshape(1)
    gains = [[norm_of[layer][i : i + 1] for i in range(4)] for layer in range(2)]

    both_cores = [(0, 1), (1, 0)]
    sections = ("section", "tensor")
    attention_cut = swap_tensor(cuts[0])
    feed_cut = lax.ppermute(cuts[1], sections, [(0, 1), (1, 0)])
    span = width // size
    came = swap_cores(jnp.concatenate([attention_cut[span:], feed_cut[span:]], axis=0))
    first_piece = jnp.where(
        sec == 0, jnp.concatenate([attention_cut[:span], feed_cut[:span]], axis=0), came
    )
    second_piece = jnp.where(sec == 1, attention_cut[:span], came[:span])

    def slots_of(arrays, rows, last):
        half = span // 2
        return [((x, rows), (x, rows + half)) for x in arrays[: size - 1]] + [last(arrays[size - 1 :])]

    def pieces_of(gathered, rows, last):
        return Pieces(sec, slot_places, *(slots_of(arrays, rows, last) for arrays in gathered))

    half = span // 2
    first_gather = Flow(spread_steps(first_piece, both_cores))
    second_gather = Flow(spread_steps(second_piece, both_cores))
    operand = first_gather.advance()
    (u0, start), _ = lax.optimization_barrier(((u0, start), operand))
    a0 = first_call(here, own_weights[0], u0, start, gains[0][0], gains[0][2])
    whole_up = lax.ppermute(mine[2], sections, [(2, 3), (3, 2)])
    whole_down = lax.ppermute(mine[3], sections, [(2, 3), (3, 2)])
    together([first_gather], a0["h"])
    together([first_gather])
    together([first_gather])
    operands, (n1_zero, whole_up) = together([first_gather, second_gather], a0["n1"], whole_up)
    a0 = dict(a0, n1=n1_zero)
    gathered = finished(first_gather)
    far_zero = pieces_of(gathered, 0, lambda x: ((x[0], 0), (x[0], half)))
    far_two_zero = pieces_of(gathered, span, lambda x: ((x[1], 0), (x[1], half)))
    b0 = kernel_after(
        lambda *x: second_call(here, far_zero, *x), [], None,
        a0["n1"], start, a0["h"], gains[0][1], gains[0][3],
    )
    late, _ = lax.optimization_barrier((lax.dynamic_index_in_dim(cotangent, sec, 0, False), b0["h"]))
    gy1 = across(late)
    operands, (n2_zero,) = together([second_gather], b0["n2"])
    b0 = dict(b0, n2=n2_zero)
    c0 = kernel_after(
        lambda *x: feed_call(here, own_weights[0], far_two_zero, *x), [], None, b0["n2"], b0["h"]
    )
    operands, (u1, whole_down) = together([second_gather], c0["y"], whole_down)
    a1 = kernel_after(
        lambda *x: first_call(here, own_weights[1], *x), [], None, u1, start, gains[1][0], gains[1][2]
    )
    together([second_gather], a1["h"])
    far_one = pieces_of(finished(second_gather), 0, lambda x: ((x[0], 0), (x[1], 0)))
    b1 = kernel_after(
        lambda *x: second_call(here, far_one, *x), [], None,
        a1["n1"], start, a1["h"], gains[1][1], gains[1][3],
    )
    to_first = move("section", [(1, 0)])
    far_two_one = Own(
        1, sec, dict(up=whole_up, down=whole_down), dict(up=to_first(whole_up), down=to_first(whole_down))
    )
    c1 = kernel_after(
        lambda *x: feed_call(here, own_weights[1], far_two_one, *x), [], None, b1["n2"], b1["h"]
    )
    outputs = to_outputs([c0["y"], c1["y"]])

    def feed_back(layer, far_two, moving, last, gy, b, c):
        return kernel_after(
            lambda *x: feed_back_call(here, own_weights[layer], far_two, *x), moving, last,
            gy, c["slope"], c["slope_far"], b["h"], c["z"], b["n2"], gains[layer][1],
        )

    def heads_back(layer, moving, last, a, e):
        return kernel_after(
            lambda *x: heads_back_call(here, own_weights[layer], *x), moving, last,
            a["qkv"], start, e["gh"], a["o"], a["n1"],
        )

    def input_back(layer, far, moving, last, a, b, e, f, u):
        return kernel_after(
            lambda *x: input_back_call(here, own_weights[layer], far, *x), moving, last,
            b["qkv"], start, e["gh"], f["d"], e["dh"], u, gains[layer][0],
        )

    e1 = feed_back(1, far_two_one, [], None, gy1, b1, c1)
    outputs, gh = lax.optimization_barrier((outputs, e1["gh"]))
    e1 = dict(e1, gh=gh)
    sums = [Flow(sum_steps(1, e1["give"], e1["keep"]))]
    f1 = heads_back(1, sums, gh, a1, e1)
    sums.append(Flow(sum_steps(1, f1["give"], f1["keep"])))
    g1 = input_back(1, far_one, sums, f1["d"], a1, b1, e1, f1, c0["y"])
    e0 = feed_back(0, far_two_zero, sums, g1["du"], g1["du"], b0, c0)
    sums.append(Flow(sum_steps(0, e0["give"], e0["keep"])))
    f0 = heads_back(0, sums, e0["gh"], a0, e0)
    sums.append(Flow(sum_steps(0, f0["give"], f0["keep"])))
    sums[3].advance()
    g0 = input_back(0, far_zero, sums, f0["d"], a0, b0, e0, f0, u0)
    norm_grads = [
        jnp.concatenate([g["grads"][:1], e["grads"][:1], g["grads"][1:], e["grads"][1:]])
        for g, e in ((g0, e0), (g1, e1))
    ]
    norm_flow = Flow(butterfly_steps(jnp.concatenate(norm_grads, axis=0)))
    norm_flow.advance()
    grads_in = to_outputs([g0["du"], g1["du"]])
    for flow in sums:
        flow.advance(g0["du"])
    (grads_in, results), _ = lax.optimization_barrier(((grads_in, sums[3].results), g0["du"]))
    sums[3].results = results
    while any(not flow.done for flow in sums + [norm_flow]):
        for flow in sums + [norm_flow]:
            if not flow.done:
                flow.advance()
    parts = [flow.value for flow in sums]
    grad_down, grad_up = final_mlp_call(here, [*parts[2], *parts[0]], width)
    grad_out, grad_qkv = final_attention_call(here, [*parts[3], *parts[1]], width)
    norm_total = norm_flow.value
    norm_sum = jnp.where(sec == 0, norm_total[:4], norm_total[4:])
    norm_sum = lax.dynamic_slice_in_dim(norm_sum, tensor * local, local, 1)

    return (
        outputs,
        grads_in,
        jnp.transpose(grad_qkv, (1, 0, 2))[None],
        grad_out[None],
        grad_up[None],
        grad_down[None],
        norm_sum[None, :2],
        norm_sum[None, 2:],
    )


def solution(mesh):
    in_specs = (
        P(None, ("dp", "tensor"), None),
        P("dp", None, None),
        P("section", None, None, "tensor"),
        P("section", "tensor", None),
        P("section", None, "tensor"),
        P("section", "tensor", None),
        P("section", None, None),
        P("section", None, None),
        P(None, ("dp", "tensor"), None),
    )
    out_specs = (
        P("section", None, ("dp", "tensor"), None),
        P("section", None, ("dp", "tensor"), None),
        P("section", None, None, "tensor"),
        P("section", "tensor", None),
        P("section", None, "tensor"),
        P("section", "tensor", None),
        P("section", None, "tensor"),
        P("section", None, "tensor"),
    )
    return jax.shard_map(
        per_device, mesh=mesh, in_specs=in_specs, out_specs=out_specs, check_vma=False
    )
```

```python
import functools

import jax
import jax.numpy as jnp
import numpy as np
from jax import lax
from jax.experimental import pallas as pl
from jax.experimental.pallas import tpu as pltpu
from jax.sharding import PartitionSpec as P

HEAD_DIM = 128
BAND = 128
EPSILON = 1e-05
MASKED = -1e30
VMEM = 60 * 1024 * 1024
bf16 = jnp.bfloat16
f32 = jnp.float32


def params():
    return pltpu.CompilerParams(vmem_limit_bytes=VMEM)


def cost(flops, moved):
    return pl.CostEstimate(
        flops=int(flops), bytes_accessed=int(moved), transcendentals=0
    )


def dot(a, b):
    return jnp.dot(a, b, preferred_element_type=f32)


def dot_nt(a, b):
    return lax.dot_general(a, b, (((1,), (1,)), ((), ())), preferred_element_type=f32)


def dot_tn(a, b):
    return lax.dot_general(a, b, (((0,), (0,)), ((), ())), preferred_element_type=f32)


def unit_of(values):
    centre = values - jnp.mean(values, axis=-1, keepdims=True)
    spread = jnp.mean(centre * centre, axis=-1, keepdims=True)
    scale = lax.rsqrt(spread + EPSILON)
    return centre * scale, scale


def norm_back(incoming, values, gain):
    unit, scale = unit_of(values)
    scaled = incoming * gain
    inner = (
        scaled
        - jnp.mean(scaled, axis=-1, keepdims=True)
        - unit * jnp.mean(scaled * unit, axis=-1, keepdims=True)
    )
    grads = jnp.concatenate(
        [
            jnp.sum(incoming * unit, axis=0, keepdims=True),
            jnp.sum(incoming, axis=0, keepdims=True),
        ],
        axis=0,
    )
    return scale * inner, grads


def any_specs(n):
    return [pl.BlockSpec(memory_space=pl.ANY)] * n


class Own:
    def __init__(self, layer, sec, mine, swapped):
        self.scalars = jnp.stack([sec, jnp.full_like(sec, layer)])
        self.mine, self.swapped = mine, swapped

    def operands(self, names):
        return [self.mine[n] for n in names] + [self.swapped[n] for n in names]

    def start(self, names, scalars, refs, targets, sems):
        mine, swapped = refs[: len(names)], refs[len(names) :]
        for condition, side in ((True, mine), (False, swapped)):

            @pl.when((scalars[0] == scalars[1]) == condition)
            def _():
                for n, (ref, target) in enumerate(zip(side, targets)):
                    pltpu.make_async_copy(ref, target, sems.at[n, 0]).start()

    def wait(self, n, name, target, sems):
        pltpu.make_async_copy(target, target, sems.at[n, 0]).wait()


class Pieces:
    def __init__(self, sec, places, own, far):
        self.count = len(own)
        self.scalars = jnp.concatenate([sec.reshape(1), places])
        self.arrays, self.index = [], []
        for side in (own, far):
            rows = []
            for slot in side:
                parts = []
                for array, row in slot:
                    known = [n for n, x in enumerate(self.arrays) if x is array]
                    if not known:
                        self.arrays.append(array)
                        known = [len(self.arrays) - 1]
                    parts.append((known[0], row))
                rows.append(parts)
            self.index.append(rows)

    def operands(self, names):
        return self.arrays

    def start(self, names, scalars, refs, targets, sems):
        every = slice(None)
        for side, slots in enumerate(self.index):
            core = lax.rem(scalars[0] + side, 2)
            for slot, ((n0, row0), (n1, row1)) in enumerate(slots):
                spot = scalars[1 + slot] * 2 + core
                first, second = refs[n0], refs[n1]
                for n, (name, target) in enumerate(zip(names, targets)):

                    def put(source, place):
                        pltpu.make_async_copy(source, place, sems.at[n, side]).start()

                    if name == "qkv":
                        deep, local = target.shape[1], target.shape[2]
                        fine = deep // self.count // 2
                        half = fine // 2
                        row = spot * fine
                        for j in range(2):
                            columns = slice(j * local, (j + 1) * local)
                            put(
                                first.at[row0 : row0 + fine, columns],
                                target.at[j, pl.ds(row, fine), :],
                            )
                            put(
                                second.at[row1 : row1 + half, columns],
                                target.at[2, pl.ds(row + j * half, half), :],
                            )
                    elif name == "out":
                        fine = target.shape[0] // self.count // 2
                        put(
                            second.at[row1 + fine : row1 + 2 * fine, every],
                            target.at[pl.ds(spot * fine, fine), :],
                        )
                    else:
                        fine = target.shape[0] // self.count // 2
                        source = second.at[row1 : row1 + fine, every] if name == "down" else first.at[row0 : row0 + fine, every]
                        put(source, target.at[pl.ds(spot * fine, fine), :])

    def wait(self, n, name, target, sems):
        for side in range(2):
            if name == "qkv":
                part = target.at[:, : target.shape[1] // 2, :]
            else:
                part = target.at[: target.shape[0] // 2, :]
            pltpu.make_async_copy(part, part, sems.at[n, side]).wait()


def struct(shape, dtype):
    return jax.ShapeDtypeStruct(shape, dtype)


class Room:
    def __init__(self, refs, sources, sinks, in_sems, out_sems, weights):
        self.refs, self.sources, self.sinks = refs, sources, sinks
        self.in_sems, self.out_sems, self.weights = in_sems, out_sems, weights
        self.waited, self.leaving = set(), []

    def start(self, names):
        for n, name in enumerate(names):
            pltpu.make_async_copy(self.sources[name], self.refs[name], self.in_sems.at[n]).start()
        self.order = list(names)

    def get(self, name):
        if name in self.sources and name not in self.waited:
            self.waited.add(name)
            ref = self.refs[name]
            pltpu.make_async_copy(ref, ref, self.in_sems.at[self.order.index(name)]).wait()
        return self.refs[name]

    def weight(self, name):
        loader, place, kind, target, sems = self.weights[name]
        if name not in self.waited:
            self.waited.add(name)
            loader.wait(place, kind, target, sems)
        return target

    def send(self, pairs):
        for source, sink in pairs:
            copy = pltpu.make_async_copy(source, sink, self.out_sems.at[len(self.leaving)])
            copy.start()
            self.leaving.append(copy)

    def flush(self, *names):
        self.send([(self.refs[name], self.sinks[name]) for name in names])

    def close(self):
        for copy in self.leaving:
            copy.wait()


def room_call(name, body, scalars, weights, inputs, outputs, scratch, copies, flops):
    in_names, out_names, temp_names = list(inputs), list(outputs), list(scratch)
    operands = [loader.operands([k for k, _ in kinds]) for _, loader, kinds in weights]
    scalar_list = [scalars] + [loader.scalars for _, loader, _ in weights]
    local_out = [n for n in out_names if n not in scratch]

    def whole(*refs):
        refs = list(refs)

        def take(n):
            got = refs[:n]
            del refs[:n]
            return got

        scalar_refs = take(len(scalar_list))
        sources = dict(zip(in_names, take(len(in_names))))
        weight_sources = [take(len(o)) for o in operands]
        sinks = dict(zip(out_names, take(len(out_names))))
        held = dict(zip(in_names, take(len(in_names))))
        held.update(zip(local_out, take(len(local_out))))
        held.update(zip(temp_names, take(len(temp_names))))
        in_sems, out_sems = take(2)
        table = {}
        starts = []
        for (prefix, loader, kinds), source, scalar in zip(weights, weight_sources, scalar_refs[1:]):
            targets = take(len(kinds))
            sems = take(1)[0]
            starts.append((loader, [k for k, _ in kinds], scalar, source, targets, sems))
            for place, (kind, _) in enumerate(kinds):
                table[prefix + kind] = (loader, place, kind, targets[place], sems)
        room = Room(held, sources, sinks, in_sems, out_sems, table)
        room.start(in_names)
        for loader, kinds, scalar, source, targets, sems in starts:
            loader.start(kinds, scalar, source, targets, sems)
        body(room, scalar_refs[0])
        for name in in_names:
            room.get(name)
        for key in table:
            room.weight(key)
        room.close()

    vmem = [pltpu.VMEM(inputs[n].shape, inputs[n].dtype) for n in in_names]
    vmem += [pltpu.VMEM(outputs[n].shape, outputs[n].dtype) for n in local_out]
    vmem += [pltpu.VMEM(*scratch[n]) for n in temp_names]
    vmem += [pltpu.SemaphoreType.DMA((max(len(in_names), 1),)), pltpu.SemaphoreType.DMA((copies,))]
    for _, _, kinds in weights:
        vmem += [pltpu.VMEM(shape, bf16) for _, shape in kinds]
        vmem.append(pltpu.SemaphoreType.DMA((len(kinds), 2)))
    flat = [x for o in operands for x in o]
    moved = sum(x.size * x.dtype.itemsize for x in list(inputs.values()) + list(outputs.values()))
    moved += sum(2 * int(np.prod(shape)) for _, _, kinds in weights for _, shape in kinds)
    result = pl.pallas_call(
        whole,
        in_specs=[pl.BlockSpec(memory_space=pltpu.SMEM)] * len(scalar_list)
        + any_specs(len(in_names) + len(flat)),
        out_specs=any_specs(len(out_names)),
        out_shape=[outputs[n] for n in out_names],
        scratch_shapes=vmem,
        compiler_params=params(),
        cost_estimate=cost(flops, moved),
        name=name,
    )(*scalar_list, *inputs.values(), *flat)
    return dict(zip(out_names, result))


def band_probs(q, k, start_ref, block):
    low = max(block - 1, 0) * BAND
    high = (block + 1) * BAND
    scores = dot_nt(q[block * BAND : high], k[low:high]) * HEAD_DIM**-0.5
    row = lax.broadcasted_iota(jnp.int32, scores.shape, 0) + block * BAND
    column = lax.broadcasted_iota(jnp.int32, scores.shape, 1) + low
    first = start_ref[block * BAND : high, :]
    allowed = (column <= row) & (column >= first)
    scores = jnp.where(allowed, scores, MASKED)
    expo = jnp.exp(scores - jnp.max(scores, axis=-1, keepdims=True))
    return expo / jnp.sum(expo, axis=-1, keepdims=True), low, high


def heads_of(qkv_ref, head, local):
    return [
        qkv_ref[:, j * local + head * HEAD_DIM : j * local + (head + 1) * HEAD_DIM] for j in range(3)
    ]


def attend(qkv_ref, start_ref, o_ref):
    rows, local = o_ref.shape
    for head in range(local // HEAD_DIM):
        cut = slice(head * HEAD_DIM, (head + 1) * HEAD_DIM)
        q, k, v = heads_of(qkv_ref, head, local)
        for block in range(rows // BAND):
            probs, low, high = band_probs(q, k, start_ref, block)
            o_ref[block * BAND : high, cut] = dot(probs.astype(bf16), v[low:high]).astype(bf16)


def project(left, w, out_ref):
    local = w.shape[2]
    for j in range(3):
        out_ref[:, j * local : (j + 1) * local] = dot(left[...], w[j]).astype(bf16)


def activate(n2_ref, up, z_ref, slope_ref):
    c = np.float32(np.sqrt(2 / np.pi))
    tile = 512
    for i in range(z_ref.shape[1] // tile):
        cut = slice(i * tile, (i + 1) * tile)
        a = dot(n2_ref[...], up[:, cut])
        square = a * a
        t = jnp.tanh(c * a * (1.0 + 0.044715 * square))
        half = 0.5 * (1.0 + t)
        slope = half + 0.5 * c * a * (1.0 - t * t) * (1.0 + 3 * 0.044715 * square)
        z_ref[:, cut] = (a * half).astype(bf16)
        slope_ref[:, cut] = slope.astype(bf16)


def sizes(width):
    local, units = width // 2, width
    return {
        "qkv": (3, width, local),
        "out": (local, width),
        "up": (width, units),
        "down": (units, width),
    }


def group(prefix, loader, kinds, width):
    return prefix, loader, [(k, sizes(width)[k]) for k in kinds]


def first_call(scalars, own, u, start, gain, bias):
    rows, width = u.shape
    local = width // 2

    def body(room, _):
        u_ref = room.get("u")
        unit, _ = unit_of(u_ref[...].astype(f32))
        n1 = room.get("n1")
        n1[...] = (unit * room.get("gain")[...] + room.get("bias")[...]).astype(bf16)
        project(n1, room.weight("own_qkv"), room.get("qkv"))
        room.flush("n1", "qkv")
        attend(room.get("qkv"), room.get("start"), room.get("o"))
        room.flush("o")
        room.get("h")[...] = u_ref[...].astype(f32) + dot(room.get("o")[...], room.weight("own_out")[...])
        room.flush("h")

    return room_call(
        "first", body, scalars, [group("own_", own, ["qkv", "out"], width)],
        dict(u=u, start=start, gain=gain, bias=bias),
        dict(n1=struct((rows, width), bf16), qkv=struct((rows, 3 * local), bf16),
             o=struct((rows, local), bf16), h=struct((rows, width), f32)),
        {}, 4, 9 * rows * width * local,
    )


def second_call(scalars, far, n1, start, base, gain, bias):
    rows, width = base.shape
    local = width // 2

    def body(room, _):
        project(room.get("n1"), room.weight("far_qkv"), room.get("qkv"))
        room.flush("qkv")
        attend(room.get("qkv"), room.get("start"), room.get("o"))
        h = room.get("base")[...] + dot(room.get("o")[...], room.weight("far_out")[...])
        room.get("h")[...] = h
        unit, _ = unit_of(h)
        n2 = room.get("n2")
        n2[...] = (unit * room.get("gain")[...] + room.get("bias")[...]).astype(bf16)
        room.flush("h", "n2")

    return room_call(
        "second", body, scalars, [group("far_", far, ["qkv", "out"], width)],
        dict(n1=n1, start=start, base=base, gain=gain, bias=bias),
        dict(qkv=struct((rows, 3 * local), bf16), h=struct((rows, width), f32),
             n2=struct((rows, width), bf16)),
        dict(o=((rows, local), bf16)), 3, 9 * rows * width * local,
    )


def feed_call(scalars, own, far_two, n2, h):
    rows, width = h.shape
    units = width

    def body(room, _):
        n2 = room.get("n2")
        activate(n2, room.weight("own_up"), room.get("z"), room.get("slope"))
        room.flush("z", "slope")
        activate(n2, room.weight("two_up"), room.get("z_far"), room.get("slope_far"))
        room.flush("slope_far")
        y = room.get("h")[...] + dot(room.get("z")[...], room.weight("own_down")[...])
        room.get("y")[...] = (y + dot(room.get("z_far")[...], room.weight("two_down")[...])).astype(bf16)
        room.flush("y")

    tall = struct((rows, width), bf16)
    return room_call(
        "feed", body, scalars,
        [group("own_", own, ["up", "down"], width), group("two_", far_two, ["up", "down"], width)],
        dict(n2=n2, h=h), dict(z=tall, slope=tall, slope_far=tall, y=tall),
        dict(z_far=((rows, units), bf16)), 4, 8 * rows * width * units,
    )


def feed_back_call(scalars, own, far_two, gy, slope, slope_far, h, z, n2, gain):
    rows, width = gy.shape
    units = width
    half = units // 2

    def body(room, scalar):
        gy_ref = room.get("gy")
        dz = dot_nt(gy_ref[...], room.weight("own_down")[...])
        da = room.get("da")
        da[...] = (dz * room.get("slope")[...].astype(f32)).astype(bf16)
        down, up = room.get("grad_down"), room.get("grad_up")
        down[...] = dot_tn(room.get("z")[...], gy_ref[...]).astype(bf16)
        up[...] = dot_tn(room.get("n2")[...], da[...]).astype(bf16)
        for name, which in (("give", 1 - scalar[0]), ("keep", scalar[0])):
            at = pl.multiple_of(which * half, half)
            sink = room.sinks[name]
            room.send([(down.at[pl.ds(at, half), :], sink.at[:half, :])])
            room.send([(up.at[pl.ds(at, half), :], sink.at[half:, :])])
        term = dot_nt(da[...], room.weight("own_up")[...])
        dz = dot_nt(gy_ref[...], room.weight("two_down")[...])
        da = (dz * room.get("slope_far")[...].astype(f32)).astype(bf16)
        term = term + dot_nt(da, room.weight("two_up")[...])
        back, grads = norm_back(term, room.get("h")[...], room.get("gain")[...])
        dh = gy_ref[...].astype(f32) + back
        room.get("dh")[...] = dh
        room.get("gh")[...] = dh.astype(bf16)
        room.get("grads")[...] = grads
        room.flush("dh", "gh", "grads")

    part = struct((2 * half, width), bf16)
    tall = ((rows, width), bf16)
    return room_call(
        "feed_back", body, scalars,
        [group("own_", own, ["down", "up"], width), group("two_", far_two, ["down", "up"], width)],
        dict(gy=gy, slope=slope, z=z, n2=n2, slope_far=slope_far, h=h, gain=gain),
        dict(give=part, keep=part, dh=struct((rows, width), f32), gh=struct((rows, width), bf16),
             grads=struct((2, width), f32)),
        dict(da=tall, grad_down=((units, width), bf16), grad_up=((width, units), bf16),
             give=((16, 128), bf16), keep=((16, 128), bf16)),
        7, 12 * rows * width * units,
    )


def attend_back(qkv_ref, start_ref, do_all, out):
    rows, local = do_all.shape
    blocks = rows // BAND
    for head in range(local // HEAD_DIM):
        q, k, v = heads_of(qkv_ref, head, local)
        do = do_all[:, head * HEAD_DIM : (head + 1) * HEAD_DIM]
        columns = [
            slice(j * local + head * HEAD_DIM, j * local + (head + 1) * HEAD_DIM) for j in range(3)
        ]
        dk_parts, dv_parts = [None] * blocks, [None] * blocks

        def put(parts, term, low):
            for piece in range(term.shape[0] // BAND):
                place = low // BAND + piece
                add = term[piece * BAND : (piece + 1) * BAND]
                parts[place] = add if parts[place] is None else parts[place] + add

        for block in range(blocks):
            probs, low, high = band_probs(q, k, start_ref, block)
            here = slice(block * BAND, high)
            dp = dot_nt(do[here], v[low:high])
            inner = jnp.sum(probs * dp, axis=-1, keepdims=True)
            ds = (probs * (dp - inner) * HEAD_DIM**-0.5).astype(bf16)
            out[here, columns[0]] = dot(ds, k[low:high]).astype(bf16)
            put(dk_parts, dot_tn(ds, q[here]), low)
            put(dv_parts, dot_tn(probs.astype(bf16), do[here]), low)
        for block in range(blocks):
            here = slice(block * BAND, (block + 1) * BAND)
            out[here, columns[1]] = dk_parts[block].astype(bf16)
            out[here, columns[2]] = dv_parts[block].astype(bf16)


def heads_back_call(scalars, own, qkv, start, gh, o, n1):
    rows, width = gh.shape
    local = width // 2
    first, deep = local // 2, width // 4

    def body(room, scalar):
        gh_ref = room.get("gh")
        do_all = dot_nt(gh_ref[...], room.weight("own_out")[...]).astype(bf16)
        d = room.get("d")
        attend_back(room.get("qkv"), room.get("start"), do_all, d)
        room.flush("d")
        grad_out, grad_qkv = room.get("grad_out"), room.get("grad_qkv")
        grad_out[...] = dot_tn(room.get("o")[...], gh_ref[...]).astype(bf16)
        grad_qkv[...] = dot_tn(room.get("n1")[...], d[...]).astype(bf16)
        for name, which in (("give", 1 - scalar[0]), ("keep", scalar[0])):
            sink = room.sinks[name]
            at = pl.multiple_of(which * first, first)
            room.send([(grad_out.at[pl.ds(at, first), :], sink.at[:first, :])])
            for side in range(2):
                at = pl.multiple_of((which * 2 + side) * deep, deep)
                for j in range(3):
                    room.send([(
                        grad_qkv.at[pl.ds(at, deep), j * local : (j + 1) * local],
                        sink.at[
                            first + j * deep : first + (j + 1) * deep,
                            side * local : (side + 1) * local,
                        ],
                    )])

    part = struct((first + 3 * deep, width), bf16)
    return room_call(
        "heads_back", body, scalars, [group("own_", own, ["out"], width)],
        dict(gh=gh, qkv=qkv, start=start, o=o, n1=n1),
        dict(give=part, keep=part, d=struct((rows, 3 * local), bf16)),
        dict(grad_out=((local, width), bf16), grad_qkv=((width, 3 * local), bf16),
             give=((16, 128), bf16), keep=((16, 128), bf16)),
        15, 17 * rows * width * local,
    )


def input_back_call(scalars, own, far, qkv_far, start, gh, d, dh, u, gain):
    rows, width = gh.shape
    local = width // 2

    def body(room, _):
        do_all = dot_nt(room.get("gh")[...], room.weight("far_out")[...]).astype(bf16)
        d_far = room.get("d_far")
        attend_back(room.get("qkv"), room.get("start"), do_all, d_far)
        term = None
        for ref, w in ((room.get("d"), room.weight("own_qkv")), (d_far, room.weight("far_qkv"))):
            for j in range(3):
                part = dot_nt(ref[:, j * local : (j + 1) * local], w[j])
                term = part if term is None else term + part
        back, grads = norm_back(term, room.get("u")[...].astype(f32), room.get("gain")[...])
        room.get("du")[...] = (room.get("dh")[...] + back).astype(bf16)
        room.get("grads")[...] = grads
        room.flush("du", "grads")

    return room_call(
        "input_back", body, scalars,
        [group("far_", far, ["out", "qkv"], width), group("own_", own, ["qkv"], width)],
        dict(gh=gh, qkv=qkv_far, start=start, d=d, u=u, gain=gain, dh=dh),
        dict(du=struct((rows, width), bf16), grads=struct((2, width), f32)),
        dict(d_far=((rows, 3 * local), bf16)), 2, 21 * rows * width * local,
    )


def ring_walk(size):
    return list(range(0, size, 2)) + list(range(1, size, 2))[::-1]


def ring_routes(count, size):
    walk = ring_walk(size)
    up = []
    for base in range(0, count, size):
        for place in range(size):
            up.append((base + walk[place], base + walk[(place + 1) % size]))
    return up, [(b, a) for a, b in up]


def slot_steps(size):
    return list(range(0, -size // 2, -1)) + list(range(1, size // 2)) + [size // 2]


def halving_order(count):
    bits = count.bit_length() - 1
    first = list(range(bits))
    second = [1, 0] + first[2:] if bits > 1 else first
    return first, second


def pairs_of(count, step):
    routes = []
    for core, order in enumerate(halving_order(count)):
        for i in range(count):
            routes.append((core * count + i, core * count + (i ^ (1 << order[step]))))
    return routes


def own_bits(sec, rank, count):
    first, second = halving_order(count)
    return [
        lax.rem(rank >> jnp.where(sec == 0, a, b), 2) for a, b in zip(first, second)
    ]


class Flow:
    def __init__(self, steps):
        self.steps, self.results, self.value, self.done = steps, None, None, False

    def advance(self, after=None):
        if after is not None and self.results is not None:
            self.results, _ = lax.optimization_barrier((self.results, after))
        try:
            operands, send = self.steps.send(self.results)
        except StopIteration as stop:
            self.value, self.done = stop.value, True
            return ()
        self.results = send(operands)
        return operands


def finished(flow):
    while not flow.done:
        flow.advance()
    return flow.value


def together(flows, *others):
    moving = [flow for flow in flows if not flow.done]
    results, others = lax.optimization_barrier(([flow.results for flow in moving], others))
    for flow, result in zip(moving, results):
        flow.results = result
    return [flow.advance() for flow in moving], others


def kernel_after(kernel, moving, last, *inputs):
    operands = [flow.advance(last) for flow in moving if not flow.done]
    inputs, _ = lax.optimization_barrier((inputs, operands))
    return kernel(*inputs)


def cut_body(count, spots, qkv, out, up, down, attention, feed, sems):
    width = up.shape[0]
    local = qkv.shape[2]
    place, sec = spots[0], spots[1]
    fine = width // count // 2
    half = fine // 2
    for which in range(2):
        core = sec if which == 0 else 1 - sec
        row = (place * 2 + core) * fine
        base = which * 2 * fine

        def put(n, source, target):
            pltpu.make_async_copy(source, target, sems.at[n]).start()

        mid = base + fine
        put(0, qkv.at[0, pl.ds(row, fine), :], attention.at[base:mid, :local])
        put(0, qkv.at[1, pl.ds(row, fine), :], attention.at[base:mid, local:])
        put(0, qkv.at[2, pl.ds(row, half), :], attention.at[mid : mid + half, :local])
        put(0, qkv.at[2, pl.ds(row + half, half), :], attention.at[mid : mid + half, local:])
        put(0, out.at[pl.ds((place * 2 + core) * half, half), :], attention.at[mid + half : mid + fine, :])
        put(1, up.at[pl.ds(row, fine), :], feed.at[base:mid, :])
        put(1, down.at[pl.ds(row, fine), :], feed.at[mid : mid + fine, :])
    pltpu.make_async_copy(attention, attention, sems.at[0]).wait()
    pltpu.make_async_copy(feed, feed, sems.at[1]).wait()


def cut_call(spots, count, mine):
    width = mine[2].shape[0]
    shapes = [struct((2 * width // count, width), bf16)] * 2
    return pl.pallas_call(
        functools.partial(cut_body, count),
        grid=(1,),
        in_specs=[pl.BlockSpec(memory_space=pltpu.SMEM)] + any_specs(4),
        out_specs=[pl.BlockSpec(x.shape, lambda i: (0, 0)) for x in shapes],
        out_shape=shapes,
        scratch_shapes=[pltpu.SemaphoreType.DMA((2,))],
        compiler_params=params(),
        cost_estimate=cost(0, 4 * width * width),
        name="cut",
    )(spots, *mine)


def final_call(name, body, scalars, sums, outputs):
    whole, width = sums[0].shape

    def kernel(scalar_ref, own0, far0, own1, far1, *refs):
        refs = list(refs)
        sinks = refs[: len(outputs)]
        held, sems, out_sems, *wide = refs[len(outputs) :]
        sec = scalar_ref[0]
        for layer, sides in enumerate(((own0, far0), (own1, far1))):

            @pl.when(sec == layer)
            def _():
                for side, ref in enumerate(sides):
                    pltpu.make_async_copy(ref, held.at[side], sems.at[side]).start()

        leaving = []
        for side in range(2):
            pltpu.make_async_copy(held.at[side], held.at[side], sems.at[side]).wait()
            for source, sink in body(held, side, lax.rem(sec + side, 2), wide, sinks):
                copy = pltpu.make_async_copy(source, sink, out_sems.at[len(leaving)])
                copy.start()
                leaving.append(copy)
        for copy in leaving:
            copy.wait()

    return pl.pallas_call(
        kernel,
        in_specs=[pl.BlockSpec(memory_space=pltpu.SMEM)] + any_specs(4),
        out_specs=any_specs(len(outputs)),
        out_shape=outputs,
        scratch_shapes=[
            pltpu.VMEM((2, whole, width), bf16),
            pltpu.SemaphoreType.DMA((2,)),
            pltpu.SemaphoreType.DMA((16,)),
        ]
        + [pltpu.VMEM((2,) + x.shape[:-2] + (x.shape[-2] // 2, x.shape[-1]), f32) for x in outputs],
        compiler_params=params(),
        cost_estimate=cost(0, 12 * whole * width),
        name=name,
    )(scalars, *sums)


def final_mlp_call(scalars, sums, width):
    half = width // 2

    def body(held, side, core, wide, sinks):
        at = pl.multiple_of(core * half, half)
        for n in range(2):
            wide[n][side] = held[side, n * half : (n + 1) * half, :].astype(f32)
            yield wide[n].at[side], sinks[n].at[pl.ds(at, half), :]

    return final_call("final_mlp", body, scalars, sums, [struct((width, width), f32)] * 2)


def final_attention_call(scalars, sums, width):
    local = width // 2
    first, deep = local // 2, width // 4

    def body(held, side, core, wide, sinks):
        wide[0][side] = held[side, :first, :].astype(f32)
        yield wide[0].at[side], sinks[0].at[pl.ds(pl.multiple_of(core * first, first), first), :]
        low = pl.multiple_of(core * 2 * deep, 2 * deep)
        for j in range(3):
            block = held[side, first + j * deep : first + (j + 1) * deep, :].astype(f32)
            wide[1][side, j, :deep, :] = block[:, :local]
            wide[1][side, j, deep:, :] = block[:, local:]
            yield wide[1].at[side, j], sinks[1].at[j, pl.ds(low, 2 * deep), :]

    return final_call(
        "final_attention", body, scalars, sums,
        [struct((local, width), f32), struct((3, width, local), f32)],
    )


def series_starts(lengths, rows):
    ends = jnp.cumsum(lengths)
    places = jnp.arange(rows, dtype=jnp.int32)
    passed = jnp.where(ends[None, :] <= places[:, None], ends[None, :], 0)
    return jnp.max(passed, axis=1, keepdims=True).astype(jnp.int32)


def per_device(tokens, lengths, w_qkv, w_out, w_up, w_down, norm_gain, norm_bias, cotangent):
    sec = lax.axis_index("section").astype(jnp.int32)
    tensor = lax.axis_index("tensor")
    rank = lax.axis_index("dp")
    count = lax.axis_size("dp")
    own_rows = tokens.shape[1]
    rows = 2 * own_rows
    width = tokens.shape[2]
    local = width // 2
    swap = [(0, 1), (1, 0)]
    bits = own_bits(sec, rank, count)
    fan = min(3, len(bits))
    size = 1 << fan
    ring_up, ring_down = ring_routes(count, size)
    in_ring = lax.rem(rank, size)
    place = jnp.where(lax.rem(in_ring, 2) == 0, in_ring // 2, size - 1 - in_ring // 2)
    slot_places = lax.rem(place + np.asarray(slot_steps(size), np.int32) + size, size).astype(jnp.int32)

    def across(shard):
        other = lax.ppermute(shard, "tensor", swap)
        return jnp.where(
            tensor == 0,
            jnp.concatenate([shard, other], axis=0),
            jnp.concatenate([other, shard], axis=0),
        )

    def to_other_core(value):
        return lax.ppermute(value, "section", swap)

    def swap_cores(value):
        return lax.ppermute(value, "section", swap)

    def swap_tensor(value):
        return lax.ppermute(value, "tensor", swap)

    def move(axis, route):
        return lambda value: lax.ppermute(value, axis, route)

    def doubled(held, away, step):
        low = bits[step] == 0
        return jnp.concatenate([jnp.where(low, held, away), jnp.where(low, away, held)], axis=0)

    def sum_steps(layer, send, kept):
        received = yield send, swap_cores
        rows = kept.shape[0] // 2

        def both(side):
            a = lax.dynamic_slice_in_dim(kept, side * rows, rows, 0).astype(f32)
            b = lax.dynamic_slice_in_dim(received, side * rows, rows, 0).astype(f32)
            return a + b

        away = yield both(1 - bits[0]).astype(bf16), move(("section", "dp"), pairs_of(count, 0))
        held = (both(bits[0]) + away.astype(f32)).astype(bf16)
        for step in range(1, len(bits)):
            rows //= 2
            part = lax.dynamic_slice_in_dim(held, (1 - bits[step]) * rows, rows, 0)
            rest = lax.dynamic_slice_in_dim(held, bits[step] * rows, rows, 0)
            away = yield part, move(("section", "dp"), pairs_of(count, step))
            held = (rest.astype(f32) + away.astype(f32)).astype(bf16)
        for step in reversed(range(len(bits))):
            away = yield held, move(("section", "dp"), pairs_of(count, step))
            held = doubled(held, away, step)
        far = yield held, move("section", [(1 - layer, layer)])
        return held, far

    def around(pair):
        return lax.ppermute(pair[0], "dp", ring_up), lax.ppermute(pair[1], "dp", ring_down)

    def spread_steps(piece, route):
        send = move("section", route)

        def both_ways(pair):
            return around(pair) + (send(pair[0]), send(pair[1]))

        def first_way(pair):
            return around(pair) + (send(pair[0]),)

        a, b, far = yield (piece, piece), first_way
        ups, downs, far_ups, far_downs = [piece, a], [b], [far], []
        for _ in range(size // 2 - 2):
            a, b, c, d = yield (ups[-1], downs[-1]), both_ways
            ups.append(a)
            downs.append(b)
            far_ups.append(c)
            far_downs.append(d)
        half = piece.shape[0] // 2
        whole = ups[-1], downs[-1]

        def last_way(pair):
            return around((pair[0][:half], pair[1][half:])) + (send(pair[0]), send(pair[1]))

        a, b, c, d = yield whole, last_way
        far_ups.append(c)
        far_downs.append(d)
        c, d = yield (a, b), lambda pair: (send(pair[0]), send(pair[1]))
        return ups + downs + [a, b], far_ups + far_downs + [c, d]

    def butterfly_steps(part):
        away = yield part, swap_cores
        part = part + away
        distance = 1
        while distance < count:
            away = yield part, move("dp", [(i, i ^ distance) for i in range(count)])
            part = part + away
            distance *= 2
        return part

    mine = (jnp.transpose(w_qkv[0], (1, 0, 2)), w_out[0], w_up[0], w_down[0])
    u0 = across(lax.dynamic_index_in_dim(tokens, sec, 0, False))
    start = series_starts(lax.dynamic_index_in_dim(lengths[0], sec, 0, False), rows)
    norms = jnp.concatenate([norm_gain[0], norm_bias[0]], axis=0)
    swap_norms = to_other_core(norms)
    norm_of = [
        jnp.where(sec == 0, norms, swap_norms),
        jnp.where(sec == 0, swap_norms, norms),
    ]

    spots = jnp.stack([place, sec]).astype(jnp.int32)
    cuts = cut_call(spots, size, mine)

    swapped = tuple(to_other_core(w) for w in mine)
    names = ("qkv", "out", "up", "down")
    mine_of, swapped_of = dict(zip(names, mine)), dict(zip(names, swapped))
    def to_outputs(pair):
        rows_of = [
            lax.dynamic_slice_in_dim(value, tensor * own_rows, own_rows, 0) for value in pair
        ]
        stay = jnp.where(sec == 0, rows_of[0], rows_of[1])
        go = jnp.where(sec == 0, rows_of[1], rows_of[0])
        came = to_other_core(go)
        return jnp.where(sec == 0, jnp.stack([stay, came]), jnp.stack([came, stay]))[None]

    own_weights = [Own(layer, sec, mine_of, swapped_of) for layer in range(2)]
    here = sec.reshape(1)
    gains = [[norm_of[layer][i : i + 1] for i in range(4)] for layer in range(2)]

    both_cores = [(0, 1), (1, 0)]
    sections = ("section", "tensor")
    attention_cut = swap_tensor(cuts[0])
    feed_cut = lax.ppermute(cuts[1], sections, [(0, 1), (1, 0)])
    span = width // size
    came = swap_cores(jnp.concatenate([attention_cut[span:], feed_cut[span:]], axis=0))
    attention_mine = attention_cut[:span]
    piece = jnp.concatenate(
        [
            jnp.where(sec == 0, attention_mine, came[:span]),
            jnp.where(sec == 0, feed_cut[:span], came[span:]),
            jnp.where(sec == 0, came[:span], attention_mine),
        ],
        axis=0,
    )

    def slots_of(arrays, rows, last):
        half = span // 2
        return [((x, rows), (x, rows + half)) for x in arrays[: size - 1]] + [last(arrays[size - 1 :])]

    def pieces_of(gathered, rows, last):
        return Pieces(sec, slot_places, *(slots_of(arrays, rows, last) for arrays in gathered))

    half = span // 2
    gather = Flow(spread_steps(piece, both_cores))
    operand = gather.advance()
    (u0, start), _ = lax.optimization_barrier(((u0, start), operand))
    a0 = first_call(here, own_weights[0], u0, start, gains[0][0], gains[0][2])
    whole_up = lax.ppermute(mine[2], sections, [(2, 3), (3, 2)])
    whole_down = lax.ppermute(mine[3], sections, [(2, 3), (3, 2)])
    together([gather], a0["h"])
    together([gather])
    together([gather])
    operands, (n1_zero, whole_up) = together([gather], a0["n1"], whole_up)
    a0 = dict(a0, n1=n1_zero)
    gathered = finished(gather)
    far_zero = pieces_of(gathered, 0, lambda x: ((x[0], 0), (x[0], half)))
    far_two_zero = pieces_of(gathered, span, lambda x: ((x[0], span), (x[1], 0)))
    far_one = pieces_of(gathered, 2 * span, lambda x: ((x[1], half), (x[1], span)))
    b0 = kernel_after(
        lambda *x: second_call(here, far_zero, *x), [], None,
        a0["n1"], start, a0["h"], gains[0][1], gains[0][3],
    )
    n2_zero, whole_down = lax.optimization_barrier((b0["n2"], whole_down))
    b0 = dict(b0, n2=n2_zero)
    c0 = kernel_after(
        lambda *x: feed_call(here, own_weights[0], far_two_zero, *x), [], None, b0["n2"], b0["h"]
    )
    late, _ = lax.optimization_barrier((lax.dynamic_index_in_dim(cotangent, sec, 0, False), c0["y"]))
    gy1 = across(late)
    a1 = kernel_after(
        lambda *x: first_call(here, own_weights[1], *x), [], None, c0["y"], start, gains[1][0], gains[1][2]
    )
    (whole_up, whole_down), _ = lax.optimization_barrier(((whole_up, whole_down), c0["y"]))
    b1 = kernel_after(
        lambda *x: second_call(here, far_one, *x), [], None,
        a1["n1"], start, a1["h"], gains[1][1], gains[1][3],
    )
    to_first = move("section", [(1, 0)])
    far_two_one = Own(
        1, sec, dict(up=whole_up, down=whole_down), dict(up=to_first(whole_up), down=to_first(whole_down))
    )
    c1 = kernel_after(
        lambda *x: feed_call(here, own_weights[1], far_two_one, *x), [], None, b1["n2"], b1["h"]
    )
    outputs = to_outputs([c0["y"], c1["y"]])

    def feed_back(layer, far_two, moving, last, gy, b, c):
        return kernel_after(
            lambda *x: feed_back_call(here, own_weights[layer], far_two, *x), moving, last,
            gy, c["slope"], c["slope_far"], b["h"], c["z"], b["n2"], gains[layer][1],
        )

    def heads_back(layer, moving, last, a, e):
        return kernel_after(
            lambda *x: heads_back_call(here, own_weights[layer], *x), moving, last,
            a["qkv"], start, e["gh"], a["o"], a["n1"],
        )

    def input_back(layer, far, moving, last, a, b, e, f, u):
        return kernel_after(
            lambda *x: input_back_call(here, own_weights[layer], far, *x), moving, last,
            b["qkv"], start, e["gh"], f["d"], e["dh"], u, gains[layer][0],
        )

    e1 = feed_back(1, far_two_one, [], None, gy1, b1, c1)
    outputs, gh = lax.optimization_barrier((outputs, e1["gh"]))
    e1 = dict(e1, gh=gh)
    sums = [Flow(sum_steps(1, e1["give"], e1["keep"]))]
    f1 = heads_back(1, sums, gh, a1, e1)
    sums.append(Flow(sum_steps(1, f1["give"], f1["keep"])))
    g1 = input_back(1, far_one, sums, f1["d"], a1, b1, e1, f1, c0["y"])
    e0 = feed_back(0, far_two_zero, sums, g1["du"], g1["du"], b0, c0)
    sums.append(Flow(sum_steps(0, e0["give"], e0["keep"])))
    f0 = heads_back(0, sums, e0["gh"], a0, e0)
    sums.append(Flow(sum_steps(0, f0["give"], f0["keep"])))
    g0 = input_back(0, far_zero, sums, f0["d"], a0, b0, e0, f0, u0)
    norm_grads = [
        jnp.concatenate([g["grads"][:1], e["grads"][:1], g["grads"][1:], e["grads"][1:]])
        for g, e in ((g0, e0), (g1, e1))
    ]
    norm_flow = Flow(butterfly_steps(jnp.concatenate(norm_grads, axis=0)))
    norm_flow.advance()
    grads_in = to_outputs([g0["du"], g1["du"]])
    for flow in sums:
        flow.advance(g0["du"])
    (grads_in, results), _ = lax.optimization_barrier(((grads_in, sums[3].results), g0["du"]))
    sums[3].results = results
    while any(not flow.done for flow in sums + [norm_flow]):
        for flow in sums + [norm_flow]:
            if not flow.done:
                flow.advance()
    parts = [flow.value for flow in sums]
    grad_down, grad_up = final_mlp_call(here, [*parts[2], *parts[0]], width)
    grad_out, grad_qkv = final_attention_call(here, [*parts[3], *parts[1]], width)
    norm_total = norm_flow.value
    norm_sum = jnp.where(sec == 0, norm_total[:4], norm_total[4:])
    norm_sum = lax.dynamic_slice_in_dim(norm_sum, tensor * local, local, 1)

    return (
        outputs,
        grads_in,
        jnp.transpose(grad_qkv, (1, 0, 2))[None],
        grad_out[None],
        grad_up[None],
        grad_down[None],
        norm_sum[None, :2],
        norm_sum[None, 2:],
    )


def solution(mesh):
    in_specs = (
        P(None, ("dp", "tensor"), None),
        P("dp", None, None),
        P("section", None, None, "tensor"),
        P("section", "tensor", None),
        P("section", None, "tensor"),
        P("section", "tensor", None),
        P("section", None, None),
        P("section", None, None),
        P(None, ("dp", "tensor"), None),
    )
    out_specs = (
        P("section", None, ("dp", "tensor"), None),
        P("section", None, ("dp", "tensor"), None),
        P("section", None, None, "tensor"),
        P("section", "tensor", None),
        P("section", None, "tensor"),
        P("section", "tensor", None),
        P("section", None, "tensor"),
        P("section", None, "tensor"),
    )
    return jax.shard_map(
        per_device, mesh=mesh, in_specs=in_specs, out_specs=out_specs, check_vma=False
    )
```

```python
import functools

import jax
import jax.numpy as jnp
import numpy as np
from jax import lax
from jax.experimental import pallas as pl
from jax.experimental.pallas import tpu as pltpu
from jax.sharding import PartitionSpec as P

HEAD_DIM = 128
BAND = 128
EPSILON = 1e-05
MASKED = -1e30
VMEM = 60 * 1024 * 1024
bf16 = jnp.bfloat16
f32 = jnp.float32


def params():
    return pltpu.CompilerParams(vmem_limit_bytes=VMEM)


def cost(flops, moved):
    return pl.CostEstimate(
        flops=int(flops), bytes_accessed=int(moved), transcendentals=0
    )


def dot(a, b):
    return jnp.dot(a, b, preferred_element_type=f32)


def dot_nt(a, b):
    return lax.dot_general(a, b, (((1,), (1,)), ((), ())), preferred_element_type=f32)


def dot_tn(a, b):
    return lax.dot_general(a, b, (((0,), (0,)), ((), ())), preferred_element_type=f32)


def unit_of(values):
    centre = values - jnp.mean(values, axis=-1, keepdims=True)
    spread = jnp.mean(centre * centre, axis=-1, keepdims=True)
    scale = lax.rsqrt(spread + EPSILON)
    return centre * scale, scale


def norm_back(incoming, values, gain):
    unit, scale = unit_of(values)
    scaled = incoming * gain
    inner = (
        scaled
        - jnp.mean(scaled, axis=-1, keepdims=True)
        - unit * jnp.mean(scaled * unit, axis=-1, keepdims=True)
    )
    grads = jnp.concatenate(
        [
            jnp.sum(incoming * unit, axis=0, keepdims=True),
            jnp.sum(incoming, axis=0, keepdims=True),
        ],
        axis=0,
    )
    return scale * inner, grads


def any_specs(n):
    return [pl.BlockSpec(memory_space=pl.ANY)] * n


class Own:
    def __init__(self, layer, sec, mine, swapped):
        self.scalars = jnp.stack([sec, jnp.full_like(sec, layer)])
        self.mine, self.swapped = mine, swapped

    def operands(self, names):
        return [self.mine[n] for n in names] + [self.swapped[n] for n in names]

    def start(self, names, scalars, refs, targets, sems):
        mine, swapped = refs[: len(names)], refs[len(names) :]
        for condition, side in ((True, mine), (False, swapped)):

            @pl.when((scalars[0] == scalars[1]) == condition)
            def _():
                for n, (ref, target) in enumerate(zip(side, targets)):
                    pltpu.make_async_copy(ref, target, sems.at[n, 0]).start()

    def wait(self, n, name, target, sems):
        pltpu.make_async_copy(target, target, sems.at[n, 0]).wait()


class Pieces:
    def __init__(self, sec, places, own, far):
        self.count = len(own)
        self.scalars = jnp.concatenate([sec.reshape(1), places])
        self.arrays, self.index = [], []
        for side in (own, far):
            rows = []
            for slot in side:
                parts = []
                for array, row in slot:
                    known = [n for n, x in enumerate(self.arrays) if x is array]
                    if not known:
                        self.arrays.append(array)
                        known = [len(self.arrays) - 1]
                    parts.append((known[0], row))
                rows.append(parts)
            self.index.append(rows)

    def operands(self, names):
        return self.arrays

    def start(self, names, scalars, refs, targets, sems):
        every = slice(None)
        for side, slots in enumerate(self.index):
            core = lax.rem(scalars[0] + side, 2)
            for slot, ((n0, row0), (n1, row1)) in enumerate(slots):
                spot = scalars[1 + slot] * 2 + core
                first, second = refs[n0], refs[n1]
                for n, (name, target) in enumerate(zip(names, targets)):

                    def put(source, place):
                        pltpu.make_async_copy(source, place, sems.at[n, side]).start()

                    if name == "qkv":
                        deep, local = target.shape[1], target.shape[2]
                        fine = deep // self.count // 2
                        half = fine // 2
                        row = spot * fine
                        for j in range(2):
                            columns = slice(j * local, (j + 1) * local)
                            put(
                                first.at[row0 : row0 + fine, columns],
                                target.at[j, pl.ds(row, fine), :],
                            )
                            put(
                                second.at[row1 : row1 + half, columns],
                                target.at[2, pl.ds(row + j * half, half), :],
                            )
                    elif name == "out":
                        fine = target.shape[0] // self.count // 2
                        put(
                            second.at[row1 + fine : row1 + 2 * fine, every],
                            target.at[pl.ds(spot * fine, fine), :],
                        )
                    else:
                        fine = target.shape[0] // self.count // 2
                        source = second.at[row1 : row1 + fine, every] if name == "down" else first.at[row0 : row0 + fine, every]
                        put(source, target.at[pl.ds(spot * fine, fine), :])

    def wait(self, n, name, target, sems):
        for side in range(2):
            if name == "qkv":
                part = target.at[:, : target.shape[1] // 2, :]
            else:
                part = target.at[: target.shape[0] // 2, :]
            pltpu.make_async_copy(part, part, sems.at[n, side]).wait()


def struct(shape, dtype):
    return jax.ShapeDtypeStruct(shape, dtype)


class Room:
    def __init__(self, refs, sources, sinks, in_sems, out_sems, weights):
        self.refs, self.sources, self.sinks = refs, sources, sinks
        self.in_sems, self.out_sems, self.weights = in_sems, out_sems, weights
        self.waited, self.leaving = set(), []

    def start(self, names):
        for n, name in enumerate(names):
            pltpu.make_async_copy(self.sources[name], self.refs[name], self.in_sems.at[n]).start()
        self.order = list(names)

    def get(self, name):
        if name in self.sources and name not in self.waited:
            self.waited.add(name)
            ref = self.refs[name]
            pltpu.make_async_copy(ref, ref, self.in_sems.at[self.order.index(name)]).wait()
        return self.refs[name]

    def weight(self, name):
        loader, place, kind, target, sems = self.weights[name]
        if name not in self.waited:
            self.waited.add(name)
            loader.wait(place, kind, target, sems)
        return target

    def send(self, pairs):
        for source, sink in pairs:
            copy = pltpu.make_async_copy(source, sink, self.out_sems.at[len(self.leaving)])
            copy.start()
            self.leaving.append(copy)

    def flush(self, *names):
        self.send([(self.refs[name], self.sinks[name]) for name in names])

    def close(self):
        for copy in self.leaving:
            copy.wait()


def room_call(name, body, scalars, weights, inputs, outputs, scratch, copies, flops):
    in_names, out_names, temp_names = list(inputs), list(outputs), list(scratch)
    operands = [loader.operands([k for k, _ in kinds]) for _, loader, kinds in weights]
    scalar_list = [scalars] + [loader.scalars for _, loader, _ in weights]
    local_out = [n for n in out_names if n not in scratch]

    def whole(*refs):
        refs = list(refs)

        def take(n):
            got = refs[:n]
            del refs[:n]
            return got

        scalar_refs = take(len(scalar_list))
        sources = dict(zip(in_names, take(len(in_names))))
        weight_sources = [take(len(o)) for o in operands]
        sinks = dict(zip(out_names, take(len(out_names))))
        held = dict(zip(in_names, take(len(in_names))))
        held.update(zip(local_out, take(len(local_out))))
        held.update(zip(temp_names, take(len(temp_names))))
        in_sems, out_sems = take(2)
        table = {}
        starts = []
        for (prefix, loader, kinds), source, scalar in zip(weights, weight_sources, scalar_refs[1:]):
            targets = take(len(kinds))
            sems = take(1)[0]
            starts.append((loader, [k for k, _ in kinds], scalar, source, targets, sems))
            for place, (kind, _) in enumerate(kinds):
                table[prefix + kind] = (loader, place, kind, targets[place], sems)
        room = Room(held, sources, sinks, in_sems, out_sems, table)
        room.start(in_names)
        for loader, kinds, scalar, source, targets, sems in starts:
            loader.start(kinds, scalar, source, targets, sems)
        body(room, scalar_refs[0])
        for name in in_names:
            room.get(name)
        for key in table:
            room.weight(key)
        room.close()

    vmem = [pltpu.VMEM(inputs[n].shape, inputs[n].dtype) for n in in_names]
    vmem += [pltpu.VMEM(outputs[n].shape, outputs[n].dtype) for n in local_out]
    vmem += [pltpu.VMEM(*scratch[n]) for n in temp_names]
    vmem += [pltpu.SemaphoreType.DMA((max(len(in_names), 1),)), pltpu.SemaphoreType.DMA((copies,))]
    for _, _, kinds in weights:
        vmem += [pltpu.VMEM(shape, bf16) for _, shape in kinds]
        vmem.append(pltpu.SemaphoreType.DMA((len(kinds), 2)))
    flat = [x for o in operands for x in o]
    moved = sum(x.size * x.dtype.itemsize for x in list(inputs.values()) + list(outputs.values()))
    moved += sum(2 * int(np.prod(shape)) for _, _, kinds in weights for _, shape in kinds)
    result = pl.pallas_call(
        whole,
        in_specs=[pl.BlockSpec(memory_space=pltpu.SMEM)] * len(scalar_list)
        + any_specs(len(in_names) + len(flat)),
        out_specs=any_specs(len(out_names)),
        out_shape=[outputs[n] for n in out_names],
        scratch_shapes=vmem,
        compiler_params=params(),
        cost_estimate=cost(flops, moved),
        name=name,
    )(*scalar_list, *inputs.values(), *flat)
    return dict(zip(out_names, result))


def band_probs(q, k, start_ref, block):
    low = max(block - 1, 0) * BAND
    high = (block + 1) * BAND
    scores = dot_nt(q[block * BAND : high], k[low:high]) * HEAD_DIM**-0.5
    row = lax.broadcasted_iota(jnp.int32, scores.shape, 0) + block * BAND
    column = lax.broadcasted_iota(jnp.int32, scores.shape, 1) + low
    first = start_ref[block * BAND : high, :]
    allowed = (column <= row) & (column >= first)
    scores = jnp.where(allowed, scores, MASKED)
    expo = jnp.exp(scores - jnp.max(scores, axis=-1, keepdims=True))
    return expo / jnp.sum(expo, axis=-1, keepdims=True), low, high


def heads_of(qkv_ref, head, local):
    return [
        qkv_ref[:, j * local + head * HEAD_DIM : j * local + (head + 1) * HEAD_DIM] for j in range(3)
    ]


def attend(qkv_ref, start_ref, o_ref):
    rows, local = o_ref.shape
    for head in range(local // HEAD_DIM):
        cut = slice(head * HEAD_DIM, (head + 1) * HEAD_DIM)
        q, k, v = heads_of(qkv_ref, head, local)
        for block in range(rows // BAND):
            probs, low, high = band_probs(q, k, start_ref, block)
            o_ref[block * BAND : high, cut] = dot(probs.astype(bf16), v[low:high]).astype(bf16)


def project(left, w, out_ref):
    local = w.shape[2]
    for j in range(3):
        out_ref[:, j * local : (j + 1) * local] = dot(left[...], w[j]).astype(bf16)


def activate(n2_ref, up, z_ref, slope_ref):
    c = np.float32(np.sqrt(2 / np.pi))
    tile = 512
    for i in range(z_ref.shape[1] // tile):
        cut = slice(i * tile, (i + 1) * tile)
        a = dot(n2_ref[...], up[:, cut])
        square = a * a
        t = jnp.tanh(c * a * (1.0 + 0.044715 * square))
        half = 0.5 * (1.0 + t)
        slope = half + 0.5 * c * a * (1.0 - t * t) * (1.0 + 3 * 0.044715 * square)
        z_ref[:, cut] = (a * half).astype(bf16)
        slope_ref[:, cut] = slope.astype(bf16)


def sizes(width):
    local, units = width // 2, width
    return {
        "qkv": (3, width, local),
        "out": (local, width),
        "up": (width, units),
        "down": (units, width),
    }


def group(prefix, loader, kinds, width):
    return prefix, loader, [(k, sizes(width)[k]) for k in kinds]


def first_call(scalars, own, u, start, gain, bias):
    rows, width = u.shape
    local = width // 2

    def body(room, _):
        u_ref = room.get("u")
        unit, _ = unit_of(u_ref[...].astype(f32))
        n1 = room.get("n1")
        n1[...] = (unit * room.get("gain")[...] + room.get("bias")[...]).astype(bf16)
        project(n1, room.weight("own_qkv"), room.get("qkv"))
        room.flush("n1", "qkv")
        attend(room.get("qkv"), room.get("start"), room.get("o"))
        room.flush("o")
        room.get("h")[...] = u_ref[...].astype(f32) + dot(room.get("o")[...], room.weight("own_out")[...])
        room.flush("h")

    return room_call(
        "first", body, scalars, [group("own_", own, ["qkv", "out"], width)],
        dict(u=u, start=start, gain=gain, bias=bias),
        dict(n1=struct((rows, width), bf16), qkv=struct((rows, 3 * local), bf16),
             o=struct((rows, local), bf16), h=struct((rows, width), f32)),
        {}, 4, 9 * rows * width * local,
    )


def second_call(scalars, far, n1, start, base, gain, bias):
    rows, width = base.shape
    local = width // 2

    def body(room, _):
        project(room.get("n1"), room.weight("far_qkv"), room.get("qkv"))
        room.flush("qkv")
        attend(room.get("qkv"), room.get("start"), room.get("o"))
        h = room.get("base")[...] + dot(room.get("o")[...], room.weight("far_out")[...])
        room.get("h")[...] = h
        unit, _ = unit_of(h)
        n2 = room.get("n2")
        n2[...] = (unit * room.get("gain")[...] + room.get("bias")[...]).astype(bf16)
        room.flush("h", "n2")

    return room_call(
        "second", body, scalars, [group("far_", far, ["qkv", "out"], width)],
        dict(n1=n1, start=start, base=base, gain=gain, bias=bias),
        dict(qkv=struct((rows, 3 * local), bf16), h=struct((rows, width), f32),
             n2=struct((rows, width), bf16)),
        dict(o=((rows, local), bf16)), 3, 9 * rows * width * local,
    )


def feed_call(scalars, own, far_two, n2, h):
    rows, width = h.shape
    units = width

    def body(room, _):
        n2 = room.get("n2")
        activate(n2, room.weight("own_up"), room.get("z"), room.get("slope"))
        room.flush("z", "slope")
        activate(n2, room.weight("two_up"), room.get("z_far"), room.get("slope_far"))
        room.flush("slope_far")
        y = room.get("h")[...] + dot(room.get("z")[...], room.weight("own_down")[...])
        room.get("y")[...] = (y + dot(room.get("z_far")[...], room.weight("two_down")[...])).astype(bf16)
        room.flush("y")

    tall = struct((rows, width), bf16)
    return room_call(
        "feed", body, scalars,
        [group("own_", own, ["up", "down"], width), group("two_", far_two, ["up", "down"], width)],
        dict(n2=n2, h=h), dict(z=tall, slope=tall, slope_far=tall, y=tall),
        dict(z_far=((rows, units), bf16)), 4, 8 * rows * width * units,
    )


def feed_back_call(scalars, own, far_two, gy, slope, slope_far, h, z, n2, gain):
    rows, width = gy.shape
    units = width
    half = units // 2

    def body(room, scalar):
        gy_ref = room.get("gy")
        dz = dot_nt(gy_ref[...], room.weight("own_down")[...])
        da = room.get("da")
        da[...] = (dz * room.get("slope")[...].astype(f32)).astype(bf16)
        down, up = room.get("grad_down"), room.get("grad_up")
        down[...] = dot_tn(room.get("z")[...], gy_ref[...]).astype(bf16)
        up[...] = dot_tn(room.get("n2")[...], da[...]).astype(bf16)
        for name, which in (("give", 1 - scalar[0]), ("keep", scalar[0])):
            at = pl.multiple_of(which * half, half)
            sink = room.sinks[name]
            room.send([(down.at[pl.ds(at, half), :], sink.at[:half, :])])
            room.send([(up.at[pl.ds(at, half), :], sink.at[half:, :])])
        term = dot_nt(da[...], room.weight("own_up")[...])
        dz = dot_nt(gy_ref[...], room.weight("two_down")[...])
        da = (dz * room.get("slope_far")[...].astype(f32)).astype(bf16)
        term = term + dot_nt(da, room.weight("two_up")[...])
        back, grads = norm_back(term, room.get("h")[...], room.get("gain")[...])
        dh = gy_ref[...].astype(f32) + back
        room.get("dh")[...] = dh
        room.get("gh")[...] = dh.astype(bf16)
        room.get("grads")[...] = grads
        room.flush("dh", "gh", "grads")

    part = struct((2 * half, width), bf16)
    tall = ((rows, width), bf16)
    return room_call(
        "feed_back", body, scalars,
        [group("own_", own, ["down", "up"], width), group("two_", far_two, ["down", "up"], width)],
        dict(gy=gy, slope=slope, z=z, n2=n2, slope_far=slope_far, h=h, gain=gain),
        dict(give=part, keep=part, dh=struct((rows, width), f32), gh=struct((rows, width), bf16),
             grads=struct((2, width), f32)),
        dict(da=tall, grad_down=((units, width), bf16), grad_up=((width, units), bf16),
             give=((16, 128), bf16), keep=((16, 128), bf16)),
        7, 12 * rows * width * units,
    )


def attend_back(qkv_ref, start_ref, do_all, out):
    rows, local = do_all.shape
    blocks = rows // BAND
    for head in range(local // HEAD_DIM):
        q, k, v = heads_of(qkv_ref, head, local)
        do = do_all[:, head * HEAD_DIM : (head + 1) * HEAD_DIM]
        columns = [
            slice(j * local + head * HEAD_DIM, j * local + (head + 1) * HEAD_DIM) for j in range(3)
        ]
        dk_parts, dv_parts = [None] * blocks, [None] * blocks

        def put(parts, term, low):
            for piece in range(term.shape[0] // BAND):
                place = low // BAND + piece
                add = term[piece * BAND : (piece + 1) * BAND]
                parts[place] = add if parts[place] is None else parts[place] + add

        for block in range(blocks):
            probs, low, high = band_probs(q, k, start_ref, block)
            here = slice(block * BAND, high)
            dp = dot_nt(do[here], v[low:high])
            inner = jnp.sum(probs * dp, axis=-1, keepdims=True)
            ds = (probs * (dp - inner) * HEAD_DIM**-0.5).astype(bf16)
            out[here, columns[0]] = dot(ds, k[low:high]).astype(bf16)
            put(dk_parts, dot_tn(ds, q[here]), low)
            put(dv_parts, dot_tn(probs.astype(bf16), do[here]), low)
        for block in range(blocks):
            here = slice(block * BAND, (block + 1) * BAND)
            out[here, columns[1]] = dk_parts[block].astype(bf16)
            out[here, columns[2]] = dv_parts[block].astype(bf16)


def heads_back_call(scalars, own, qkv, start, gh, o, n1):
    rows, width = gh.shape
    local = width // 2
    first, deep = local // 2, width // 4

    def body(room, scalar):
        gh_ref = room.get("gh")
        do_all = dot_nt(gh_ref[...], room.weight("own_out")[...]).astype(bf16)
        d = room.get("d")
        attend_back(room.get("qkv"), room.get("start"), do_all, d)
        room.flush("d")
        grad_out, grad_qkv = room.get("grad_out"), room.get("grad_qkv")
        grad_out[...] = dot_tn(room.get("o")[...], gh_ref[...]).astype(bf16)
        grad_qkv[...] = dot_tn(room.get("n1")[...], d[...]).astype(bf16)
        for name, which in (("give", 1 - scalar[0]), ("keep", scalar[0])):
            sink = room.sinks[name]
            at = pl.multiple_of(which * first, first)
            room.send([(grad_out.at[pl.ds(at, first), :], sink.at[:first, :])])
            for side in range(2):
                at = pl.multiple_of((which * 2 + side) * deep, deep)
                for j in range(3):
                    room.send([(
                        grad_qkv.at[pl.ds(at, deep), j * local : (j + 1) * local],
                        sink.at[
                            first + j * deep : first + (j + 1) * deep,
                            side * local : (side + 1) * local,
                        ],
                    )])

    part = struct((first + 3 * deep, width), bf16)
    return room_call(
        "heads_back", body, scalars, [group("own_", own, ["out"], width)],
        dict(gh=gh, qkv=qkv, start=start, o=o, n1=n1),
        dict(give=part, keep=part, d=struct((rows, 3 * local), bf16)),
        dict(grad_out=((local, width), bf16), grad_qkv=((width, 3 * local), bf16),
             give=((16, 128), bf16), keep=((16, 128), bf16)),
        15, 17 * rows * width * local,
    )


def input_back_call(scalars, own, far, qkv_far, start, gh, d, dh, u, gain):
    rows, width = gh.shape
    local = width // 2

    def body(room, _):
        do_all = dot_nt(room.get("gh")[...], room.weight("far_out")[...]).astype(bf16)
        d_far = room.get("d_far")
        attend_back(room.get("qkv"), room.get("start"), do_all, d_far)
        term = None
        for ref, w in ((room.get("d"), room.weight("own_qkv")), (d_far, room.weight("far_qkv"))):
            for j in range(3):
                part = dot_nt(ref[:, j * local : (j + 1) * local], w[j])
                term = part if term is None else term + part
        back, grads = norm_back(term, room.get("u")[...].astype(f32), room.get("gain")[...])
        room.get("du")[...] = (room.get("dh")[...] + back).astype(bf16)
        room.get("grads")[...] = grads
        room.flush("du", "grads")

    return room_call(
        "input_back", body, scalars,
        [group("far_", far, ["out", "qkv"], width), group("own_", own, ["qkv"], width)],
        dict(gh=gh, qkv=qkv_far, start=start, d=d, u=u, gain=gain, dh=dh),
        dict(du=struct((rows, width), bf16), grads=struct((2, width), f32)),
        dict(d_far=((rows, 3 * local), bf16)), 2, 21 * rows * width * local,
    )


def ring_walk(size):
    return list(range(0, size, 2)) + list(range(1, size, 2))[::-1]


def ring_routes(count, size):
    walk = ring_walk(size)
    up = []
    for base in range(0, count, size):
        for place in range(size):
            up.append((base + walk[place], base + walk[(place + 1) % size]))
    return up, [(b, a) for a, b in up]


def slot_steps(size):
    return list(range(0, -size // 2, -1)) + list(range(1, size // 2)) + [size // 2]


def halving_order(count):
    bits = count.bit_length() - 1
    first = list(range(bits))
    second = [1, 0] + first[2:] if bits > 1 else first
    return first, second


def pairs_of(count, step):
    routes = []
    for core, order in enumerate(halving_order(count)):
        for i in range(count):
            routes.append((core * count + i, core * count + (i ^ (1 << order[step]))))
    return routes


def own_bits(sec, rank, count):
    first, second = halving_order(count)
    return [
        lax.rem(rank >> jnp.where(sec == 0, a, b), 2) for a, b in zip(first, second)
    ]


class Flow:
    def __init__(self, steps):
        self.steps, self.results, self.value, self.done = steps, None, None, False

    def advance(self, after=None):
        if after is not None and self.results is not None:
            self.results, _ = lax.optimization_barrier((self.results, after))
        try:
            operands, send = self.steps.send(self.results)
        except StopIteration as stop:
            self.value, self.done = stop.value, True
            return ()
        self.results = send(operands)
        return operands


def finished(flow):
    while not flow.done:
        flow.advance()
    return flow.value


def together(flows, *others):
    moving = [flow for flow in flows if not flow.done]
    results, others = lax.optimization_barrier(([flow.results for flow in moving], others))
    for flow, result in zip(moving, results):
        flow.results = result
    return [flow.advance() for flow in moving], others


def kernel_after(kernel, moving, last, *inputs):
    operands = [flow.advance(last) for flow in moving if not flow.done]
    inputs, _ = lax.optimization_barrier((inputs, operands))
    return kernel(*inputs)


def cut_body(count, spots, qkv, out, up, down, attention, feed, sems):
    width = up.shape[0]
    local = qkv.shape[2]
    place, sec = spots[0], spots[1]
    fine = width // count // 2
    half = fine // 2
    for which in range(2):
        core = sec if which == 0 else 1 - sec
        row = (place * 2 + core) * fine
        base = which * 2 * fine

        def put(n, source, target):
            pltpu.make_async_copy(source, target, sems.at[n]).start()

        mid = base + fine
        put(0, qkv.at[0, pl.ds(row, fine), :], attention.at[base:mid, :local])
        put(0, qkv.at[1, pl.ds(row, fine), :], attention.at[base:mid, local:])
        put(0, qkv.at[2, pl.ds(row, half), :], attention.at[mid : mid + half, :local])
        put(0, qkv.at[2, pl.ds(row + half, half), :], attention.at[mid : mid + half, local:])
        put(0, out.at[pl.ds((place * 2 + core) * half, half), :], attention.at[mid + half : mid + fine, :])
        put(1, up.at[pl.ds(row, fine), :], feed.at[base:mid, :])
        put(1, down.at[pl.ds(row, fine), :], feed.at[mid : mid + fine, :])
    pltpu.make_async_copy(attention, attention, sems.at[0]).wait()
    pltpu.make_async_copy(feed, feed, sems.at[1]).wait()


def cut_call(spots, count, mine):
    width = mine[2].shape[0]
    shapes = [struct((2 * width // count, width), bf16)] * 2
    return pl.pallas_call(
        functools.partial(cut_body, count),
        grid=(1,),
        in_specs=[pl.BlockSpec(memory_space=pltpu.SMEM)] + any_specs(4),
        out_specs=[pl.BlockSpec(x.shape, lambda i: (0, 0)) for x in shapes],
        out_shape=shapes,
        scratch_shapes=[pltpu.SemaphoreType.DMA((2,))],
        compiler_params=params(),
        cost_estimate=cost(0, 4 * width * width),
        name="cut",
    )(spots, *mine)


def final_call(name, body, scalars, sums, outputs):
    whole, width = sums[0].shape

    def kernel(scalar_ref, own0, far0, own1, far1, *refs):
        refs = list(refs)
        sinks = refs[: len(outputs)]
        held, sems, out_sems, *wide = refs[len(outputs) :]
        sec = scalar_ref[0]
        for layer, sides in enumerate(((own0, far0), (own1, far1))):

            @pl.when(sec == layer)
            def _():
                for side, ref in enumerate(sides):
                    pltpu.make_async_copy(ref, held.at[side], sems.at[side]).start()

        leaving = []
        for side in range(2):
            pltpu.make_async_copy(held.at[side], held.at[side], sems.at[side]).wait()
            for source, sink in body(held, side, lax.rem(sec + side, 2), wide, sinks):
                copy = pltpu.make_async_copy(source, sink, out_sems.at[len(leaving)])
                copy.start()
                leaving.append(copy)
        for copy in leaving:
            copy.wait()

    return pl.pallas_call(
        kernel,
        in_specs=[pl.BlockSpec(memory_space=pltpu.SMEM)] + any_specs(4),
        out_specs=any_specs(len(outputs)),
        out_shape=outputs,
        scratch_shapes=[
            pltpu.VMEM((2, whole, width), bf16),
            pltpu.SemaphoreType.DMA((2,)),
            pltpu.SemaphoreType.DMA((16,)),
        ]
        + [pltpu.VMEM((2,) + x.shape[:-2] + (x.shape[-2] // 2, x.shape[-1]), f32) for x in outputs],
        compiler_params=params(),
        cost_estimate=cost(0, 12 * whole * width),
        name=name,
    )(scalars, *sums)


def final_mlp_call(scalars, sums, width):
    half = width // 2

    def body(held, side, core, wide, sinks):
        at = pl.multiple_of(core * half, half)
        for n in range(2):
            wide[n][side] = held[side, n * half : (n + 1) * half, :].astype(f32)
            yield wide[n].at[side], sinks[n].at[pl.ds(at, half), :]

    return final_call("final_mlp", body, scalars, sums, [struct((width, width), f32)] * 2)


def final_attention_call(scalars, sums, width):
    local = width // 2
    first, deep = local // 2, width // 4

    def body(held, side, core, wide, sinks):
        wide[0][side] = held[side, :first, :].astype(f32)
        yield wide[0].at[side], sinks[0].at[pl.ds(pl.multiple_of(core * first, first), first), :]
        low = pl.multiple_of(core * 2 * deep, 2 * deep)
        for j in range(3):
            block = held[side, first + j * deep : first + (j + 1) * deep, :].astype(f32)
            wide[1][side, j, :deep, :] = block[:, :local]
            wide[1][side, j, deep:, :] = block[:, local:]
            yield wide[1].at[side, j], sinks[1].at[j, pl.ds(low, 2 * deep), :]

    return final_call(
        "final_attention", body, scalars, sums,
        [struct((local, width), f32), struct((3, width, local), f32)],
    )


def series_starts(lengths, rows):
    ends = jnp.cumsum(lengths)
    places = jnp.arange(rows, dtype=jnp.int32)
    passed = jnp.where(ends[None, :] <= places[:, None], ends[None, :], 0)
    return jnp.max(passed, axis=1, keepdims=True).astype(jnp.int32)


def per_device(tokens, lengths, w_qkv, w_out, w_up, w_down, norm_gain, norm_bias, cotangent):
    sec = lax.axis_index("section").astype(jnp.int32)
    tensor = lax.axis_index("tensor")
    rank = lax.axis_index("dp")
    count = lax.axis_size("dp")
    own_rows = tokens.shape[1]
    rows = 2 * own_rows
    width = tokens.shape[2]
    local = width // 2
    swap = [(0, 1), (1, 0)]
    bits = own_bits(sec, rank, count)
    fan = min(3, len(bits))
    size = 1 << fan
    ring_up, ring_down = ring_routes(count, size)
    in_ring = lax.rem(rank, size)
    place = jnp.where(lax.rem(in_ring, 2) == 0, in_ring // 2, size - 1 - in_ring // 2)
    slot_places = lax.rem(place + np.asarray(slot_steps(size), np.int32) + size, size).astype(jnp.int32)

    def across(shard):
        other = lax.ppermute(shard, "tensor", swap)
        return jnp.where(
            tensor == 0,
            jnp.concatenate([shard, other], axis=0),
            jnp.concatenate([other, shard], axis=0),
        )

    def to_other_core(value):
        return lax.ppermute(value, "section", swap)

    def swap_cores(value):
        return lax.ppermute(value, "section", swap)

    def swap_tensor(value):
        return lax.ppermute(value, "tensor", swap)

    def move(axis, route):
        return lambda value: lax.ppermute(value, axis, route)

    def doubled(held, away, step):
        low = bits[step] == 0
        return jnp.concatenate([jnp.where(low, held, away), jnp.where(low, away, held)], axis=0)

    def sum_steps(layer, send, kept):
        received = yield send, swap_cores
        rows = kept.shape[0] // 2

        def both(side):
            a = lax.dynamic_slice_in_dim(kept, side * rows, rows, 0).astype(f32)
            b = lax.dynamic_slice_in_dim(received, side * rows, rows, 0).astype(f32)
            return a + b

        away = yield both(1 - bits[0]).astype(bf16), move(("section", "dp"), pairs_of(count, 0))
        held = (both(bits[0]) + away.astype(f32)).astype(bf16)
        for step in range(1, len(bits)):
            rows //= 2
            part = lax.dynamic_slice_in_dim(held, (1 - bits[step]) * rows, rows, 0)
            rest = lax.dynamic_slice_in_dim(held, bits[step] * rows, rows, 0)
            away = yield part, move(("section", "dp"), pairs_of(count, step))
            held = (rest.astype(f32) + away.astype(f32)).astype(bf16)
        for step in reversed(range(len(bits))):
            away = yield held, move(("section", "dp"), pairs_of(count, step))
            held = doubled(held, away, step)
        far = yield held, move("section", [(1 - layer, layer)])
        return held, far

    def around(pair):
        return lax.ppermute(pair[0], "dp", ring_up), lax.ppermute(pair[1], "dp", ring_down)

    def spread_steps(piece, route):
        send = move("section", route)

        def both_ways(pair):
            return around(pair) + (send(pair[0]), send(pair[1]))

        def first_way(pair):
            return around(pair) + (send(pair[0]),)

        a, b, far = yield (piece, piece), first_way
        ups, downs, far_ups, far_downs = [piece, a], [b], [far], []
        for _ in range(size // 2 - 2):
            a, b, c, d = yield (ups[-1], downs[-1]), both_ways
            ups.append(a)
            downs.append(b)
            far_ups.append(c)
            far_downs.append(d)
        half = piece.shape[0] // 2
        whole = ups[-1], downs[-1]

        def last_way(pair):
            return around((pair[0][:half], pair[1][half:])) + (send(pair[0]), send(pair[1]))

        a, b, c, d = yield whole, last_way
        far_ups.append(c)
        far_downs.append(d)
        c, d = yield (a, b), lambda pair: (send(pair[0]), send(pair[1]))
        return ups + downs + [a, b], far_ups + far_downs + [c, d]

    def butterfly_steps(part):
        away = yield part, swap_cores
        part = part + away
        distance = 1
        while distance < count:
            away = yield part, move("dp", [(i, i ^ distance) for i in range(count)])
            part = part + away
            distance *= 2
        return part

    mine = (jnp.transpose(w_qkv[0], (1, 0, 2)), w_out[0], w_up[0], w_down[0])
    u0 = across(lax.dynamic_index_in_dim(tokens, sec, 0, False))
    start = series_starts(lax.dynamic_index_in_dim(lengths[0], sec, 0, False), rows)
    norms = jnp.concatenate([norm_gain[0], norm_bias[0]], axis=0)
    swap_norms = to_other_core(norms)
    norm_of = [
        jnp.where(sec == 0, norms, swap_norms),
        jnp.where(sec == 0, swap_norms, norms),
    ]

    spots = jnp.stack([place, sec]).astype(jnp.int32)
    cuts = cut_call(spots, size, mine)

    swapped = tuple(to_other_core(w) for w in mine)
    names = ("qkv", "out", "up", "down")
    mine_of, swapped_of = dict(zip(names, mine)), dict(zip(names, swapped))
    def to_outputs(pair):
        rows_of = [
            lax.dynamic_slice_in_dim(value, tensor * own_rows, own_rows, 0) for value in pair
        ]
        stay = jnp.where(sec == 0, rows_of[0], rows_of[1])
        go = jnp.where(sec == 0, rows_of[1], rows_of[0])
        came = to_other_core(go)
        return jnp.where(sec == 0, jnp.stack([stay, came]), jnp.stack([came, stay]))[None]

    own_weights = [Own(layer, sec, mine_of, swapped_of) for layer in range(2)]
    here = sec.reshape(1)
    gains = [[norm_of[layer][i : i + 1] for i in range(4)] for layer in range(2)]

    both_cores = [(0, 1), (1, 0)]
    sections = ("section", "tensor")
    attention_cut = swap_tensor(cuts[0])
    feed_cut = lax.ppermute(cuts[1], sections, [(0, 1), (1, 0)])
    span = width // size
    came = swap_cores(jnp.concatenate([attention_cut[span:], feed_cut[span:]], axis=0))
    attention_mine = attention_cut[:span]
    piece = jnp.concatenate(
        [
            jnp.where(sec == 0, attention_mine, came[:span]),
            jnp.where(sec == 0, feed_cut[:span], came[span:]),
            jnp.where(sec == 0, came[:span], attention_mine),
        ],
        axis=0,
    )

    def slots_of(arrays, rows, last):
        half = span // 2
        return [((x, rows), (x, rows + half)) for x in arrays[: size - 1]] + [last(arrays[size - 1 :])]

    def pieces_of(gathered, rows, last):
        return Pieces(sec, slot_places, *(slots_of(arrays, rows, last) for arrays in gathered))

    half = span // 2
    gather = Flow(spread_steps(piece, both_cores))
    operand = gather.advance()
    (u0, start), _ = lax.optimization_barrier(((u0, start), operand))
    a0 = first_call(here, own_weights[0], u0, start, gains[0][0], gains[0][2])
    whole_up = lax.ppermute(mine[2], sections, [(2, 3), (3, 2)])
    whole_down = lax.ppermute(mine[3], sections, [(2, 3), (3, 2)])
    together([gather], a0["h"])
    together([gather])
    together([gather])
    operands, (n1_zero, whole_up) = together([gather], a0["n1"], whole_up)
    a0 = dict(a0, n1=n1_zero)
    gathered = finished(gather)
    far_zero = pieces_of(gathered, 0, lambda x: ((x[0], 0), (x[0], half)))
    far_two_zero = pieces_of(gathered, span, lambda x: ((x[0], span), (x[1], 0)))
    far_one = pieces_of(gathered, 2 * span, lambda x: ((x[1], half), (x[1], span)))
    b0 = kernel_after(
        lambda *x: second_call(here, far_zero, *x), [], None,
        a0["n1"], start, a0["h"], gains[0][1], gains[0][3],
    )
    n2_zero, whole_down = lax.optimization_barrier((b0["n2"], whole_down))
    b0 = dict(b0, n2=n2_zero)
    c0 = kernel_after(
        lambda *x: feed_call(here, own_weights[0], far_two_zero, *x), [], None, b0["n2"], b0["h"]
    )
    late, _ = lax.optimization_barrier((lax.dynamic_index_in_dim(cotangent, sec, 0, False), c0["y"]))
    gy1 = across(late)
    a1 = kernel_after(
        lambda *x: first_call(here, own_weights[1], *x), [], None, c0["y"], start, gains[1][0], gains[1][2]
    )
    (whole_up, whole_down), _ = lax.optimization_barrier(((whole_up, whole_down), c0["y"]))
    b1 = kernel_after(
        lambda *x: second_call(here, far_one, *x), [], None,
        a1["n1"], start, a1["h"], gains[1][1], gains[1][3],
    )
    to_first = move("section", [(1, 0)])
    far_two_one = Own(
        1, sec, dict(up=whole_up, down=whole_down), dict(up=to_first(whole_up), down=to_first(whole_down))
    )
    c1 = kernel_after(
        lambda *x: feed_call(here, own_weights[1], far_two_one, *x), [], None, b1["n2"], b1["h"]
    )
    outputs = to_outputs([c0["y"], c1["y"]])

    def feed_back(layer, far_two, moving, last, gy, b, c):
        return kernel_after(
            lambda *x: feed_back_call(here, own_weights[layer], far_two, *x), moving, last,
            gy, c["slope"], c["slope_far"], b["h"], c["z"], b["n2"], gains[layer][1],
        )

    def heads_back(layer, moving, last, a, e):
        return kernel_after(
            lambda *x: heads_back_call(here, own_weights[layer], *x), moving, last,
            a["qkv"], start, e["gh"], a["o"], a["n1"],
        )

    def input_back(layer, far, moving, last, a, b, e, f, u):
        return kernel_after(
            lambda *x: input_back_call(here, own_weights[layer], far, *x), moving, last,
            b["qkv"], start, e["gh"], f["d"], e["dh"], u, gains[layer][0],
        )

    e1 = feed_back(1, far_two_one, [], None, gy1, b1, c1)
    outputs, gh = lax.optimization_barrier((outputs, e1["gh"]))
    e1 = dict(e1, gh=gh)
    sums = [Flow(sum_steps(1, e1["give"], e1["keep"]))]
    f1 = heads_back(1, sums, gh, a1, e1)
    sums.append(Flow(sum_steps(1, f1["give"], f1["keep"])))
    g1 = input_back(1, far_one, sums, f1["d"], a1, b1, e1, f1, c0["y"])
    e0 = feed_back(0, far_two_zero, sums, g1["du"], g1["du"], b0, c0)
    sums.append(Flow(sum_steps(0, e0["give"], e0["keep"])))
    f0 = heads_back(0, sums, e0["gh"], a0, e0)
    sums.append(Flow(sum_steps(0, f0["give"], f0["keep"])))
    g0 = input_back(0, far_zero, sums, f0["d"], a0, b0, e0, f0, u0)
    norm_grads = [
        jnp.concatenate([g["grads"][:1], e["grads"][:1], g["grads"][1:], e["grads"][1:]])
        for g, e in ((g0, e0), (g1, e1))
    ]
    norm_flow = Flow(butterfly_steps(jnp.concatenate(norm_grads, axis=0)))
    norm_flow.advance()
    grads_in = to_outputs([g0["du"], g1["du"]])
    for flow in sums:
        flow.advance(g0["du"])
    (grads_in, results), _ = lax.optimization_barrier(((grads_in, sums[3].results), g0["du"]))
    sums[3].results = results
    while any(not flow.done for flow in sums + [norm_flow]):
        for n in (1, 2, 3):
            if not sums[n].done:
                sums[n].advance()
        together([sums[0], norm_flow])
    parts = [flow.value for flow in sums]
    grad_down, grad_up = final_mlp_call(here, [*parts[2], *parts[0]], width)
    grad_out, grad_qkv = final_attention_call(here, [*parts[3], *parts[1]], width)
    norm_total = norm_flow.value
    norm_sum = jnp.where(sec == 0, norm_total[:4], norm_total[4:])
    norm_sum = lax.dynamic_slice_in_dim(norm_sum, tensor * local, local, 1)

    return (
        outputs,
        grads_in,
        jnp.transpose(grad_qkv, (1, 0, 2))[None],
        grad_out[None],
        grad_up[None],
        grad_down[None],
        norm_sum[None, :2],
        norm_sum[None, 2:],
    )


def solution(mesh):
    in_specs = (
        P(None, ("dp", "tensor"), None),
        P("dp", None, None),
        P("section", None, None, "tensor"),
        P("section", "tensor", None),
        P("section", None, "tensor"),
        P("section", "tensor", None),
        P("section", None, None),
        P("section", None, None),
        P(None, ("dp", "tensor"), None),
    )
    out_specs = (
        P("section", None, ("dp", "tensor"), None),
        P("section", None, ("dp", "tensor"), None),
        P("section", None, None, "tensor"),
        P("section", "tensor", None),
        P("section", None, "tensor"),
        P("section", "tensor", None),
        P("section", None, "tensor"),
        P("section", None, "tensor"),
    )
    return jax.shard_map(
        per_device, mesh=mesh, in_specs=in_specs, out_specs=out_specs, check_vma=False
    )
```

```python
import functools

import jax
import jax.numpy as jnp
import numpy as np
from jax import lax
from jax.experimental import pallas as pl
from jax.experimental.pallas import tpu as pltpu
from jax.sharding import PartitionSpec as P

HEAD_DIM = 128
BAND = 128
EPSILON = 1e-05
MASKED = -1e30
VMEM = 60 * 1024 * 1024
bf16 = jnp.bfloat16
f32 = jnp.float32


def params():
    return pltpu.CompilerParams(vmem_limit_bytes=VMEM)


def cost(flops, moved):
    return pl.CostEstimate(
        flops=int(flops), bytes_accessed=int(moved), transcendentals=0
    )


def dot(a, b):
    return jnp.dot(a, b, preferred_element_type=f32)


def dot_nt(a, b):
    return lax.dot_general(a, b, (((1,), (1,)), ((), ())), preferred_element_type=f32)


def dot_tn(a, b):
    return lax.dot_general(a, b, (((0,), (0,)), ((), ())), preferred_element_type=f32)


def unit_of(values):
    centre = values - jnp.mean(values, axis=-1, keepdims=True)
    spread = jnp.mean(centre * centre, axis=-1, keepdims=True)
    scale = lax.rsqrt(spread + EPSILON)
    return centre * scale, scale


def norm_back(incoming, values, gain):
    unit, scale = unit_of(values)
    scaled = incoming * gain
    inner = (
        scaled
        - jnp.mean(scaled, axis=-1, keepdims=True)
        - unit * jnp.mean(scaled * unit, axis=-1, keepdims=True)
    )
    grads = jnp.concatenate(
        [
            jnp.sum(incoming * unit, axis=0, keepdims=True),
            jnp.sum(incoming, axis=0, keepdims=True),
        ],
        axis=0,
    )
    return scale * inner, grads


def any_specs(n):
    return [pl.BlockSpec(memory_space=pl.ANY)] * n


class Own:
    def __init__(self, layer, sec, mine, swapped):
        self.scalars = jnp.stack([sec, jnp.full_like(sec, layer)])
        self.mine, self.swapped = mine, swapped

    def operands(self, names):
        return [self.mine[n] for n in names] + [self.swapped[n] for n in names]

    def start(self, names, scalars, refs, targets, sems):
        mine, swapped = refs[: len(names)], refs[len(names) :]
        for condition, side in ((True, mine), (False, swapped)):

            @pl.when((scalars[0] == scalars[1]) == condition)
            def _():
                for n, (ref, target) in enumerate(zip(side, targets)):
                    pltpu.make_async_copy(ref, target, sems.at[n, 0]).start()

    def wait(self, n, name, target, sems):
        pltpu.make_async_copy(target, target, sems.at[n, 0]).wait()


class Pieces:
    def __init__(self, sec, places, own, far):
        self.count = len(own)
        self.scalars = jnp.concatenate([sec.reshape(1), places])
        self.arrays, self.index = [], []
        for side in (own, far):
            rows = []
            for slot in side:
                parts = []
                for array, row in slot:
                    known = [n for n, x in enumerate(self.arrays) if x is array]
                    if not known:
                        self.arrays.append(array)
                        known = [len(self.arrays) - 1]
                    parts.append((known[0], row))
                rows.append(parts)
            self.index.append(rows)

    def operands(self, names):
        return self.arrays

    def start(self, names, scalars, refs, targets, sems):
        every = slice(None)
        for side, slots in enumerate(self.index):
            core = lax.rem(scalars[0] + side, 2)
            for slot, ((n0, row0), (n1, row1)) in enumerate(slots):
                spot = scalars[1 + slot] * 2 + core
                first, second = refs[n0], refs[n1]
                for n, (name, target) in enumerate(zip(names, targets)):

                    def put(source, place):
                        pltpu.make_async_copy(source, place, sems.at[n, side]).start()

                    if name == "qkv":
                        deep, local = target.shape[1], target.shape[2]
                        fine = deep // self.count // 2
                        half = fine // 2
                        row = spot * fine
                        for j in range(2):
                            columns = slice(j * local, (j + 1) * local)
                            put(
                                first.at[row0 : row0 + fine, columns],
                                target.at[j, pl.ds(row, fine), :],
                            )
                            put(
                                second.at[row1 : row1 + half, columns],
                                target.at[2, pl.ds(row + j * half, half), :],
                            )
                    elif name == "out":
                        fine = target.shape[0] // self.count // 2
                        put(
                            second.at[row1 + fine : row1 + 2 * fine, every],
                            target.at[pl.ds(spot * fine, fine), :],
                        )
                    else:
                        fine = target.shape[0] // self.count // 2
                        source = second.at[row1 : row1 + fine, every] if name == "down" else first.at[row0 : row0 + fine, every]
                        put(source, target.at[pl.ds(spot * fine, fine), :])

    def wait(self, n, name, target, sems):
        for side in range(2):
            if name == "qkv":
                part = target.at[:, : target.shape[1] // 2, :]
            else:
                part = target.at[: target.shape[0] // 2, :]
            pltpu.make_async_copy(part, part, sems.at[n, side]).wait()


def struct(shape, dtype):
    return jax.ShapeDtypeStruct(shape, dtype)


class Room:
    def __init__(self, refs, sources, sinks, in_sems, out_sems, weights):
        self.refs, self.sources, self.sinks = refs, sources, sinks
        self.in_sems, self.out_sems, self.weights = in_sems, out_sems, weights
        self.waited, self.leaving = set(), []

    def start(self, names):
        for n, name in enumerate(names):
            pltpu.make_async_copy(self.sources[name], self.refs[name], self.in_sems.at[n]).start()
        self.order = list(names)

    def get(self, name):
        if name in self.sources and name not in self.waited:
            self.waited.add(name)
            ref = self.refs[name]
            pltpu.make_async_copy(ref, ref, self.in_sems.at[self.order.index(name)]).wait()
        return self.refs[name]

    def weight(self, name):
        loader, place, kind, target, sems = self.weights[name]
        if name not in self.waited:
            self.waited.add(name)
            loader.wait(place, kind, target, sems)
        return target

    def send(self, pairs):
        for source, sink in pairs:
            copy = pltpu.make_async_copy(source, sink, self.out_sems.at[len(self.leaving)])
            copy.start()
            self.leaving.append(copy)

    def flush(self, *names):
        self.send([(self.refs[name], self.sinks[name]) for name in names])

    def close(self):
        for copy in self.leaving:
            copy.wait()


def room_call(name, body, scalars, weights, inputs, outputs, scratch, copies, flops):
    in_names, out_names, temp_names = list(inputs), list(outputs), list(scratch)
    operands = [loader.operands([k for k, _ in kinds]) for _, loader, kinds in weights]
    scalar_list = [scalars] + [loader.scalars for _, loader, _ in weights]
    local_out = [n for n in out_names if n not in scratch]

    def whole(*refs):
        refs = list(refs)

        def take(n):
            got = refs[:n]
            del refs[:n]
            return got

        scalar_refs = take(len(scalar_list))
        sources = dict(zip(in_names, take(len(in_names))))
        weight_sources = [take(len(o)) for o in operands]
        sinks = dict(zip(out_names, take(len(out_names))))
        held = dict(zip(in_names, take(len(in_names))))
        held.update(zip(local_out, take(len(local_out))))
        held.update(zip(temp_names, take(len(temp_names))))
        in_sems, out_sems = take(2)
        table = {}
        starts = []
        for (prefix, loader, kinds), source, scalar in zip(weights, weight_sources, scalar_refs[1:]):
            targets = take(len(kinds))
            sems = take(1)[0]
            starts.append((loader, [k for k, _ in kinds], scalar, source, targets, sems))
            for place, (kind, _) in enumerate(kinds):
                table[prefix + kind] = (loader, place, kind, targets[place], sems)
        room = Room(held, sources, sinks, in_sems, out_sems, table)
        room.start(in_names)
        for loader, kinds, scalar, source, targets, sems in starts:
            loader.start(kinds, scalar, source, targets, sems)
        body(room, scalar_refs[0])
        for name in in_names:
            room.get(name)
        for key in table:
            room.weight(key)
        room.close()

    vmem = [pltpu.VMEM(inputs[n].shape, inputs[n].dtype) for n in in_names]
    vmem += [pltpu.VMEM(outputs[n].shape, outputs[n].dtype) for n in local_out]
    vmem += [pltpu.VMEM(*scratch[n]) for n in temp_names]
    vmem += [pltpu.SemaphoreType.DMA((max(len(in_names), 1),)), pltpu.SemaphoreType.DMA((copies,))]
    for _, _, kinds in weights:
        vmem += [pltpu.VMEM(shape, bf16) for _, shape in kinds]
        vmem.append(pltpu.SemaphoreType.DMA((len(kinds), 2)))
    flat = [x for o in operands for x in o]
    moved = sum(x.size * x.dtype.itemsize for x in list(inputs.values()) + list(outputs.values()))
    moved += sum(2 * int(np.prod(shape)) for _, _, kinds in weights for _, shape in kinds)
    result = pl.pallas_call(
        whole,
        in_specs=[pl.BlockSpec(memory_space=pltpu.SMEM)] * len(scalar_list)
        + any_specs(len(in_names) + len(flat)),
        out_specs=any_specs(len(out_names)),
        out_shape=[outputs[n] for n in out_names],
        scratch_shapes=vmem,
        compiler_params=params(),
        cost_estimate=cost(flops, moved),
        name=name,
    )(*scalar_list, *inputs.values(), *flat)
    return dict(zip(out_names, result))


def band_probs(q, k, start_ref, block):
    low = max(block - 1, 0) * BAND
    high = (block + 1) * BAND
    scores = dot_nt(q[block * BAND : high], k[low:high]) * HEAD_DIM**-0.5
    row = lax.broadcasted_iota(jnp.int32, scores.shape, 0) + block * BAND
    column = lax.broadcasted_iota(jnp.int32, scores.shape, 1) + low
    first = start_ref[block * BAND : high, :]
    allowed = (column <= row) & (column >= first)
    scores = jnp.where(allowed, scores, MASKED)
    expo = jnp.exp(scores - jnp.max(scores, axis=-1, keepdims=True))
    return expo / jnp.sum(expo, axis=-1, keepdims=True), low, high


def heads_of(qkv_ref, head, local):
    return [
        qkv_ref[:, j * local + head * HEAD_DIM : j * local + (head + 1) * HEAD_DIM] for j in range(3)
    ]


def attend(qkv_ref, start_ref, o_ref):
    rows, local = o_ref.shape
    for head in range(local // HEAD_DIM):
        cut = slice(head * HEAD_DIM, (head + 1) * HEAD_DIM)
        q, k, v = heads_of(qkv_ref, head, local)
        for block in range(rows // BAND):
            probs, low, high = band_probs(q, k, start_ref, block)
            o_ref[block * BAND : high, cut] = dot(probs.astype(bf16), v[low:high]).astype(bf16)


def project(left, w, out_ref):
    local = w.shape[2]
    for j in range(3):
        out_ref[:, j * local : (j + 1) * local] = dot(left[...], w[j]).astype(bf16)


def activate(n2_ref, up, z_ref, slope_ref):
    c = np.float32(np.sqrt(2 / np.pi))
    tile = 512
    for i in range(z_ref.shape[1] // tile):
        cut = slice(i * tile, (i + 1) * tile)
        a = dot(n2_ref[...], up[:, cut])
        square = a * a
        t = jnp.tanh(c * a * (1.0 + 0.044715 * square))
        half = 0.5 * (1.0 + t)
        slope = half + 0.5 * c * a * (1.0 - t * t) * (1.0 + 3 * 0.044715 * square)
        z_ref[:, cut] = (a * half).astype(bf16)
        slope_ref[:, cut] = slope.astype(bf16)


def sizes(width):
    local, units = width // 2, width
    return {
        "qkv": (3, width, local),
        "out": (local, width),
        "up": (width, units),
        "down": (units, width),
    }


def group(prefix, loader, kinds, width):
    return prefix, loader, [(k, sizes(width)[k]) for k in kinds]


def first_call(scalars, own, u, start, gain, bias):
    rows, width = u.shape
    local = width // 2

    def body(room, _):
        u_ref = room.get("u")
        unit, _ = unit_of(u_ref[...].astype(f32))
        n1 = room.get("n1")
        n1[...] = (unit * room.get("gain")[...] + room.get("bias")[...]).astype(bf16)
        project(n1, room.weight("own_qkv"), room.get("qkv"))
        room.flush("n1", "qkv")
        attend(room.get("qkv"), room.get("start"), room.get("o"))
        room.flush("o")
        room.get("h")[...] = u_ref[...].astype(f32) + dot(room.get("o")[...], room.weight("own_out")[...])
        room.flush("h")

    return room_call(
        "first", body, scalars, [group("own_", own, ["qkv", "out"], width)],
        dict(u=u, start=start, gain=gain, bias=bias),
        dict(n1=struct((rows, width), bf16), qkv=struct((rows, 3 * local), bf16),
             o=struct((rows, local), bf16), h=struct((rows, width), f32)),
        {}, 4, 9 * rows * width * local,
    )


def second_call(scalars, far, n1, start, base, gain, bias):
    rows, width = base.shape
    local = width // 2

    def body(room, _):
        project(room.get("n1"), room.weight("far_qkv"), room.get("qkv"))
        room.flush("qkv")
        attend(room.get("qkv"), room.get("start"), room.get("o"))
        h = room.get("base")[...] + dot(room.get("o")[...], room.weight("far_out")[...])
        room.get("h")[...] = h
        unit, _ = unit_of(h)
        n2 = room.get("n2")
        n2[...] = (unit * room.get("gain")[...] + room.get("bias")[...]).astype(bf16)
        room.flush("h", "n2")

    return room_call(
        "second", body, scalars, [group("far_", far, ["qkv", "out"], width)],
        dict(n1=n1, start=start, base=base, gain=gain, bias=bias),
        dict(qkv=struct((rows, 3 * local), bf16), h=struct((rows, width), f32),
             n2=struct((rows, width), bf16)),
        dict(o=((rows, local), bf16)), 3, 9 * rows * width * local,
    )


def feed_call(scalars, own, far_two, n2, h):
    rows, width = h.shape
    units = width

    def body(room, _):
        n2 = room.get("n2")
        activate(n2, room.weight("own_up"), room.get("z"), room.get("slope"))
        room.flush("z", "slope")
        activate(n2, room.weight("two_up"), room.get("z_far"), room.get("slope_far"))
        room.flush("slope_far")
        y = room.get("h")[...] + dot(room.get("z")[...], room.weight("own_down")[...])
        room.get("y")[...] = (y + dot(room.get("z_far")[...], room.weight("two_down")[...])).astype(bf16)
        room.flush("y")

    tall = struct((rows, width), bf16)
    return room_call(
        "feed", body, scalars,
        [group("own_", own, ["up", "down"], width), group("two_", far_two, ["up", "down"], width)],
        dict(n2=n2, h=h), dict(z=tall, slope=tall, slope_far=tall, y=tall),
        dict(z_far=((rows, units), bf16)), 4, 8 * rows * width * units,
    )


def feed_back_call(scalars, own, far_two, gy, slope, slope_far, h, z, n2, gain):
    rows, width = gy.shape
    units = width
    half = units // 2

    def body(room, scalar):
        gy_ref = room.get("gy")
        dz = dot_nt(gy_ref[...], room.weight("own_down")[...])
        da = room.get("da")
        da[...] = (dz * room.get("slope")[...].astype(f32)).astype(bf16)
        down, up = room.get("grad_down"), room.get("grad_up")
        down[...] = dot_tn(room.get("z")[...], gy_ref[...]).astype(bf16)
        up[...] = dot_tn(room.get("n2")[...], da[...]).astype(bf16)
        for name, which in (("give", 1 - scalar[0]), ("keep", scalar[0])):
            at = pl.multiple_of(which * half, half)
            sink = room.sinks[name]
            room.send([(down.at[pl.ds(at, half), :], sink.at[:half, :])])
            room.send([(up.at[pl.ds(at, half), :], sink.at[half:, :])])
        term = dot_nt(da[...], room.weight("own_up")[...])
        dz = dot_nt(gy_ref[...], room.weight("two_down")[...])
        da = (dz * room.get("slope_far")[...].astype(f32)).astype(bf16)
        term = term + dot_nt(da, room.weight("two_up")[...])
        back, grads = norm_back(term, room.get("h")[...], room.get("gain")[...])
        dh = gy_ref[...].astype(f32) + back
        room.get("dh")[...] = dh
        room.get("gh")[...] = dh.astype(bf16)
        room.get("grads")[...] = grads
        room.flush("dh", "gh", "grads")

    part = struct((2 * half, width), bf16)
    tall = ((rows, width), bf16)
    return room_call(
        "feed_back", body, scalars,
        [group("own_", own, ["down", "up"], width), group("two_", far_two, ["down", "up"], width)],
        dict(gy=gy, slope=slope, z=z, n2=n2, slope_far=slope_far, h=h, gain=gain),
        dict(give=part, keep=part, dh=struct((rows, width), f32), gh=struct((rows, width), bf16),
             grads=struct((2, width), f32)),
        dict(da=tall, grad_down=((units, width), bf16), grad_up=((width, units), bf16),
             give=((16, 128), bf16), keep=((16, 128), bf16)),
        7, 12 * rows * width * units,
    )


def attend_back(qkv_ref, start_ref, do_all, out):
    rows, local = do_all.shape
    blocks = rows // BAND
    for head in range(local // HEAD_DIM):
        q, k, v = heads_of(qkv_ref, head, local)
        do = do_all[:, head * HEAD_DIM : (head + 1) * HEAD_DIM]
        columns = [
            slice(j * local + head * HEAD_DIM, j * local + (head + 1) * HEAD_DIM) for j in range(3)
        ]
        dk_parts, dv_parts = [None] * blocks, [None] * blocks

        def put(parts, term, low):
            for piece in range(term.shape[0] // BAND):
                place = low // BAND + piece
                add = term[piece * BAND : (piece + 1) * BAND]
                parts[place] = add if parts[place] is None else parts[place] + add

        for block in range(blocks):
            probs, low, high = band_probs(q, k, start_ref, block)
            here = slice(block * BAND, high)
            dp = dot_nt(do[here], v[low:high])
            inner = jnp.sum(probs * dp, axis=-1, keepdims=True)
            ds = (probs * (dp - inner) * HEAD_DIM**-0.5).astype(bf16)
            out[here, columns[0]] = dot(ds, k[low:high]).astype(bf16)
            put(dk_parts, dot_tn(ds, q[here]), low)
            put(dv_parts, dot_tn(probs.astype(bf16), do[here]), low)
        for block in range(blocks):
            here = slice(block * BAND, (block + 1) * BAND)
            out[here, columns[1]] = dk_parts[block].astype(bf16)
            out[here, columns[2]] = dv_parts[block].astype(bf16)


def heads_back_call(scalars, own, qkv, start, gh, o, n1):
    rows, width = gh.shape
    local = width // 2
    first, deep = local // 2, width // 4

    def body(room, scalar):
        gh_ref = room.get("gh")
        do_all = dot_nt(gh_ref[...], room.weight("own_out")[...]).astype(bf16)
        d = room.get("d")
        attend_back(room.get("qkv"), room.get("start"), do_all, d)
        room.flush("d")
        grad_out, grad_qkv = room.get("grad_out"), room.get("grad_qkv")
        grad_out[...] = dot_tn(room.get("o")[...], gh_ref[...]).astype(bf16)
        grad_qkv[...] = dot_tn(room.get("n1")[...], d[...]).astype(bf16)
        for name, which in (("give", 1 - scalar[0]), ("keep", scalar[0])):
            sink = room.sinks[name]
            at = pl.multiple_of(which * first, first)
            room.send([(grad_out.at[pl.ds(at, first), :], sink.at[:first, :])])
            for side in range(2):
                at = pl.multiple_of((which * 2 + side) * deep, deep)
                for j in range(3):
                    room.send([(
                        grad_qkv.at[pl.ds(at, deep), j * local : (j + 1) * local],
                        sink.at[
                            first + j * deep : first + (j + 1) * deep,
                            side * local : (side + 1) * local,
                        ],
                    )])

    part = struct((first + 3 * deep, width), bf16)
    return room_call(
        "heads_back", body, scalars, [group("own_", own, ["out"], width)],
        dict(gh=gh, qkv=qkv, start=start, o=o, n1=n1),
        dict(give=part, keep=part, d=struct((rows, 3 * local), bf16)),
        dict(grad_out=((local, width), bf16), grad_qkv=((width, 3 * local), bf16),
             give=((16, 128), bf16), keep=((16, 128), bf16)),
        15, 17 * rows * width * local,
    )


def input_back_call(scalars, own, far, qkv_far, start, gh, d, dh, u, gain):
    rows, width = gh.shape
    local = width // 2

    def body(room, _):
        do_all = dot_nt(room.get("gh")[...], room.weight("far_out")[...]).astype(bf16)
        d_far = room.get("d_far")
        attend_back(room.get("qkv"), room.get("start"), do_all, d_far)
        term = None
        for ref, w in ((room.get("d"), room.weight("own_qkv")), (d_far, room.weight("far_qkv"))):
            for j in range(3):
                part = dot_nt(ref[:, j * local : (j + 1) * local], w[j])
                term = part if term is None else term + part
        back, grads = norm_back(term, room.get("u")[...].astype(f32), room.get("gain")[...])
        room.get("du")[...] = (room.get("dh")[...] + back).astype(bf16)
        room.get("grads")[...] = grads
        room.flush("du", "grads")

    return room_call(
        "input_back", body, scalars,
        [group("far_", far, ["out", "qkv"], width), group("own_", own, ["qkv"], width)],
        dict(gh=gh, qkv=qkv_far, start=start, d=d, u=u, gain=gain, dh=dh),
        dict(du=struct((rows, width), bf16), grads=struct((2, width), f32)),
        dict(d_far=((rows, 3 * local), bf16)), 2, 21 * rows * width * local,
    )


def ring_walk(size):
    return list(range(0, size, 2)) + list(range(1, size, 2))[::-1]


def ring_routes(count, size):
    walk = ring_walk(size)
    up = []
    for base in range(0, count, size):
        for place in range(size):
            up.append((base + walk[place], base + walk[(place + 1) % size]))
    return up, [(b, a) for a, b in up]


def slot_steps(size):
    return list(range(0, -size // 2, -1)) + list(range(1, size // 2)) + [size // 2]


def halving_order(count):
    bits = count.bit_length() - 1
    first = list(range(bits))
    second = [1, 0] + first[2:] if bits > 1 else first
    return first, second


def pairs_of(count, step):
    routes = []
    for core, order in enumerate(halving_order(count)):
        for i in range(count):
            routes.append((core * count + i, core * count + (i ^ (1 << order[step]))))
    return routes


def own_bits(sec, rank, count):
    first, second = halving_order(count)
    return [
        lax.rem(rank >> jnp.where(sec == 0, a, b), 2) for a, b in zip(first, second)
    ]


class Flow:
    def __init__(self, steps):
        self.steps, self.results, self.value, self.done = steps, None, None, False

    def advance(self, after=None):
        if after is not None and self.results is not None:
            self.results, _ = lax.optimization_barrier((self.results, after))
        try:
            operands, send = self.steps.send(self.results)
        except StopIteration as stop:
            self.value, self.done = stop.value, True
            return ()
        self.results = send(operands)
        return operands


def finished(flow):
    while not flow.done:
        flow.advance()
    return flow.value


def together(flows, *others):
    moving = [flow for flow in flows if not flow.done]
    results, others = lax.optimization_barrier(([flow.results for flow in moving], others))
    for flow, result in zip(moving, results):
        flow.results = result
    return [flow.advance() for flow in moving], others


def kernel_after(kernel, moving, last, *inputs):
    operands = [flow.advance(last) for flow in moving if not flow.done]
    inputs, _ = lax.optimization_barrier((inputs, operands))
    return kernel(*inputs)


def cut_body(count, spots, qkv, out, up, down, attention, feed, sems):
    width = up.shape[0]
    local = qkv.shape[2]
    place, sec = spots[0], spots[1]
    fine = width // count // 2
    half = fine // 2
    for which in range(2):
        core = sec if which == 0 else 1 - sec
        row = (place * 2 + core) * fine
        base = which * 2 * fine

        def put(n, source, target):
            pltpu.make_async_copy(source, target, sems.at[n]).start()

        mid = base + fine
        put(0, qkv.at[0, pl.ds(row, fine), :], attention.at[base:mid, :local])
        put(0, qkv.at[1, pl.ds(row, fine), :], attention.at[base:mid, local:])
        put(0, qkv.at[2, pl.ds(row, half), :], attention.at[mid : mid + half, :local])
        put(0, qkv.at[2, pl.ds(row + half, half), :], attention.at[mid : mid + half, local:])
        put(0, out.at[pl.ds((place * 2 + core) * half, half), :], attention.at[mid + half : mid + fine, :])
        put(1, up.at[pl.ds(row, fine), :], feed.at[base:mid, :])
        put(1, down.at[pl.ds(row, fine), :], feed.at[mid : mid + fine, :])
    pltpu.make_async_copy(attention, attention, sems.at[0]).wait()
    pltpu.make_async_copy(feed, feed, sems.at[1]).wait()


def cut_call(spots, count, mine):
    width = mine[2].shape[0]
    shapes = [struct((2 * width // count, width), bf16)] * 2
    return pl.pallas_call(
        functools.partial(cut_body, count),
        grid=(1,),
        in_specs=[pl.BlockSpec(memory_space=pltpu.SMEM)] + any_specs(4),
        out_specs=[pl.BlockSpec(x.shape, lambda i: (0, 0)) for x in shapes],
        out_shape=shapes,
        scratch_shapes=[pltpu.SemaphoreType.DMA((2,))],
        compiler_params=params(),
        cost_estimate=cost(0, 4 * width * width),
        name="cut",
    )(spots, *mine)


def final_call(name, body, scalars, sums, outputs):
    whole, width = sums[0].shape

    def kernel(scalar_ref, own0, far0, own1, far1, *refs):
        refs = list(refs)
        sinks = refs[: len(outputs)]
        held, sems, out_sems, *wide = refs[len(outputs) :]
        sec = scalar_ref[0]
        for layer, sides in enumerate(((own0, far0), (own1, far1))):

            @pl.when(sec == layer)
            def _():
                for side, ref in enumerate(sides):
                    pltpu.make_async_copy(ref, held.at[side], sems.at[side]).start()

        leaving = []
        for side in range(2):
            pltpu.make_async_copy(held.at[side], held.at[side], sems.at[side]).wait()
            for source, sink in body(held, side, lax.rem(sec + side, 2), wide, sinks):
                copy = pltpu.make_async_copy(source, sink, out_sems.at[len(leaving)])
                copy.start()
                leaving.append(copy)
        for copy in leaving:
            copy.wait()

    return pl.pallas_call(
        kernel,
        in_specs=[pl.BlockSpec(memory_space=pltpu.SMEM)] + any_specs(4),
        out_specs=any_specs(len(outputs)),
        out_shape=outputs,
        scratch_shapes=[
            pltpu.VMEM((2, whole, width), bf16),
            pltpu.SemaphoreType.DMA((2,)),
            pltpu.SemaphoreType.DMA((16,)),
        ]
        + [pltpu.VMEM((2,) + x.shape[:-2] + (x.shape[-2] // 2, x.shape[-1]), f32) for x in outputs],
        compiler_params=params(),
        cost_estimate=cost(0, 12 * whole * width),
        name=name,
    )(scalars, *sums)


def final_mlp_call(scalars, sums, width):
    half = width // 2

    def body(held, side, core, wide, sinks):
        at = pl.multiple_of(core * half, half)
        for n in range(2):
            wide[n][side] = held[side, n * half : (n + 1) * half, :].astype(f32)
            yield wide[n].at[side], sinks[n].at[pl.ds(at, half), :]

    return final_call("final_mlp", body, scalars, sums, [struct((width, width), f32)] * 2)


def final_attention_call(scalars, sums, width):
    local = width // 2
    first, deep = local // 2, width // 4

    def body(held, side, core, wide, sinks):
        wide[0][side] = held[side, :first, :].astype(f32)
        yield wide[0].at[side], sinks[0].at[pl.ds(pl.multiple_of(core * first, first), first), :]
        low = pl.multiple_of(core * 2 * deep, 2 * deep)
        for j in range(3):
            block = held[side, first + j * deep : first + (j + 1) * deep, :].astype(f32)
            wide[1][side, j, :deep, :] = block[:, :local]
            wide[1][side, j, deep:, :] = block[:, local:]
            yield wide[1].at[side, j], sinks[1].at[j, pl.ds(low, 2 * deep), :]

    return final_call(
        "final_attention", body, scalars, sums,
        [struct((local, width), f32), struct((3, width, local), f32)],
    )


def series_starts(lengths, rows):
    ends = jnp.cumsum(lengths)
    places = jnp.arange(rows, dtype=jnp.int32)
    passed = jnp.where(ends[None, :] <= places[:, None], ends[None, :], 0)
    return jnp.max(passed, axis=1, keepdims=True).astype(jnp.int32)


def per_device(tokens, lengths, w_qkv, w_out, w_up, w_down, norm_gain, norm_bias, cotangent):
    sec = lax.axis_index("section").astype(jnp.int32)
    tensor = lax.axis_index("tensor")
    rank = lax.axis_index("dp")
    count = lax.axis_size("dp")
    own_rows = tokens.shape[1]
    rows = 2 * own_rows
    width = tokens.shape[2]
    local = width // 2
    swap = [(0, 1), (1, 0)]
    bits = own_bits(sec, rank, count)
    fan = min(3, len(bits))
    size = 1 << fan
    ring_up, ring_down = ring_routes(count, size)
    in_ring = lax.rem(rank, size)
    place = jnp.where(lax.rem(in_ring, 2) == 0, in_ring // 2, size - 1 - in_ring // 2)
    slot_places = lax.rem(place + np.asarray(slot_steps(size), np.int32) + size, size).astype(jnp.int32)

    def across(shard):
        other = lax.ppermute(shard, "tensor", swap)
        return jnp.where(
            tensor == 0,
            jnp.concatenate([shard, other], axis=0),
            jnp.concatenate([other, shard], axis=0),
        )

    def to_other_core(value):
        return lax.ppermute(value, "section", swap)

    def swap_cores(value):
        return lax.ppermute(value, "section", swap)

    def swap_tensor(value):
        return lax.ppermute(value, "tensor", swap)

    def move(axis, route):
        return lambda value: lax.ppermute(value, axis, route)

    def doubled(held, away, step):
        low = bits[step] == 0
        return jnp.concatenate([jnp.where(low, held, away), jnp.where(low, away, held)], axis=0)

    def sum_steps(layer, send, kept):
        received = yield send, swap_cores
        rows = kept.shape[0] // 2

        def both(side):
            a = lax.dynamic_slice_in_dim(kept, side * rows, rows, 0).astype(f32)
            b = lax.dynamic_slice_in_dim(received, side * rows, rows, 0).astype(f32)
            return a + b

        away = yield both(1 - bits[0]).astype(bf16), move(("section", "dp"), pairs_of(count, 0))
        held = (both(bits[0]) + away.astype(f32)).astype(bf16)
        for step in range(1, len(bits)):
            rows //= 2
            part = lax.dynamic_slice_in_dim(held, (1 - bits[step]) * rows, rows, 0)
            rest = lax.dynamic_slice_in_dim(held, bits[step] * rows, rows, 0)
            away = yield part, move(("section", "dp"), pairs_of(count, step))
            held = (rest.astype(f32) + away.astype(f32)).astype(bf16)
        for step in reversed(range(len(bits))):
            away = yield held, move(("section", "dp"), pairs_of(count, step))
            held = doubled(held, away, step)
        far = yield held, move("section", [(1 - layer, layer)])
        return held, far

    def around(pair):
        return lax.ppermute(pair[0], "dp", ring_up), lax.ppermute(pair[1], "dp", ring_down)

    def spread_steps(piece, route):
        send = move("section", route)

        def both_ways(pair):
            return around(pair) + (send(pair[0]), send(pair[1]))

        def first_way(pair):
            return around(pair) + (send(pair[0]),)

        a, b, far = yield (piece, piece), first_way
        ups, downs, far_ups, far_downs = [piece, a], [b], [far], []
        for _ in range(size // 2 - 2):
            a, b, c, d = yield (ups[-1], downs[-1]), both_ways
            ups.append(a)
            downs.append(b)
            far_ups.append(c)
            far_downs.append(d)
        half = piece.shape[0] // 2
        whole = ups[-1], downs[-1]

        def last_way(pair):
            return around((pair[0][:half], pair[1][half:])) + (send(pair[0]), send(pair[1]))

        a, b, c, d = yield whole, last_way
        far_ups.append(c)
        far_downs.append(d)
        c, d = yield (a, b), lambda pair: (send(pair[0]), send(pair[1]))
        return ups + downs + [a, b], far_ups + far_downs + [c, d]

    def butterfly_steps(part):
        away = yield part, swap_cores
        part = part + away
        distance = 1
        while distance < count:
            away = yield part, move("dp", [(i, i ^ distance) for i in range(count)])
            part = part + away
            distance *= 2
        return part

    mine = (jnp.transpose(w_qkv[0], (1, 0, 2)), w_out[0], w_up[0], w_down[0])
    u0 = across(lax.dynamic_index_in_dim(tokens, sec, 0, False))
    start = series_starts(lax.dynamic_index_in_dim(lengths[0], sec, 0, False), rows)
    norms = jnp.concatenate([norm_gain[0], norm_bias[0]], axis=0)
    swap_norms = to_other_core(norms)
    norm_of = [
        jnp.where(sec == 0, norms, swap_norms),
        jnp.where(sec == 0, swap_norms, norms),
    ]

    spots = jnp.stack([place, sec]).astype(jnp.int32)
    cuts = cut_call(spots, size, mine)

    swapped = tuple(to_other_core(w) for w in mine)
    names = ("qkv", "out", "up", "down")
    mine_of, swapped_of = dict(zip(names, mine)), dict(zip(names, swapped))
    def to_outputs(pair):
        rows_of = [
            lax.dynamic_slice_in_dim(value, tensor * own_rows, own_rows, 0) for value in pair
        ]
        stay = jnp.where(sec == 0, rows_of[0], rows_of[1])
        go = jnp.where(sec == 0, rows_of[1], rows_of[0])
        came = to_other_core(go)
        return jnp.where(sec == 0, jnp.stack([stay, came]), jnp.stack([came, stay]))[None]

    own_weights = [Own(layer, sec, mine_of, swapped_of) for layer in range(2)]
    here = sec.reshape(1)
    gains = [[norm_of[layer][i : i + 1] for i in range(4)] for layer in range(2)]

    both_cores = [(0, 1), (1, 0)]
    sections = ("section", "tensor")
    attention_cut = swap_tensor(cuts[0])
    feed_cut = lax.ppermute(cuts[1], sections, [(0, 1), (1, 0)])
    span = width // size
    came = swap_cores(jnp.concatenate([attention_cut[span:], feed_cut[span:]], axis=0))
    attention_mine = attention_cut[:span]
    piece = jnp.concatenate(
        [
            jnp.where(sec == 0, attention_mine, came[:span]),
            jnp.where(sec == 0, feed_cut[:span], came[span:]),
            jnp.where(sec == 0, came[:span], attention_mine),
        ],
        axis=0,
    )

    def slots_of(arrays, rows, last):
        half = span // 2
        return [((x, rows), (x, rows + half)) for x in arrays[: size - 1]] + [last(arrays[size - 1 :])]

    def pieces_of(gathered, rows, last):
        return Pieces(sec, slot_places, *(slots_of(arrays, rows, last) for arrays in gathered))

    half = span // 2
    gather = Flow(spread_steps(piece, both_cores))
    operand = gather.advance()
    (u0, start), _ = lax.optimization_barrier(((u0, start), operand))
    a0 = first_call(here, own_weights[0], u0, start, gains[0][0], gains[0][2])
    whole_up = lax.ppermute(mine[2], sections, [(2, 3), (3, 2)])
    whole_down = lax.ppermute(mine[3], sections, [(2, 3), (3, 2)])
    together([gather], a0["h"])
    together([gather])
    together([gather])
    operands, (n1_zero, whole_up) = together([gather], a0["n1"], whole_up)
    a0 = dict(a0, n1=n1_zero)
    gathered = finished(gather)
    far_zero = pieces_of(gathered, 0, lambda x: ((x[0], 0), (x[0], half)))
    far_two_zero = pieces_of(gathered, span, lambda x: ((x[0], span), (x[1], 0)))
    far_one = pieces_of(gathered, 2 * span, lambda x: ((x[1], half), (x[1], span)))
    b0 = kernel_after(
        lambda *x: second_call(here, far_zero, *x), [], None,
        a0["n1"], start, a0["h"], gains[0][1], gains[0][3],
    )
    n2_zero, whole_down = lax.optimization_barrier((b0["n2"], whole_down))
    b0 = dict(b0, n2=n2_zero)
    c0 = kernel_after(
        lambda *x: feed_call(here, own_weights[0], far_two_zero, *x), [], None, b0["n2"], b0["h"]
    )
    late, _ = lax.optimization_barrier((lax.dynamic_index_in_dim(cotangent, sec, 0, False), c0["y"]))
    gy1 = across(late)
    a1 = kernel_after(
        lambda *x: first_call(here, own_weights[1], *x), [], None, c0["y"], start, gains[1][0], gains[1][2]
    )
    (whole_up, whole_down), _ = lax.optimization_barrier(((whole_up, whole_down), c0["y"]))
    b1 = kernel_after(
        lambda *x: second_call(here, far_one, *x), [], None,
        a1["n1"], start, a1["h"], gains[1][1], gains[1][3],
    )
    to_first = move("section", [(1, 0)])
    far_two_one = Own(
        1, sec, dict(up=whole_up, down=whole_down), dict(up=to_first(whole_up), down=to_first(whole_down))
    )
    c1 = kernel_after(
        lambda *x: feed_call(here, own_weights[1], far_two_one, *x), [], None, b1["n2"], b1["h"]
    )
    outputs = to_outputs([c0["y"], c1["y"]])

    def feed_back(layer, far_two, moving, last, gy, b, c):
        return kernel_after(
            lambda *x: feed_back_call(here, own_weights[layer], far_two, *x), moving, last,
            gy, c["slope"], c["slope_far"], b["h"], c["z"], b["n2"], gains[layer][1],
        )

    def heads_back(layer, moving, last, a, e):
        return kernel_after(
            lambda *x: heads_back_call(here, own_weights[layer], *x), moving, last,
            a["qkv"], start, e["gh"], a["o"], a["n1"],
        )

    def input_back(layer, far, moving, last, a, b, e, f, u):
        return kernel_after(
            lambda *x: input_back_call(here, own_weights[layer], far, *x), moving, last,
            b["qkv"], start, e["gh"], f["d"], e["dh"], u, gains[layer][0],
        )

    e1 = feed_back(1, far_two_one, [], None, gy1, b1, c1)
    outputs, gh = lax.optimization_barrier((outputs, e1["gh"]))
    e1 = dict(e1, gh=gh)
    sums = [Flow(sum_steps(1, e1["give"], e1["keep"]))]
    f1 = heads_back(1, sums, gh, a1, e1)
    sums.append(Flow(sum_steps(1, f1["give"], f1["keep"])))
    g1 = input_back(1, far_one, sums, f1["d"], a1, b1, e1, f1, c0["y"])
    e0 = feed_back(0, far_two_zero, sums, g1["du"], g1["du"], b0, c0)
    sums.append(Flow(sum_steps(0, e0["give"], e0["keep"])))
    f0 = heads_back(0, sums, e0["gh"], a0, e0)
    sums.append(Flow(sum_steps(0, f0["give"], f0["keep"])))
    g0 = input_back(0, far_zero, sums, f0["d"], a0, b0, e0, f0, u0)
    norm_grads = [
        jnp.concatenate([g["grads"][:1], e["grads"][:1], g["grads"][1:], e["grads"][1:]])
        for g, e in ((g0, e0), (g1, e1))
    ]
    norm_flow = Flow(butterfly_steps(jnp.concatenate(norm_grads, axis=0)))
    norm_flow.advance()
    grads_in = to_outputs([g0["du"], g1["du"]])
    for flow in sums:
        flow.advance(g0["du"])
    (grads_in, results), _ = lax.optimization_barrier(((grads_in, sums[3].results), g0["du"]))
    sums[3].results = results
    while any(not flow.done for flow in sums + [norm_flow]):
        for n in (0, 1, 3):
            if not sums[n].done:
                sums[n].advance()
        together([sums[2], norm_flow])
    parts = [flow.value for flow in sums]
    grad_down, grad_up = final_mlp_call(here, [*parts[2], *parts[0]], width)
    grad_out, grad_qkv = final_attention_call(here, [*parts[3], *parts[1]], width)
    norm_total = norm_flow.value
    norm_sum = jnp.where(sec == 0, norm_total[:4], norm_total[4:])
    norm_sum = lax.dynamic_slice_in_dim(norm_sum, tensor * local, local, 1)

    return (
        outputs,
        grads_in,
        jnp.transpose(grad_qkv, (1, 0, 2))[None],
        grad_out[None],
        grad_up[None],
        grad_down[None],
        norm_sum[None, :2],
        norm_sum[None, 2:],
    )


def solution(mesh):
    in_specs = (
        P(None, ("dp", "tensor"), None),
        P("dp", None, None),
        P("section", None, None, "tensor"),
        P("section", "tensor", None),
        P("section", None, "tensor"),
        P("section", "tensor", None),
        P("section", None, None),
        P("section", None, None),
        P(None, ("dp", "tensor"), None),
    )
    out_specs = (
        P("section", None, ("dp", "tensor"), None),
        P("section", None, ("dp", "tensor"), None),
        P("section", None, None, "tensor"),
        P("section", "tensor", None),
        P("section", None, "tensor"),
        P("section", "tensor", None),
        P("section", None, "tensor"),
        P("section", None, "tensor"),
    )
    return jax.shard_map(
        per_device, mesh=mesh, in_specs=in_specs, out_specs=out_specs, check_vma=False
    )
```
